32 devices in a mesh: dp: 8 (over z, core), tensor: 4 (over y, x).
Axes of the slice: x: 2, y: 2, z: 4, core: 2. Of those that a mesh axis runs over, the one named last changes fastest.
Arguments:
- tokens: bfloat16 [16384, 2048], P(('dp', 'tensor')), may hold values from -6 to 6
- norm_gain: float32 [2048], replicated, may hold values from 0.1 to 1.9
- norm_shift: float32 [2048], replicated, may hold values from -1.75 to 1.75
- weight_qkv: bfloat16 [2048, 3, 2048], P('dp', None, 'tensor'), may hold values from -0.125 to 0.125
- bias_qkv: float32 [3, 2048], P(None, 'tensor'), may hold values from -1.5 to 1.5
- weight_dense: bfloat16 [2048, 2048], P('tensor', 'dp'), may hold values from -0.5 to 0.5
- weight_up: bfloat16 [2048, 8192], P('dp', 'tensor'), may hold values from -0.125 to 0.125
- bias_up: float32 [8192], P('tensor'), may hold values from -3 to 3
- weight_down: bfloat16 [8192, 2048], P('tensor', 'dp'), may hold values from -0.0625 to 0.0625
- bias_out: float32 [2048], replicated, may hold values from -1.75 to 1.75
- cotangent: bfloat16 [16384, 2048], P(('dp', 'tensor')), may hold values from -6 to 6
Outputs:
- block_out: bfloat16 [16384, 2048], P(('dp', 'tensor'))
- grad_tokens: bfloat16 [16384, 2048], P(('dp', 'tensor'))
- grad_norm_gain: float32 [2048], replicated
- grad_norm_shift: float32 [2048], replicated
- grad_weight_qkv: float32 [2048, 3, 2048], P('dp', None, 'tensor')
- grad_bias_qkv: float32 [3, 2048], P(None, 'tensor')
- grad_weight_dense: float32 [2048, 2048], P('tensor', 'dp')
- grad_weight_up: float32 [2048, 8192], P('dp', 'tensor')
- grad_bias_up: float32 [8192], P('tensor')
- grad_weight_down: float32 [8192, 2048], P('tensor', 'dp')
- grad_bias_out: float32 [2048], replicated
The draws below stay inside these ranges and needn't reach their ends.
All inputs are finite; a program needn't handle non-finite values.
Results may differ from the reference program's by a relative error of at most 0.009.
Values may be sent and summed in bfloat16 or wider, within the bound.
No kernel may reach another device: no remote copies, remote signals or barrier semaphores. Data moves between devices by JAX's collectives and lax.ppermute only.
A program may use at most 320 MiB of HBM per device.

```python
import jax
import jax.numpy as jnp
from jax import lax

D = 2048
HEADS = 32
HEAD_DIM = 64
ROT = 32
FF = 8192
LENGTH = 2048
TOKENS = 16384


def block_levels(key, dims, shards, smallest, largest):
    def one(axis_at, parts):
        draws = jax.random.uniform(jax.random.fold_in(jax.random.fold_in(key, 6), axis_at), (parts,), jnp.float32, smallest / len(shards), largest / len(shards))
        return jnp.repeat(jnp.exp(draws), dims[axis_at] // parts).reshape((-1,) + (1,) * (len(dims) - axis_at - 1))

    loudness = one(*shards[0])
    for cut in shards[1:]:
        loudness = loudness * one(*cut)
    return loudness


def noise(own_key, dims, width, most, cuts=(), kind=jnp.bfloat16):
    values = jax.random.normal(own_key, dims, jnp.float32) * width
    if len(cuts) > 0:
        values = block_levels(own_key, dims, cuts, -0.22, 0.18) * values
    return jnp.clip(values, min=-most, max=most).astype(kind)


def setup_inputs(seed: int = 0) -> dict:
    arg_keys = jax.random.split(jax.random.key(seed), 12)
    tokens = noise(arg_keys[0], (TOKENS, D), 1.0, 6.0, ((0, 32),))
    norm_gain = jnp.clip(1.0 + 0.18 * jax.random.normal(arg_keys[1], (D,), jnp.float32), 0.1, 1.9)
    norm_shift = noise(arg_keys[2], (D,), 0.3, 1.75, (), jnp.float32)
    weight_qkv = noise(arg_keys[3], (D, 3, D), D ** -0.5, 0.125, ((0, 8), (2, 4)))
    bias_qkv = noise(arg_keys[4], (3, D), 0.25, 1.5, ((1, 4),), jnp.float32)
    weight_dense = noise(arg_keys[5], (D, D), (max(D // 16, 64)) ** -0.5, 0.5, ((0, 4), (1, 8)))
    weight_up = noise(arg_keys[6], (D, FF), D ** -0.5, 0.125, ((0, 8), (1, 4)))
    bias_up = noise(arg_keys[7], (FF,), 0.5, 3.0, ((0, 4),), jnp.float32)
    weight_down = noise(arg_keys[8], (FF, D), FF ** -0.5, 0.0625, ((0, 4), (1, 8)))
    bias_out = noise(arg_keys[9], (D,), 0.3, 1.75, (), jnp.float32)
    cotangent = noise(arg_keys[10], (TOKENS, D), 1.0, 6.0, ((0, 32),))
    return dict(tokens=tokens, norm_gain=norm_gain, norm_shift=norm_shift, weight_qkv=weight_qkv, bias_qkv=bias_qkv, weight_dense=weight_dense, weight_up=weight_up, bias_up=bias_up, weight_down=weight_down, bias_out=bias_out, cotangent=cotangent)


highest = lax.Precision.HIGHEST
epsilon = 1e-05
masked_score = -1e+30

@jax.custom_vjp
def low(v):
    return lax.optimization_barrier(v.astype(jnp.bfloat16)).astype(jnp.float32)

@jax.custom_vjp
def low_back(v):
    return v

def low_keep(v):
    return (low(v), None)

def low_pass(kept, grad):
    return (grad,)

def back_keep(v):
    return (v, None)

def back_low(kept, grad):
    return (low(grad),)
low.defvjp(low_keep, low_pass)
low_back.defvjp(back_keep, back_low)

def tables(row_total):
    half_rot = ROT // 2
    positions = (jnp.arange(row_total, dtype=jnp.int32) % LENGTH).astype(jnp.float32)
    inverse = 10000.0 ** (-(2.0 * jnp.arange(half_rot, dtype=jnp.float32)) / ROT)
    angles = positions[:, None] * inverse[None, :]
    return (jnp.cos(angles)[:, None, :], jnp.sin(angles)[:, None, :])

def rotate(field_in, cosine, sine_table):
    half_rot = ROT // 2
    first_half = field_in[..., :half_rot]
    second_half = field_in[..., half_rot:ROT]
    return jnp.concatenate([first_half * cosine - second_half * sine_table, second_half * cosine + first_half * sine_table, field_in[..., ROT:]], axis=-1)

def forward_sequence(token_rows, params):
    norm_gain, norm_shift, weight_qkv, bias_qkv, weight_dense, weight_up, bias_up, weight_down, bias_out = params
    mean_row = lax.optimization_barrier(jnp.mean(token_rows, axis=-1, keepdims=True))
    centred = token_rows - mean_row
    variance = lax.optimization_barrier(jnp.mean(centred * centred, axis=-1, keepdims=True))
    normed = low(centred * lax.rsqrt(variance + epsilon) * norm_gain + norm_shift)
    joined = jnp.dot(normed, weight_qkv.reshape(D, 3 * D), precision=highest) + bias_qkv.reshape(3 * D)
    joined = low_back(joined).reshape(LENGTH, 3, HEADS, HEAD_DIM)
    cosine, sine_table = tables(LENGTH)
    queries = low(rotate(joined[:, 0], cosine, sine_table))
    key_rows = low(rotate(joined[:, 1], cosine, sine_table))
    values = low(joined[:, 2])
    scores = jnp.einsum('qhe,khe->hqk', queries, key_rows, precision=highest) * HEAD_DIM ** (-0.5)
    scores = low_back(scores)
    positions = jnp.arange(LENGTH, dtype=jnp.int32)
    causal = positions[:, None] >= positions[None, :]
    scores = jnp.where(causal[None], scores, masked_score)
    row_top = lax.optimization_barrier(jnp.max(scores, axis=-1, keepdims=True))
    weights = jnp.exp(scores - row_top)
    probabilities = low(weights / lax.optimization_barrier(jnp.sum(weights, axis=-1, keepdims=True)))
    mixed_heads = jnp.einsum('hqk,khe->qhe', probabilities, values, precision=highest).reshape(LENGTH, D)
    mixed_heads = low(low_back(mixed_heads))
    attended = jnp.dot(mixed_heads, weight_dense, precision=highest)
    hidden = low_back(jnp.dot(normed, weight_up, precision=highest) + bias_up)
    activated = low(jax.nn.gelu(hidden, approximate=True))
    feed_out = jnp.dot(activated, weight_down, precision=highest)
    return token_rows + attended + feed_out + bias_out

def reference(tokens, norm_gain, norm_shift, weight_qkv, bias_qkv, weight_dense, weight_up, bias_up, weight_down, bias_out, cotangent):
    params = tuple((argument.astype(jnp.float32) for argument in (norm_gain, norm_shift, weight_qkv, bias_qkv, weight_dense, weight_up, bias_up, weight_down, bias_out)))
    token_seqs = tokens.astype(jnp.float32).reshape(-1, LENGTH, D)
    grad_seqs = cotangent.astype(jnp.float32).reshape(-1, LENGTH, D)

    def per_sequence(carried, sequence_pair):
        token_rows, grad_out = sequence_pair
        result, pullback = jax.vjp(forward_sequence, token_rows, params)
        grad_rows, grad_params = pullback(grad_out)
        carried = tuple((total + update for total, update in zip(carried, grad_params)))
        return (carried, (result, grad_rows))
    initial = tuple((jnp.zeros_like(argument) for argument in params))
    totals, (results, grad_rows) = lax.scan(per_sequence, initial, (token_seqs, grad_seqs))
    grad_gain, grad_shift, grad_qkv, grad_bias_qkv, grad_dense, grad_up, grad_bias_up, grad_down, grad_bias_out = totals
    return (results.reshape(-1, D).astype(jnp.bfloat16), grad_rows.reshape(-1, D).astype(jnp.bfloat16), grad_gain, grad_shift, grad_qkv, grad_bias_qkv, grad_dense, grad_up, grad_bias_up, grad_down, grad_bias_out)
```

```python
import functools

import jax
import jax.numpy as jnp
from jax import lax
from jax.experimental import pallas as pl
from jax.experimental.pallas import tpu as pltpu
from jax.sharding import PartitionSpec as P

HEAD_DIM = 64
ROT = 32
LENGTH = 2048
PAIR = 2 * HEAD_DIM

epsilon = 1e-05
masked_score = -1e30
MIB = 1024 * 1024
ROWS_BY_ROWS = (((1,), (1,)), ((), ()))


def after(value, *earlier):
    return lax.optimization_barrier((value,) + earlier)[0]


def swap(value, bit):
    count = lax.axis_size("tensor")
    return lax.ppermute(value, "tensor", [(i, i ^ bit) for i in range(count)])


def group_gather(block):
    half = block.shape[0] // 2
    one = swap(block, 1)
    two = swap(block, 2)
    low = swap(one[:half], 2)
    high = swap(two[half:], 1)
    return block, one, two, low, high


def place_group(parts):
    block, one, two, low, high = parts
    rows = block.shape[0]
    me = lax.axis_index("tensor")
    full = jnp.zeros((4 * rows,) + block.shape[1:], block.dtype)

    def put(full, piece, owner, shift=0):
        start = (owner * rows + shift,) + (0,) * (block.ndim - 1)
        return lax.dynamic_update_slice(full, piece, start)

    full = put(full, block, me)
    full = put(full, one, me ^ 1)
    full = put(full, two, me ^ 2)
    full = put(full, low, me ^ 3)
    return put(full, high, me ^ 3, rows // 2)


def group_scatter(partial):
    rows = partial.shape[0] // 4
    half = rows // 2
    me = lax.axis_index("tensor")

    def take(bit, shift):
        return lax.dynamic_slice_in_dim(partial, (me ^ bit) * rows + shift, half, 0)

    def wide(piece):
        return piece.astype(jnp.float32)

    first = swap(jnp.concatenate([take(1, 0), take(3, 0)]), 1)
    second = swap(jnp.concatenate([take(2, half), take(3, half)]), 2)
    forward_first = (wide(take(2, 0)) + wide(first[half:])).astype(partial.dtype)
    forward_second = (wide(take(1, half)) + wide(second[half:])).astype(partial.dtype)
    last_first = swap(forward_first, 2)
    last_second = swap(forward_second, 1)
    low = wide(take(0, 0)) + wide(first[:half]) + wide(last_first)
    high = wide(take(0, half)) + wide(second[:half]) + wide(last_second)
    return jnp.concatenate([low, high])


def lane_tables(row_total):
    half_rot = ROT // 2
    positions = (jnp.arange(row_total, dtype=jnp.int32) % LENGTH).astype(jnp.float32)
    inverse = 10000.0 ** (-(2.0 * jnp.arange(half_rot, dtype=jnp.float32)) / ROT)
    angles = positions[:, None] * inverse[None, :]
    cosine, sine = jnp.cos(angles), jnp.sin(angles)
    ones = jnp.ones((row_total, HEAD_DIM - ROT), jnp.float32)
    zeros = jnp.zeros((row_total, half_rot), jnp.float32)
    rest = jnp.zeros((row_total, HEAD_DIM - ROT), jnp.float32)
    cos_lanes = jnp.concatenate([cosine, cosine, ones] * 2, axis=1)
    from_above = jnp.concatenate([-sine, zeros, rest] * 2, axis=1)
    from_below = jnp.concatenate([zeros, sine, rest] * 2, axis=1)
    return cos_lanes, from_above, from_below


def turn(field, cos_lanes, from_above, from_below):
    half_rot = ROT // 2
    above = pltpu.roll(field, PAIR - half_rot, 1)
    below = pltpu.roll(field, half_rot, 1)
    return field * cos_lanes + above * from_above + below * from_below


def turn_back(field, cos_lanes, from_above, from_below):
    half_rot = ROT // 2
    above = pltpu.roll(field, PAIR - half_rot, 1)
    below = pltpu.roll(field, half_rot, 1)
    return field * cos_lanes - above * from_above - below * from_below


def joined_kernel(x_ref, w_ref, bias_ref, cos_ref, above_ref, below_ref, out_ref):
    product = jnp.dot(x_ref[...], w_ref[0], preferred_element_type=jnp.float32) + bias_ref[0]
    slot = pl.program_id(1)

    @pl.when(slot < 2)
    def _():
        for start in range(0, product.shape[1], PAIR):
            lanes = product[:, start : start + PAIR]
            turned = turn(lanes, cos_ref[...], above_ref[...], below_ref[...])
            out_ref[:, start : start + PAIR] = turned.astype(out_ref.dtype)

    @pl.when(slot == 2)
    def _():
        out_ref[...] = product.astype(out_ref.dtype)


def joined_rows(x, w, bias, lanes):
    rows, depth = x.shape
    width = w.shape[2]
    block = min(512, rows)
    return pl.pallas_call(
        joined_kernel,
        grid=(rows // block, 3),
        in_specs=[
            pl.BlockSpec((block, depth), lambda i, j: (i, 0)),
            pl.BlockSpec((1, depth, width), lambda i, j: (j, 0, 0)),
            pl.BlockSpec((1, 1, width), lambda i, j: (j, 0, 0)),
        ]
        + [pl.BlockSpec((block, PAIR), lambda i, j: (i, 0))] * 3,
        out_specs=pl.BlockSpec((block, width), lambda i, j: (i, j)),
        out_shape=jax.ShapeDtypeStruct((rows, 3 * width), jnp.bfloat16),
        compiler_params=pltpu.CompilerParams(vmem_limit_bytes=48 * MIB),
        cost_estimate=pl.CostEstimate(
            flops=6 * rows * depth * width, bytes_accessed=24 * MIB, transcendentals=0
        ),
    )(x, w, bias.reshape(3, 1, width), *lanes)


def hidden_kernel(x_ref, w_ref, bias_ref, active_ref, slope_ref):
    hidden = jnp.dot(x_ref[...], w_ref[...], preferred_element_type=jnp.float32) + bias_ref[...]
    scale = (2.0 / jnp.pi) ** 0.5
    square = hidden * hidden
    inner = scale * hidden * (1.0 + 0.044715 * square)
    bent = jnp.tanh(inner)
    half = 0.5 * (1.0 + bent)
    active_ref[...] = (hidden * half).astype(active_ref.dtype)
    growth = scale * (1.0 + (3.0 * 0.044715) * square)
    slope = half + 0.5 * hidden * (1.0 - bent * bent) * growth
    slope_ref[...] = slope.astype(slope_ref.dtype)


def hidden_rows(x, w, bias):
    rows, depth = x.shape
    width = w.shape[1]
    block, columns = min(512, rows), min(512, width)
    return pl.pallas_call(
        hidden_kernel,
        grid=(width // columns, rows // block),
        in_specs=[
            pl.BlockSpec((block, depth), lambda j, i: (i, 0)),
            pl.BlockSpec((depth, columns), lambda j, i: (0, j)),
            pl.BlockSpec((1, columns), lambda j, i: (0, j)),
        ],
        out_specs=[pl.BlockSpec((block, columns), lambda j, i: (i, j))] * 2,
        out_shape=[jax.ShapeDtypeStruct((rows, width), jnp.bfloat16)] * 2,
        compiler_params=pltpu.CompilerParams(vmem_limit_bytes=48 * MIB),
        cost_estimate=pl.CostEstimate(
            flops=2 * rows * depth * width, bytes_accessed=40 * MIB, transcendentals=rows * width
        ),
    )(x, w, bias.reshape(1, width))


def grad_hidden_kernel(g_ref, w_ref, slope_ref, out_ref, sum_ref):
    product = lax.dot_general(
        g_ref[...], w_ref[...], ROWS_BY_ROWS, preferred_element_type=jnp.float32
    )
    low = (product * slope_ref[...].astype(jnp.float32)).astype(out_ref.dtype)
    out_ref[...] = low

    @pl.when(pl.program_id(1) == 0)
    def _():
        sum_ref[...] = jnp.zeros_like(sum_ref)

    sum_ref[...] += jnp.sum(low.astype(jnp.float32), axis=0, keepdims=True)


def grad_hidden_rows(g, w, slope):
    rows, depth = g.shape
    width = w.shape[0]
    block, columns = min(512, rows), min(512, width)
    return pl.pallas_call(
        grad_hidden_kernel,
        grid=(width // columns, rows // block),
        in_specs=[
            pl.BlockSpec((block, depth), lambda j, i: (i, 0)),
            pl.BlockSpec((columns, depth), lambda j, i: (j, 0)),
            pl.BlockSpec((block, columns), lambda j, i: (i, j)),
        ],
        out_specs=[
            pl.BlockSpec((block, columns), lambda j, i: (i, j)),
            pl.BlockSpec((1, columns), lambda j, i: (0, j)),
        ],
        out_shape=[
            jax.ShapeDtypeStruct((rows, width), jnp.bfloat16),
            jax.ShapeDtypeStruct((1, width), jnp.float32),
        ],
        compiler_params=pltpu.CompilerParams(vmem_limit_bytes=48 * MIB),
        cost_estimate=pl.CostEstimate(
            flops=2 * rows * depth * width, bytes_accessed=40 * MIB, transcendentals=0
        ),
    )(g, w, slope)


def attention_kernel(
    q_ref,
    k_ref,
    v_ref,
    g_ref,
    cos_ref,
    above_ref,
    below_ref,
    mixed_ref,
    grads_ref,
    sums_ref,
    keys_across,
    values_across,
    query_total,
    key_total,
    value_total,
    *,
    block,
    block_count,
):
    step = pl.program_id(1)
    scale = HEAD_DIM**-0.5
    log2_e = 1.4426950408889634

    @pl.when(step == 0)
    def _():
        keys_across[...] = k_ref[...].T
        values_across[...] = v_ref[...].T
        key_total[...] = jnp.zeros_like(key_total)
        value_total[...] = jnp.zeros_like(value_total)

    def rows_from(index):
        reach = (index + 1) * block
        queries, grads = q_ref[...], g_ref[...]
        keys, values = k_ref[0:reach, :], v_ref[0:reach, :]
        grads_across = grads.T.astype(jnp.float32)
        lane = lax.broadcasted_iota(jnp.int32, (block, PAIR), 1)
        key_pos = lax.broadcasted_iota(jnp.int32, (block, block), 0)
        query_pos = lax.broadcasted_iota(jnp.int32, (block, block), 1)
        mixed, grad_queries = [], []
        grad_keys = grad_values = None
        for head in range(2):
            own = lane // HEAD_DIM == head
            part = slice(head * HEAD_DIM, (head + 1) * HEAD_DIM)
            query_own = jnp.where(own, queries, jnp.zeros_like(queries))
            grad_own = jnp.where(own, grads, jnp.zeros_like(grads))
            scores = lax.dot_general(
                keys, query_own, ROWS_BY_ROWS, preferred_element_type=jnp.float32
            )
            corner = jnp.where(key_pos <= query_pos, scores[reach - block :], masked_score)
            if index:
                scores = jnp.concatenate([scores[: reach - block], corner], axis=0)
            else:
                scores = corner
            top = jnp.max(scores, axis=0, keepdims=True)
            weights = jnp.exp2(scores * (scale * log2_e) - top * (scale * log2_e))
            total = jnp.sum(weights, axis=0, keepdims=True)
            exact = weights * (1.0 / total)
            rounded = exact.astype(jnp.bfloat16)
            out = jnp.dot(
                values_across[part, 0:reach], rounded, preferred_element_type=jnp.float32
            )
            inner = jnp.sum(out * grads_across[part], axis=0, keepdims=True)
            grad_probs = lax.dot_general(
                values, grad_own, ROWS_BY_ROWS, preferred_element_type=jnp.float32
            )
            grad_scores = (exact * (grad_probs - inner)).astype(jnp.bfloat16)
            mixed.append(out)
            grad_queries.append(
                jnp.dot(
                    keys_across[part, 0:reach], grad_scores, preferred_element_type=jnp.float32
                )
            )
            value_part = jnp.dot(rounded, grad_own, preferred_element_type=jnp.float32)
            key_part = jnp.dot(grad_scores, query_own, preferred_element_type=jnp.float32)
            grad_values = value_part if head == 0 else grad_values + value_part
            grad_keys = key_part if head == 0 else grad_keys + key_part
        value_total[0:reach, :] += grad_values
        key_total[0:reach, :] += grad_keys
        mixed_ref[...] = jnp.concatenate(mixed, axis=0).T.astype(mixed_ref.dtype)
        query_total[reach - block : reach, :] = jnp.concatenate(grad_queries, axis=0).T

    for index in range(block_count):
        pl.when(step == index)(functools.partial(rows_from, index))

    @pl.when(step == block_count - 1)
    def _():
        lanes = cos_ref[...], above_ref[...], below_ref[...]
        for slot, field in enumerate(
            (
                turn_back(query_total[...] * scale, *lanes),
                turn_back(key_total[...] * scale, *lanes),
                value_total[...],
            )
        ):
            low = field.astype(grads_ref.dtype)
            grads_ref[slot] = low
            sums_ref[slot] = jnp.sum(low.astype(jnp.float32), axis=0, keepdims=True)


def attention(joined, grad_mixed, lanes):
    rows, width = grad_mixed.shape
    block = 256
    pairs, block_count = width // PAIR, LENGTH // block
    row_block = pl.BlockSpec((block, PAIR), lambda p, i: (i, p))
    table = pl.BlockSpec((LENGTH, PAIR), lambda p, i: (0, 0))
    return pl.pallas_call(
        functools.partial(attention_kernel, block=block, block_count=block_count),
        grid=(pairs, block_count),
        in_specs=[
            row_block,
            pl.BlockSpec((LENGTH, PAIR), lambda p, i: (0, pairs + p)),
            pl.BlockSpec((LENGTH, PAIR), lambda p, i: (0, 2 * pairs + p)),
            row_block,
            table,
            table,
            table,
        ],
        out_specs=[
            row_block,
            pl.BlockSpec((3, LENGTH, PAIR), lambda p, i: (0, 0, p)),
            pl.BlockSpec((3, 1, PAIR), lambda p, i: (0, 0, p)),
        ],
        out_shape=[
            jax.ShapeDtypeStruct((rows, width), jnp.bfloat16),
            jax.ShapeDtypeStruct((3, rows, width), jnp.bfloat16),
            jax.ShapeDtypeStruct((3, 1, width), jnp.float32),
        ],
        scratch_shapes=[
            pltpu.VMEM((PAIR, LENGTH), jnp.bfloat16),
            pltpu.VMEM((PAIR, LENGTH), jnp.bfloat16),
            pltpu.VMEM((LENGTH, PAIR), jnp.float32),
            pltpu.VMEM((LENGTH, PAIR), jnp.float32),
            pltpu.VMEM((LENGTH, PAIR), jnp.float32),
        ],
        compiler_params=pltpu.CompilerParams(vmem_limit_bytes=56 * MIB),
        cost_estimate=pl.CostEstimate(
            flops=100 * rows * rows * width, bytes_accessed=16 * MIB, transcendentals=0
        ),
    )(joined, joined, joined, grad_mixed, *lanes)


def on_device(
    tokens,
    norm_gain,
    norm_shift,
    weight_qkv,
    bias_qkv,
    weight_dense,
    weight_up,
    bias_up,
    weight_down,
    bias_out,
    cotangent,
):
    f32 = jnp.float32
    token_rows = tokens.astype(f32)
    mean_row = jnp.mean(token_rows, axis=-1, keepdims=True)
    centred = token_rows - mean_row
    variance = jnp.mean(centred * centred, axis=-1, keepdims=True)
    root = lax.rsqrt(variance + epsilon)
    normed_low = (centred * root * norm_gain + norm_shift).astype(jnp.bfloat16)

    full_qkv = lax.all_gather(jnp.transpose(weight_qkv, (1, 0, 2)), "dp", axis=1, tiled=True)
    full_up = lax.all_gather(weight_up, "dp", axis=0, tiled=True)
    full_dense = lax.all_gather(weight_dense, "dp", axis=1, tiled=True)
    full_down = lax.all_gather(weight_down, "dp", axis=1, tiled=True)
    normed_parts = group_gather(normed_low)
    grad_parts = group_gather(after(cotangent, normed_parts[-1]))
    gathered = place_group(normed_parts)
    grad_rows = place_group(grad_parts)
    group_rows = gathered.shape[0]
    lanes = lane_tables(LENGTH)

    joined = joined_rows(gathered, full_qkv, bias_qkv, lanes)
    active, slope = hidden_rows(gathered, full_up, bias_up)
    grad_mixed = jnp.einsum(
        "td,kd->tk", grad_rows, full_dense, preferred_element_type=f32
    ).astype(jnp.bfloat16)
    grad_down = jnp.einsum("tf,td->fd", active, grad_rows, preferred_element_type=f32)
    grad_down = lax.psum_scatter(
        grad_down.astype(jnp.bfloat16), "dp", scatter_dimension=1, tiled=True
    )
    mixed, grad_joined, bias_qkv_part = attention(joined, grad_mixed, lanes)
    branch = (
        jnp.dot(mixed, full_dense, preferred_element_type=f32)
        + jnp.dot(active, full_down, preferred_element_type=f32)
    ).astype(jnp.bfloat16)
    branch_sum = group_scatter(branch)
    block_out = (token_rows + branch_sum + bias_out).astype(jnp.bfloat16)

    grad_hidden, bias_up_part = grad_hidden_rows(grad_rows, full_down, slope)
    grad_up = jnp.einsum("td,tf->df", gathered, grad_hidden, preferred_element_type=f32)
    grad_up = lax.psum_scatter(
        grad_up.astype(jnp.bfloat16), "dp", scatter_dimension=0, tiled=True
    )
    grad_qkv = jnp.einsum("td,jtc->jdc", gathered, grad_joined, preferred_element_type=f32)
    grad_qkv = lax.psum_scatter(
        grad_qkv.astype(jnp.bfloat16), "dp", scatter_dimension=1, tiled=True
    )
    grad_dense = jnp.einsum("tk,td->kd", mixed, grad_rows, preferred_element_type=f32)
    grad_dense = lax.psum_scatter(
        grad_dense.astype(jnp.bfloat16), "dp", scatter_dimension=1, tiled=True
    )
    grad_normed = (
        jnp.einsum("jtc,jdc->td", grad_joined, full_qkv, preferred_element_type=f32)
        + jnp.einsum("tf,df->td", grad_hidden, full_up, preferred_element_type=f32)
    ).astype(jnp.bfloat16)
    grad_normed = group_scatter(grad_normed)

    hat = centred * root
    scaled = grad_normed * norm_gain
    grad_input = root * (
        scaled
        - jnp.mean(scaled, axis=-1, keepdims=True)
        - hat * jnp.mean(scaled * hat, axis=-1, keepdims=True)
    )
    grad_tokens = (cotangent.astype(f32) + grad_input).astype(jnp.bfloat16)
    grad_bias_qkv, grad_bias_up = lax.psum(
        (bias_qkv_part.reshape(bias_qkv.shape), bias_up_part.reshape(bias_up.shape)), "dp"
    )
    gain_part = jnp.sum(grad_normed * hat, axis=0)
    shift_part = jnp.sum(grad_normed, axis=0)
    out_part = jnp.sum(cotangent, axis=0, dtype=f32)
    grad_gain, grad_shift, grad_bias_out = lax.psum(
        (gain_part, shift_part, out_part), ("dp", "tensor")
    )
    return (
        block_out,
        grad_tokens,
        grad_gain,
        grad_shift,
        jnp.transpose(grad_qkv, (1, 0, 2)).astype(f32),
        grad_bias_qkv,
        grad_dense.astype(f32),
        grad_up.astype(f32),
        grad_bias_up,
        grad_down.astype(f32),
        grad_bias_out,
    )


def solution(mesh):
    in_specs = (
        P(("dp", "tensor"), None),
        P(),
        P(),
        P("dp", None, "tensor"),
        P(None, "tensor"),
        P("tensor", "dp"),
        P("dp", "tensor"),
        P("tensor"),
        P("tensor", "dp"),
        P(),
        P(("dp", "tensor"), None),
    )
    out_specs = (
        P(("dp", "tensor"), None),
        P(("dp", "tensor"), None),
        P(),
        P(),
        P("dp", None, "tensor"),
        P(None, "tensor"),
        P("tensor", "dp"),
        P("dp", "tensor"),
        P("tensor"),
        P("tensor", "dp"),
        P(),
    )
    return jax.shard_map(
        on_device, mesh=mesh, in_specs=in_specs, out_specs=out_specs, check_vma=False
    )
```

```python
import functools
import math

import jax
import jax.numpy as jnp
from jax import lax
from jax.experimental import pallas as pl
from jax.experimental.pallas import tpu as pltpu
from jax.sharding import PartitionSpec as P

HEAD_DIM = 64
ROT = 32
LENGTH = 2048
PAIR = 2 * HEAD_DIM

epsilon = 1e-05
masked_score = -1e30
MIB = 1024 * 1024
ROWS_BY_ROWS = (((1,), (1,)), ((), ()))


def after(value, *earlier):
    return lax.optimization_barrier((value,) + earlier)[0]


def swap(value, axis, bit):
    count = lax.axis_size(axis)
    return lax.ppermute(value, axis, [(i, i ^ bit) for i in range(count)])


def place_kernel(starts_ref, *refs, dim):
    count = (len(refs) - 2) // 2
    pieces, out, buffers, sems = refs[:count], refs[count], refs[count + 1 : -1], refs[-1]
    for slot in range(count):
        pltpu.make_async_copy(pieces[slot], buffers[slot], sems.at[0, slot]).start()
    writes = []
    for slot in range(count):
        buffer = buffers[slot]
        size = buffer.shape[dim]
        where = [slice(None)] * len(buffer.shape)
        where[dim] = pl.ds(pl.multiple_of(starts_ref[slot], size), size)
        pltpu.make_async_copy(pieces[slot], buffer, sems.at[0, slot]).wait()
        write = pltpu.make_async_copy(buffer, out.at[tuple(where)], sems.at[1, slot])
        write.start()
        writes.append(write)
    for write in writes:
        write.wait()


def place(pieces, dim, total):
    starts = jnp.stack([jnp.asarray(start, jnp.int32) for start, _ in pieces])
    sources = [piece for _, piece in pieces]
    shape = list(sources[0].shape)
    shape[dim] = total
    any_space = pl.BlockSpec(memory_space=pl.ANY)
    return pl.pallas_call(
        functools.partial(place_kernel, dim=dim),
        in_specs=[pl.BlockSpec(memory_space=pltpu.SMEM)] + [any_space] * len(sources),
        out_specs=any_space,
        out_shape=jax.ShapeDtypeStruct(tuple(shape), sources[0].dtype),
        scratch_shapes=[pltpu.VMEM(source.shape, source.dtype) for source in sources]
        + [pltpu.SemaphoreType.DMA((2, len(pieces)))],
        compiler_params=pltpu.CompilerParams(vmem_limit_bytes=60 * MIB),
        cost_estimate=pl.CostEstimate(
            flops=0, bytes_accessed=4 * math.prod(shape), transcendentals=0
        ),
    )(starts, *sources)


def gather_start(block):
    if lax.axis_size("tensor") != 4:
        return (lax.all_gather(block, "tensor", axis=0, tiled=True),)
    return block, swap(block, "tensor", 1), swap(block, "tensor", 2)


def gather_pass(parts):
    if len(parts) == 1:
        return parts
    block, one, two = parts
    half = block.shape[0] // 2
    return block, one, two, swap(one[:half], "tensor", 2), swap(two[half:], "tensor", 1)


def gathered_pieces(parts):
    if len(parts) == 1:
        return [(0, parts[0])]
    block, one, two, low, high = parts
    rows = block.shape[0]
    me = lax.axis_index("tensor")
    return [
        (me * rows, block),
        ((me ^ 1) * rows, one),
        ((me ^ 2) * rows, two),
        ((me ^ 3) * rows, low),
        ((me ^ 3) * rows + rows // 2, high),
    ]


def gather_end(parts):
    if len(parts) == 1:
        return parts[0]
    return place(gathered_pieces(parts), 0, 4 * parts[0].shape[0])


def wide(piece):
    return piece.astype(jnp.float32)


def scatter_cut(partial):
    if lax.axis_size("tensor") != 4:
        return (partial,)
    rows = partial.shape[0] // 4
    half = rows // 2
    me = lax.axis_index("tensor")

    def take(bit, shift):
        return lax.dynamic_slice_in_dim(partial, (me ^ bit) * rows + shift, half, 0)

    return tuple(take(bit, shift) for bit in (3, 1, 2, 0) for shift in (0, half))


def scatter_send(cuts):
    if len(cuts) == 1:
        return (lax.psum_scatter(wide(cuts[0]), "tensor", scatter_dimension=0, tiled=True),)
    far_low, far_high, one_low, one_high, two_low, two_high, low, high = cuts
    return (
        swap(far_low, "tensor", 1),
        swap(far_high, "tensor", 2),
        swap(one_low, "tensor", 1),
        swap(two_high, "tensor", 2),
        two_low,
        one_high,
        low,
        high,
    )


def scatter_fold(parts):
    if len(parts) == 1:
        return parts
    first_far, second_far, first_near, second_near, two_low, one_high, low, high = parts
    return (
        (wide(two_low) + wide(first_far)).astype(low.dtype),
        (wide(one_high) + wide(second_far)).astype(low.dtype),
        first_near,
        second_near,
        low,
        high,
    )


def scatter_pass(parts):
    if len(parts) == 1:
        return parts
    two_low, one_high, first_near, second_near, low, high = parts
    return (
        swap(two_low, "tensor", 2),
        swap(one_high, "tensor", 1),
        first_near,
        second_near,
        low,
        high,
    )


def scatter_end(parts):
    if len(parts) == 1:
        return parts[0]
    last_first, last_second, first_near, second_near, low, high = parts
    return jnp.concatenate(
        [
            wide(low) + wide(first_near) + wide(last_first),
            wide(high) + wide(second_near) + wide(last_second),
        ]
    )


def exchange_start(columns):
    if lax.axis_size("tensor") != 4:
        return (lax.all_to_all(columns, "tensor", 0, 1, tiled=True),)
    rows = columns.shape[0] // 4
    me = lax.axis_index("tensor")
    pieces = []
    for bit in range(4):
        piece = lax.dynamic_slice_in_dim(columns, (me ^ bit) * rows, rows, 0)
        pieces.append(swap(piece, "tensor", bit) if bit else piece)
    return tuple(pieces)


def exchange_end(pieces):
    if len(pieces) == 1:
        return pieces[0]
    width = pieces[0].shape[1]
    me = lax.axis_index("tensor")
    return place([((me ^ bit) * width, piece) for bit, piece in enumerate(pieces)], 1, 4 * width)


def exchange_sum(value, axis):
    count = lax.axis_size(axis)
    parts = [value]
    for bit in range(1, count):
        parts.append(swap(value, axis, bit))
    return functools.reduce(lambda a, b: a + b, parts)


def lane_tables(row_total):
    half_rot = ROT // 2
    positions = (jnp.arange(row_total, dtype=jnp.int32) % LENGTH).astype(jnp.float32)
    inverse = 10000.0 ** (-(2.0 * jnp.arange(half_rot, dtype=jnp.float32)) / ROT)
    angles = positions[:, None] * inverse[None, :]
    cosine, sine = jnp.cos(angles), jnp.sin(angles)
    ones = jnp.ones((row_total, HEAD_DIM - ROT), jnp.float32)
    zeros = jnp.zeros((row_total, half_rot), jnp.float32)
    rest = jnp.zeros((row_total, HEAD_DIM - ROT), jnp.float32)
    cos_lanes = jnp.concatenate([cosine, cosine, ones] * 2, axis=1)
    from_above = jnp.concatenate([-sine, zeros, rest] * 2, axis=1)
    from_below = jnp.concatenate([zeros, sine, rest] * 2, axis=1)
    return cos_lanes, from_above, from_below


def turn(field, cos_lanes, from_above, from_below):
    half_rot = ROT // 2
    above = pltpu.roll(field, PAIR - half_rot, 1)
    below = pltpu.roll(field, half_rot, 1)
    return field * cos_lanes + above * from_above + below * from_below


def turn_back(field, cos_lanes, from_above, from_below):
    half_rot = ROT // 2
    above = pltpu.roll(field, PAIR - half_rot, 1)
    below = pltpu.roll(field, half_rot, 1)
    return field * cos_lanes - above * from_above - below * from_below


def joined_kernel(x_ref, w_ref, bias_ref, cos_ref, above_ref, below_ref, out_ref):
    product = jnp.dot(x_ref[...], w_ref[0], preferred_element_type=jnp.float32) + bias_ref[0]
    slot = pl.program_id(0)

    @pl.when(slot < 2)
    def _():
        for start in range(0, product.shape[1], PAIR):
            lanes = product[:, start : start + PAIR]
            turned = turn(lanes, cos_ref[...], above_ref[...], below_ref[...])
            out_ref[:, start : start + PAIR] = turned.astype(out_ref.dtype)

    @pl.when(slot == 2)
    def _():
        out_ref[...] = product.astype(out_ref.dtype)


def joined_rows(x, w, bias, lanes):
    rows, depth = x.shape
    width = w.shape[2]
    block = min(1024, rows)
    return pl.pallas_call(
        joined_kernel,
        grid=(3, rows // block),
        in_specs=[
            pl.BlockSpec((block, depth), lambda j, i: (i, 0)),
            pl.BlockSpec((1, depth, width), lambda j, i: (j, 0, 0)),
            pl.BlockSpec((1, 1, width), lambda j, i: (j, 0, 0)),
        ]
        + [pl.BlockSpec((block, PAIR), lambda j, i: (i, 0))] * 3,
        out_specs=pl.BlockSpec((block, width), lambda j, i: (i, j)),
        out_shape=jax.ShapeDtypeStruct((rows, 3 * width), jnp.bfloat16),
        compiler_params=pltpu.CompilerParams(vmem_limit_bytes=60 * MIB),
        cost_estimate=pl.CostEstimate(
            flops=6 * rows * depth * width, bytes_accessed=24 * MIB, transcendentals=0
        ),
    )(x, w, bias.reshape(3, 1, width), *lanes)


def hidden_kernel(x_ref, w_ref, bias_ref, active_ref, slope_ref):
    hidden = jnp.dot(x_ref[...], w_ref[...], preferred_element_type=jnp.float32) + bias_ref[...]
    scale = (2.0 / jnp.pi) ** 0.5
    square = hidden * hidden
    inner = scale * hidden * (1.0 + 0.044715 * square)
    bent = jnp.tanh(inner)
    half = 0.5 * (1.0 + bent)
    active_ref[...] = (hidden * half).astype(active_ref.dtype)
    growth = scale * (1.0 + (3.0 * 0.044715) * square)
    slope = half + 0.5 * hidden * (1.0 - bent * bent) * growth
    slope_ref[...] = slope.astype(slope_ref.dtype)


def hidden_rows(x, w, bias):
    rows, depth = x.shape
    width = w.shape[1]
    block, columns = min(1024, rows), min(1024, width)
    return pl.pallas_call(
        hidden_kernel,
        grid=(width // columns, rows // block),
        in_specs=[
            pl.BlockSpec((block, depth), lambda j, i: (i, 0)),
            pl.BlockSpec((depth, columns), lambda j, i: (0, j)),
            pl.BlockSpec((1, columns), lambda j, i: (0, j)),
        ],
        out_specs=[pl.BlockSpec((block, columns), lambda j, i: (i, j))] * 2,
        out_shape=[jax.ShapeDtypeStruct((rows, width), jnp.bfloat16)] * 2,
        compiler_params=pltpu.CompilerParams(vmem_limit_bytes=60 * MIB),
        cost_estimate=pl.CostEstimate(
            flops=2 * rows * depth * width, bytes_accessed=40 * MIB, transcendentals=rows * width
        ),
    )(x, w, bias.reshape(1, width))


def grad_hidden_kernel(g_ref, w_ref, slope_ref, out_ref, sum_ref):
    product = lax.dot_general(
        g_ref[...], w_ref[...], ROWS_BY_ROWS, preferred_element_type=jnp.float32
    )
    low = (product * slope_ref[...].astype(jnp.float32)).astype(out_ref.dtype)
    out_ref[...] = low

    @pl.when(pl.program_id(1) == 0)
    def _():
        sum_ref[...] = jnp.zeros_like(sum_ref)

    sum_ref[...] += jnp.sum(low.astype(jnp.float32), axis=0, keepdims=True)


def grad_hidden_rows(g, w, slope):
    rows, depth = g.shape
    width = w.shape[0]
    block, columns = min(1024, rows), min(1024, width)
    return pl.pallas_call(
        grad_hidden_kernel,
        grid=(width // columns, rows // block),
        in_specs=[
            pl.BlockSpec((block, depth), lambda j, i: (i, 0)),
            pl.BlockSpec((columns, depth), lambda j, i: (j, 0)),
            pl.BlockSpec((block, columns), lambda j, i: (i, j)),
        ],
        out_specs=[
            pl.BlockSpec((block, columns), lambda j, i: (i, j)),
            pl.BlockSpec((1, columns), lambda j, i: (0, j)),
        ],
        out_shape=[
            jax.ShapeDtypeStruct((rows, width), jnp.bfloat16),
            jax.ShapeDtypeStruct((1, width), jnp.float32),
        ],
        compiler_params=pltpu.CompilerParams(vmem_limit_bytes=60 * MIB),
        cost_estimate=pl.CostEstimate(
            flops=2 * rows * depth * width, bytes_accessed=40 * MIB, transcendentals=0
        ),
    )(g, w, slope)


def attention_kernel(
    q_ref,
    k_ref,
    v_ref,
    g_ref,
    cos_ref,
    above_ref,
    below_ref,
    mixed_ref,
    grads_ref,
    sums_ref,
    keys_across,
    values_across,
    query_total,
    key_total,
    value_total,
    *,
    block,
    block_count,
):
    step = pl.program_id(1)
    scale = HEAD_DIM**-0.5
    log2_e = 1.4426950408889634

    @pl.when(step == 0)
    def _():
        keys_across[...] = k_ref[...].T
        values_across[...] = v_ref[...].T
        key_total[...] = jnp.zeros_like(key_total)
        value_total[...] = jnp.zeros_like(value_total)

    def rows_from(index):
        reach = (index + 1) * block
        queries, grads = q_ref[...], g_ref[...]
        keys, values = k_ref[0:reach, :], v_ref[0:reach, :]
        grads_across = grads.T.astype(jnp.float32)
        lane = lax.broadcasted_iota(jnp.int32, (block, PAIR), 1)
        key_pos = lax.broadcasted_iota(jnp.int32, (block, block), 0)
        query_pos = lax.broadcasted_iota(jnp.int32, (block, block), 1)
        mixed, grad_queries = [], []
        grad_keys = grad_values = None
        for head in range(2):
            own = lane // HEAD_DIM == head
            part = slice(head * HEAD_DIM, (head + 1) * HEAD_DIM)
            query_own = jnp.where(own, queries, jnp.zeros_like(queries))
            grad_own = jnp.where(own, grads, jnp.zeros_like(grads))
            scores = lax.dot_general(
                keys, query_own, ROWS_BY_ROWS, preferred_element_type=jnp.float32
            )
            corner = jnp.where(key_pos <= query_pos, scores[reach - block :], masked_score)
            if index:
                scores = jnp.concatenate([scores[: reach - block], corner], axis=0)
            else:
                scores = corner
            top = jnp.max(scores, axis=0, keepdims=True)
            weights = jnp.exp2(scores * (scale * log2_e) - top * (scale * log2_e))
            total = jnp.sum(weights, axis=0, keepdims=True)
            exact = weights * (1.0 / total)
            rounded = exact.astype(jnp.bfloat16)
            out = jnp.dot(
                values_across[part, 0:reach], rounded, preferred_element_type=jnp.float32
            )
            inner = jnp.sum(out * grads_across[part], axis=0, keepdims=True)
            grad_probs = lax.dot_general(
                values, grad_own, ROWS_BY_ROWS, preferred_element_type=jnp.float32
            )
            grad_scores = (exact * (grad_probs - inner)).astype(jnp.bfloat16)
            mixed.append(out)
            grad_queries.append(
                jnp.dot(
                    keys_across[part, 0:reach], grad_scores, preferred_element_type=jnp.float32
                )
            )
            value_part = jnp.dot(rounded, grad_own, preferred_element_type=jnp.float32)
            key_part = jnp.dot(grad_scores, query_own, preferred_element_type=jnp.float32)
            grad_values = value_part if head == 0 else grad_values + value_part
            grad_keys = key_part if head == 0 else grad_keys + key_part
        value_total[0:reach, :] += grad_values
        key_total[0:reach, :] += grad_keys
        mixed_ref[...] = jnp.concatenate(mixed, axis=0).T.astype(mixed_ref.dtype)
        query_total[reach - block : reach, :] = jnp.concatenate(grad_queries, axis=0).T

    for index in range(block_count):
        pl.when(step == index)(functools.partial(rows_from, index))

    @pl.when(step == block_count - 1)
    def _():
        lanes = cos_ref[...], above_ref[...], below_ref[...]
        for slot, field in enumerate(
            (
                turn_back(query_total[...] * scale, *lanes),
                turn_back(key_total[...] * scale, *lanes),
                value_total[...],
            )
        ):
            low = field.astype(grads_ref.dtype)
            grads_ref[slot] = low
            sums_ref[slot] = jnp.sum(low.astype(jnp.float32), axis=0, keepdims=True)


def attention(joined, grad_mixed, lanes, first, last, earlier=None):
    rows, width = grad_mixed.shape
    block = min(256, LENGTH)
    pairs, block_count = width // PAIR, LENGTH // block
    row_block = pl.BlockSpec((block, PAIR), lambda p, i: (i, first + p))
    table = pl.BlockSpec((LENGTH, PAIR), lambda p, i: (0, 0))
    kept = () if earlier is None else tuple(earlier)
    kernel = functools.partial(attention_kernel, block=block, block_count=block_count)

    def body(*refs):
        kernel(*refs[:7], *refs[7 + len(kept) :])

    return pl.pallas_call(
        body,
        grid=(last - first, block_count),
        in_specs=[
            row_block,
            pl.BlockSpec((LENGTH, PAIR), lambda p, i: (0, pairs + first + p)),
            pl.BlockSpec((LENGTH, PAIR), lambda p, i: (0, 2 * pairs + first + p)),
            row_block,
            table,
            table,
            table,
        ]
        + [pl.BlockSpec(memory_space=pl.ANY)] * len(kept),
        out_specs=[
            row_block,
            pl.BlockSpec((3, LENGTH, PAIR), lambda p, i: (0, 0, first + p)),
            pl.BlockSpec((3, 1, PAIR), lambda p, i: (0, 0, first + p)),
        ],
        out_shape=[
            jax.ShapeDtypeStruct((rows, width), jnp.bfloat16),
            jax.ShapeDtypeStruct((3, rows, width), jnp.bfloat16),
            jax.ShapeDtypeStruct((3, 1, width), jnp.float32),
        ],
        scratch_shapes=[
            pltpu.VMEM((PAIR, LENGTH), jnp.bfloat16),
            pltpu.VMEM((PAIR, LENGTH), jnp.bfloat16),
            pltpu.VMEM((LENGTH, PAIR), jnp.float32),
            pltpu.VMEM((LENGTH, PAIR), jnp.float32),
            pltpu.VMEM((LENGTH, PAIR), jnp.float32),
        ],
        input_output_aliases={7 + i: i for i in range(len(kept))},
        compiler_params=pltpu.CompilerParams(vmem_limit_bytes=60 * MIB),
        cost_estimate=pl.CostEstimate(
            flops=60000 * MIB * (last - first) // 4 * 2, bytes_accessed=16 * MIB, transcendentals=0
        ),
    )(joined, joined, joined, grad_mixed, *lanes, *kept)


def norm_kernel(starts_ref, gain_ref, shift_ref, *refs):
    count = (len(refs) - 5) // 3
    pieces = refs[:count]
    raw, normed, mean_ref, root_ref = refs[count : count + 4]
    buffers = refs[count + 4 : 2 * count + 4]
    results = refs[2 * count + 4 : 3 * count + 4]
    sems = refs[-1]
    for slot in range(count):
        pltpu.make_async_copy(pieces[slot], buffers[slot], sems.at[0, slot]).start()
    writes = []
    for slot in range(count):
        buffer, result = buffers[slot], results[slot]
        size = buffer.shape[0]
        where = pl.ds(pl.multiple_of(starts_ref[slot], size), size)
        pltpu.make_async_copy(pieces[slot], buffer, sems.at[0, slot]).wait()
        write = pltpu.make_async_copy(buffer, raw.at[where, :], sems.at[1, slot])
        write.start()
        writes.append(write)
        chunk = min(128, size)

        @pl.loop(0, size // chunk)
        def _(step, buffer=buffer, result=result, slot=slot):
            here = pl.ds(pl.multiple_of(step * chunk, chunk), chunk)
            rows = buffer[here, :].astype(jnp.float32)
            mean = jnp.mean(rows, axis=-1, keepdims=True)
            centred = rows - mean
            variance = jnp.mean(centred * centred, axis=-1, keepdims=True)
            root = lax.rsqrt(variance + epsilon)
            out = centred * root * gain_ref[...] + shift_ref[...]
            result[here, :] = out.astype(result.dtype)
            there = pl.ds(pl.multiple_of(starts_ref[slot] + step * chunk, chunk), chunk)
            mean_ref[there, :] = mean
            root_ref[there, :] = root

        write = pltpu.make_async_copy(result, normed.at[where, :], sems.at[2, slot])
        write.start()
        writes.append(write)
    for write in writes:
        write.wait()


def norm_rows(pieces, gain, shift):
    depth = gain.shape[0]
    total = sum(piece.shape[0] for _, piece in pieces)
    count = len(pieces)
    low = jnp.bfloat16
    starts = jnp.stack([jnp.asarray(start, jnp.int32) for start, _ in pieces])
    any_space = pl.BlockSpec(memory_space=pl.ANY)
    vmem = pl.BlockSpec(memory_space=pltpu.VMEM)
    stage = [pltpu.VMEM(piece.shape, low) for _, piece in pieces]
    return pl.pallas_call(
        norm_kernel,
        in_specs=[pl.BlockSpec(memory_space=pltpu.SMEM), vmem, vmem] + [any_space] * count,
        out_specs=[any_space, any_space, vmem, vmem],
        out_shape=[
            jax.ShapeDtypeStruct((total, depth), low),
            jax.ShapeDtypeStruct((total, depth), low),
            jax.ShapeDtypeStruct((total, 1), jnp.float32),
            jax.ShapeDtypeStruct((total, 1), jnp.float32),
        ],
        scratch_shapes=stage + stage + [pltpu.SemaphoreType.DMA((3, count))],
        compiler_params=pltpu.CompilerParams(vmem_limit_bytes=60 * MIB),
        cost_estimate=pl.CostEstimate(flops=0, bytes_accessed=24 * MIB, transcendentals=0),
    )(starts, gain.reshape(1, depth), shift.reshape(1, depth), *[piece for _, piece in pieces])


def grad_normed_kernel(
    joined_ref, qkv_ref, hidden_ref, up_ref, x_ref, mean_ref, root_ref, out_ref, gain_ref, shift_ref
):
    total = lax.dot_general(
        hidden_ref[...], up_ref[...], ROWS_BY_ROWS, preferred_element_type=jnp.float32
    )
    for slot in range(3):
        total += lax.dot_general(
            joined_ref[slot], qkv_ref[slot], ROWS_BY_ROWS, preferred_element_type=jnp.float32
        )
    out_ref[...] = total.astype(out_ref.dtype)

    @pl.when(pl.program_id(1) == 0)
    def _():
        gain_ref[...] = jnp.zeros_like(gain_ref)
        shift_ref[...] = jnp.zeros_like(shift_ref)

    hat = (x_ref[...].astype(jnp.float32) - mean_ref[...]) * root_ref[...]
    gain_ref[...] += jnp.sum(total * hat, axis=0, keepdims=True)
    shift_ref[...] += jnp.sum(total, axis=0, keepdims=True)


def grad_normed_rows(grad_joined, full_qkv, grad_hidden, full_up, x, mean, root, first, last):
    rows, hidden = grad_hidden.shape
    width = grad_joined.shape[2]
    block, columns = min(1024, rows), min(512, last - first)
    skip = first // columns
    thin = pl.BlockSpec((block, 1), lambda j, i: (i, 0))
    line = pl.BlockSpec((1, columns), lambda j, i: (0, j))
    return pl.pallas_call(
        grad_normed_kernel,
        grid=((last - first) // columns, rows // block),
        in_specs=[
            pl.BlockSpec((3, block, width), lambda j, i: (0, i, 0)),
            pl.BlockSpec((3, columns, width), lambda j, i: (0, skip + j, 0)),
            pl.BlockSpec((block, hidden), lambda j, i: (i, 0)),
            pl.BlockSpec((columns, hidden), lambda j, i: (skip + j, 0)),
            pl.BlockSpec((block, columns), lambda j, i: (i, skip + j)),
            thin,
            thin,
        ],
        out_specs=[pl.BlockSpec((block, columns), lambda j, i: (i, j)), line, line],
        out_shape=[
            jax.ShapeDtypeStruct((rows, last - first), jnp.bfloat16),
            jax.ShapeDtypeStruct((1, last - first), jnp.float32),
            jax.ShapeDtypeStruct((1, last - first), jnp.float32),
        ],
        compiler_params=pltpu.CompilerParams(vmem_limit_bytes=60 * MIB),
        cost_estimate=pl.CostEstimate(
            flops=2 * rows * (hidden + 3 * width) * (last - first),
            bytes_accessed=50 * MIB,
            transcendentals=0,
        ),
    )(grad_joined, full_qkv, grad_hidden, full_up, x, mean, root)


def on_device(
    tokens,
    norm_gain,
    norm_shift,
    weight_qkv,
    bias_qkv,
    weight_dense,
    weight_up,
    bias_up,
    weight_down,
    bias_out,
    cotangent,
):
    f32, low = jnp.float32, jnp.bfloat16
    depth = tokens.shape[1]
    local_rows = tokens.shape[0]
    tensor_index = lax.axis_index("tensor")

    full_up = lax.all_gather(weight_up, "dp", axis=0, tiled=True)
    token_parts = gather_start(tokens)
    lanes = lane_tables(LENGTH)
    out_part = jnp.sum(cotangent, axis=0, dtype=f32)
    lanes, out_part, token_parts = after((lanes, out_part, token_parts))
    full_qkv = lax.all_gather(
        after(jnp.transpose(weight_qkv, (1, 0, 2)), token_parts), "dp", axis=1, tiled=True
    )
    token_parts = gather_pass(token_parts)
    grad_parts = gather_start(after(cotangent, token_parts[:3]))
    all_tokens, gathered, mean, root = norm_rows(
        gathered_pieces(token_parts), norm_gain, norm_shift
    )
    full_dense = lax.all_gather(after(weight_dense, gathered), "dp", axis=1, tiled=True)

    active, slope = hidden_rows(gathered, full_up, bias_up)
    grad_parts, active = after((grad_parts, active))
    full_down = lax.all_gather(after(weight_down, grad_parts), "dp", axis=1, tiled=True)
    grad_parts = gather_pass(grad_parts)
    joined = joined_rows(after(gathered, active, grad_parts[:3]), full_qkv, bias_qkv, lanes)
    grad_parts, joined = after((grad_parts, joined))
    grad_rows = gather_end(grad_parts)
    dense_parts = gather_start(after(full_dense, joined))
    grad_down = jnp.einsum("tf,td->fd", active, grad_rows, preferred_element_type=f32).astype(low)
    grad_mixed = jnp.einsum(
        "td,kd->tk", after(grad_rows, grad_down), full_dense, preferred_element_type=f32
    ).astype(low)
    grad_down_sum = lax.psum_scatter(grad_down, "dp", scatter_dimension=1, tiled=True)

    pairs = grad_mixed.shape[1] // PAIR
    middle = pairs // 2
    part = attention(joined, grad_mixed, lanes, 0, middle)
    dense_parts, part = after((dense_parts, part))
    dense_parts = gather_pass(dense_parts)

    feed = jnp.dot(after(active, part), full_down, preferred_element_type=f32).astype(low)
    feed, dense_parts = after((feed, dense_parts))
    feed_parts = scatter_send(scatter_cut(feed))
    grad_hidden, bias_up_part = grad_hidden_rows(after(grad_rows, feed), full_down, slope)
    dense_rows = gather_end(dense_parts)
    grad_up = jnp.einsum(
        "td,tf->df", after(gathered, dense_rows), grad_hidden, preferred_element_type=f32
    ).astype(low)
    grad_up, feed_parts = after((grad_up, feed_parts))
    grad_up_sum = lax.psum_scatter(
        after(grad_up, grad_down_sum), "dp", scatter_dimension=0, tiled=True
    )
    feed_parts = scatter_pass(scatter_fold(feed_parts))
    mixed, grad_joined, bias_qkv_part = attention(
        after(joined, grad_up), grad_mixed, lanes, middle, pairs, part
    )
    mixed, grad_joined, feed_parts = after((mixed, grad_joined, feed_parts))

    mixed_parts = exchange_start(mixed)
    grad_qkv = jnp.einsum("td,jtc->jdc", gathered, grad_joined, preferred_element_type=f32)
    grad_qkv, mixed_parts = after((grad_qkv.astype(low), mixed_parts))
    grad_qkv_sum = lax.psum_scatter(
        after(grad_qkv, grad_up_sum), "dp", scatter_dimension=1, tiled=True
    )
    half = depth // 2
    sources = full_qkv, grad_hidden, full_up, all_tokens, mean, root
    left = grad_normed_rows(after(grad_joined, grad_qkv), *sources, 0, half)
    left_cuts = after(scatter_cut(left[0]), left)
    left_parts = scatter_send(left_cuts)
    right = grad_normed_rows(after(grad_joined, left_cuts), *sources, half, depth)
    sums = jnp.stack(
        [
            jnp.concatenate([left[1][0], right[1][0]]),
            jnp.concatenate([left[2][0], right[2][0]]),
            out_part,
        ]
    )
    left_parts, sums, right = after((left_parts, sums, right))
    left_parts = scatter_fold(left_parts)
    right_cuts = scatter_cut(right[0])
    left_parts, right_cuts, sums, mixed = after((left_parts, right_cuts, sums, mixed))
    over_group = exchange_sum(sums, "tensor")
    left_parts = scatter_pass(left_parts)
    right_parts = scatter_send(right_cuts)
    grad_dense = jnp.einsum("tk,td->kd", mixed, grad_rows, preferred_element_type=f32).astype(low)
    grad_dense_sum = lax.psum_scatter(
        after(grad_dense, grad_qkv_sum), "dp", scatter_dimension=1, tiled=True
    )
    over_group, mixed_parts = after((over_group, mixed_parts), grad_dense)
    bias_size = bias_qkv.size
    over_dp = exchange_sum(
        jnp.concatenate(
            [over_group.reshape(-1), bias_qkv_part.reshape(-1), bias_up_part.reshape(-1)]
        ).reshape(-1, 128),
        "dp",
    ).reshape(-1)
    attended = jnp.dot(exchange_end(mixed_parts), dense_rows, preferred_element_type=f32)
    token_rows = tokens.astype(f32)
    block_out = (token_rows + attended + scatter_end(feed_parts) + bias_out).astype(low)
    done = block_out, grad_up_sum.astype(f32), grad_down_sum.astype(f32), over_dp
    right_parts, left_parts, done = after((right_parts, left_parts, done))
    block_out, grad_up_sum, grad_down_sum, over_dp = done
    right_parts = scatter_pass(scatter_fold(right_parts))
    grad_gain, grad_shift, grad_bias_out = over_dp[: 3 * depth].reshape(3, depth)
    grad_bias_qkv = over_dp[3 * depth : 3 * depth + bias_size].reshape(bias_qkv.shape)
    grad_bias_up = over_dp[3 * depth + bias_size :]

    grad_normed = jnp.concatenate([scatter_end(left_parts), scatter_end(right_parts)], axis=1)
    own_mean = lax.dynamic_slice_in_dim(mean, tensor_index * local_rows, local_rows, 0)
    own_root = lax.dynamic_slice_in_dim(root, tensor_index * local_rows, local_rows, 0)
    hat = (token_rows - own_mean) * own_root
    scaled = grad_normed * norm_gain
    grad_input = own_root * (
        scaled
        - jnp.mean(scaled, axis=-1, keepdims=True)
        - hat * jnp.mean(scaled * hat, axis=-1, keepdims=True)
    )
    grad_tokens = (cotangent.astype(f32) + grad_input).astype(low)
    return (
        block_out,
        grad_tokens,
        grad_gain,
        grad_shift,
        jnp.transpose(grad_qkv_sum, (1, 0, 2)).astype(f32),
        grad_bias_qkv,
        grad_dense_sum.astype(f32),
        grad_up_sum,
        grad_bias_up,
        grad_down_sum,
        grad_bias_out,
    )


def solution(mesh):
    in_specs = (
        P(("dp", "tensor"), None),
        P(),
        P(),
        P("dp", None, "tensor"),
        P(None, "tensor"),
        P("tensor", "dp"),
        P("dp", "tensor"),
        P("tensor"),
        P("tensor", "dp"),
        P(),
        P(("dp", "tensor"), None),
    )
    out_specs = (
        P(("dp", "tensor"), None),
        P(("dp", "tensor"), None),
        P(),
        P(),
        P("dp", None, "tensor"),
        P(None, "tensor"),
        P("tensor", "dp"),
        P("dp", "tensor"),
        P("tensor"),
        P("tensor", "dp"),
        P(),
    )
    return jax.shard_map(
        on_device, mesh=mesh, in_specs=in_specs, out_specs=out_specs, check_vma=False
    )
```

```python
import functools

import jax
import jax.numpy as jnp
from jax import lax
from jax.experimental import pallas as pl
from jax.experimental.pallas import tpu as pltpu
from jax.sharding import PartitionSpec as P

HEAD_DIM = 64
ROT = 32
LENGTH = 2048
PAIR = 2 * HEAD_DIM

epsilon = 1e-05
masked_score = -1e30
MIB = 1024 * 1024
VMEM_BYTES = 64 * MIB - 256 * 1024
ROWS_BY_ROWS = (((1,), (1,)), ((), ()))
COLUMNS_BY_COLUMNS = (((0,), (0,)), ((), ()))


SHORT = pl.CostEstimate(flops=1, bytes_accessed=1, transcendentals=0)


def after(value, *earlier):
    return lax.optimization_barrier((value,) + earlier)[0]


def swap(value, axis, bit):
    count = lax.axis_size(axis)
    return lax.ppermute(value, axis, [(i, i ^ bit) for i in range(count)])


def gather_start(block):
    if lax.axis_size("tensor") != 4:
        return (lax.all_gather(block, "tensor", axis=0, tiled=True),)
    return block, swap(block, "tensor", 1), swap(block, "tensor", 2)


def halves_kernel(one_ref, two_ref, low_ref, high_ref):
    half = one_ref.shape[0] // 2
    low_ref[...] = one_ref[:half, :]
    high_ref[...] = two_ref[half:, :]


def gather_pass(parts):
    if len(parts) == 1:
        return parts
    block, one, two = parts
    rows, depth = block.shape
    half = jax.ShapeDtypeStruct((rows // 2, depth), block.dtype)
    low, high = pl.pallas_call(
        halves_kernel,
        out_shape=[half, half],
        compiler_params=pltpu.CompilerParams(vmem_limit_bytes=VMEM_BYTES),
        cost_estimate=SHORT,
    )(one, two)
    return block, one, two, swap(low, "tensor", 2), swap(high, "tensor", 1)


def gathered_pieces(parts):
    if len(parts) == 1:
        return [(0, parts[0])]
    block, one, two, low, high = parts
    rows = block.shape[0]
    me = lax.axis_index("tensor")
    return [
        (me * rows, block),
        ((me ^ 1) * rows, one),
        ((me ^ 2) * rows, two),
        ((me ^ 3) * rows, low),
        ((me ^ 3) * rows + rows // 2, high),
    ]


def wide(piece):
    return piece.astype(jnp.float32)


def owner_cuts(total):
    count = lax.axis_size("tensor")
    rows = total // count
    me = lax.axis_index("tensor")
    order = [me ^ bit for bit in (3, 1, 2, 0)] if count == 4 else list(range(count))
    starts = jnp.stack([jnp.asarray(owner * rows, jnp.int32) for owner in order])
    return starts, count, 2 if count == 4 else 1


def scatter_send(cuts):
    if lax.axis_size("tensor") != 4:
        whole = wide(jnp.concatenate(cuts))
        return (lax.psum_scatter(whole, "tensor", scatter_dimension=0, tiled=True),)
    far_low, far_high, one_low, one_high, two_low, two_high, low, high = cuts
    return (
        swap(far_low, "tensor", 1),
        swap(far_high, "tensor", 2),
        swap(one_low, "tensor", 1),
        swap(two_high, "tensor", 2),
        two_low,
        one_high,
        low,
        high,
    )


def fold_kernel(a_ref, b_ref, c_ref, d_ref, ab_ref, cd_ref):
    ab_ref[...] = (wide(a_ref[...]) + wide(b_ref[...])).astype(ab_ref.dtype)
    cd_ref[...] = (wide(c_ref[...]) + wide(d_ref[...])).astype(cd_ref.dtype)


def scatter_fold(parts):
    if len(parts) == 1:
        return parts
    first_far, second_far, first_near, second_near, two_low, one_high, low, high = parts
    shape = jax.ShapeDtypeStruct(low.shape, low.dtype)
    forward = pl.pallas_call(
        fold_kernel,
        out_shape=[shape, shape],
        compiler_params=pltpu.CompilerParams(vmem_limit_bytes=VMEM_BYTES),
    )(two_low, first_far, one_high, second_far)
    return (*forward, first_near, second_near, low, high)


def scatter_pass(parts):
    if len(parts) == 1:
        return parts
    two_low, one_high, first_near, second_near, low, high = parts
    return (
        swap(two_low, "tensor", 2),
        swap(one_high, "tensor", 1),
        first_near,
        second_near,
        low,
        high,
    )


def exchange_start(columns):
    if lax.axis_size("tensor") != 4:
        return (lax.all_to_all(columns, "tensor", 0, 1, tiled=True),)
    rows = columns.shape[0] // 4
    me = lax.axis_index("tensor")
    pieces = []
    for bit in range(4):
        piece = lax.dynamic_slice_in_dim(columns, (me ^ bit) * rows, rows, 0)
        pieces.append(swap(piece, "tensor", bit) if bit else piece)
    return tuple(pieces)


def exchange_sum(value, axis, step=1):
    parts = [value]
    for bit in range(step, lax.axis_size(axis), step):
        parts.append(swap(value, axis, bit))
    return functools.reduce(lambda a, b: a + b, parts)


def lane_tables(row_total):
    half_rot = ROT // 2
    positions = (jnp.arange(row_total, dtype=jnp.int32) % LENGTH).astype(jnp.float32)
    inverse = 10000.0 ** (-(2.0 * jnp.arange(half_rot, dtype=jnp.float32)) / ROT)
    angles = positions[:, None] * inverse[None, :]
    cosine, sine = jnp.cos(angles), jnp.sin(angles)
    ones = jnp.ones((row_total, HEAD_DIM - ROT), jnp.float32)
    zeros = jnp.zeros((row_total, half_rot), jnp.float32)
    rest = jnp.zeros((row_total, HEAD_DIM - ROT), jnp.float32)
    cos_lanes = jnp.concatenate([cosine, cosine, ones] * 2, axis=1)
    from_above = jnp.concatenate([-sine, zeros, rest] * 2, axis=1)
    from_below = jnp.concatenate([zeros, sine, rest] * 2, axis=1)
    return cos_lanes, from_above, from_below


def turn(field, cos_lanes, from_above, from_below):
    half_rot = ROT // 2
    above = pltpu.roll(field, PAIR - half_rot, 1)
    below = pltpu.roll(field, half_rot, 1)
    return field * cos_lanes + above * from_above + below * from_below


def turn_back(field, cos_lanes, from_above, from_below):
    half_rot = ROT // 2
    above = pltpu.roll(field, PAIR - half_rot, 1)
    below = pltpu.roll(field, half_rot, 1)
    return field * cos_lanes - above * from_above - below * from_below


def joined_kernel(x_ref, w_ref, bias_ref, cos_ref, above_ref, below_ref, out_ref):
    width = out_ref.shape[1]
    chunk = min(256, width)
    slot = pl.program_id(0)

    def product(start):
        columns = slice(start, start + chunk)
        part = jnp.dot(x_ref[...], w_ref[0, :, columns], preferred_element_type=jnp.float32)
        return part + bias_ref[0, :, columns]

    @pl.when(slot < 2)
    def _():
        for start in range(0, width, chunk):
            part = product(start)
            for shift in range(0, chunk, PAIR):
                lanes = part[:, shift : shift + PAIR]
                turned = turn(lanes, cos_ref[...], above_ref[...], below_ref[...])
                columns = slice(start + shift, start + shift + PAIR)
                out_ref[:, columns] = turned.astype(out_ref.dtype)

    @pl.when(slot == 2)
    def _():
        for start in range(0, width, chunk):
            out_ref[:, start : start + chunk] = product(start).astype(out_ref.dtype)


def joined_rows(x, w, bias, lanes):
    rows, depth = x.shape
    width = w.shape[2]
    block = min(1024, rows)
    return pl.pallas_call(
        joined_kernel,
        grid=(3, rows // block),
        in_specs=[
            pl.BlockSpec((block, depth), lambda j, i: (i, 0)),
            pl.BlockSpec((1, depth, width), lambda j, i: (j, 0, 0)),
            pl.BlockSpec((1, 1, width), lambda j, i: (j, 0, 0)),
        ]
        + [pl.BlockSpec((block, PAIR), lambda j, i: (i, 0))] * 3,
        out_specs=pl.BlockSpec((block, width), lambda j, i: (i, j)),
        out_shape=jax.ShapeDtypeStruct((rows, 3 * width), jnp.bfloat16),
        compiler_params=pltpu.CompilerParams(vmem_limit_bytes=VMEM_BYTES),
        cost_estimate=SHORT,
    )(x, w, bias.reshape(3, 1, width), *lanes)


def hidden_kernel(x_ref, w_ref, bias_ref, active_ref, slope_ref):
    hidden = jnp.dot(x_ref[...], w_ref[...], preferred_element_type=jnp.float32) + bias_ref[...]
    scale = (2.0 / jnp.pi) ** 0.5
    square = hidden * hidden
    inner = scale * hidden * (1.0 + 0.044715 * square)
    bent = jnp.tanh(inner)
    half = 0.5 * (1.0 + bent)
    active_ref[...] = (hidden * half).astype(active_ref.dtype)
    growth = scale * (1.0 + (3.0 * 0.044715) * square)
    slope = half + 0.5 * hidden * (1.0 - bent * bent) * growth
    slope_ref[...] = slope.astype(slope_ref.dtype)


def hidden_rows(x, w, bias):
    rows, depth = x.shape
    width = w.shape[1]
    block, columns = min(1024, rows), min(1024, width)
    return pl.pallas_call(
        hidden_kernel,
        grid=(width // columns, rows // block),
        in_specs=[
            pl.BlockSpec((block, depth), lambda j, i: (i, 0)),
            pl.BlockSpec((depth, columns), lambda j, i: (0, j)),
            pl.BlockSpec((1, columns), lambda j, i: (0, j)),
        ],
        out_specs=[pl.BlockSpec((block, columns), lambda j, i: (i, j))] * 2,
        out_shape=[jax.ShapeDtypeStruct((rows, width), jnp.bfloat16)] * 2,
        compiler_params=pltpu.CompilerParams(vmem_limit_bytes=VMEM_BYTES),
        cost_estimate=SHORT,
    )(x, w, bias.reshape(1, width))


def whole_call(kernel, in_specs, out_specs, out_shape, scratch):
    return pl.pallas_call(
        kernel,
        in_specs=in_specs,
        out_specs=out_specs,
        out_shape=out_shape,
        scratch_shapes=scratch,
        compiler_params=pltpu.CompilerParams(vmem_limit_bytes=VMEM_BYTES),
        cost_estimate=SHORT,
    )


def columns_of(ref, index, size):
    return ref.at[:, pl.ds(pl.multiple_of(index * size, size), size)]


def rows_of(ref, index, size):
    return ref.at[pl.ds(pl.multiple_of(index * size, size), size), :]


def nt_dot(a, b):
    return lax.dot_general(a, b, ROWS_BY_ROWS, preferred_element_type=jnp.float32)


def tn_dot(a, b):
    return lax.dot_general(a, b, COLUMNS_BY_COLUMNS, preferred_element_type=jnp.float32)


ANY = pl.BlockSpec(memory_space=pl.ANY)
SMEM = pl.BlockSpec(memory_space=pltpu.SMEM)
VMEM = pl.BlockSpec(memory_space=pltpu.VMEM)


def tile_loop(count, tiles, tile_sems, where, compute):
    def write(step, slot):
        return pltpu.make_async_copy(tiles.at[slot], where(step), tile_sems.at[slot])

    @pl.loop(0, count)
    def _(step):
        slot = lax.rem(step, 2)

        @pl.when(step >= 2)
        def _():
            write(step, slot).wait()

        tiles[slot] = compute(step).astype(tiles.dtype)
        write(step, slot).start()

    for step in range(max(count - 2, 0), count):
        write(step, step % 2).wait()


def first_grads_kernel(starts_ref, active, dense, *refs):
    count = len(refs) - 11
    pieces = refs[:count]
    rows_out, mixed_out, down_out, grad_buf, active_buf, dense_buf, tiles = refs[count:-4]
    piece_sems, load_sems, row_sems, tile_sems = refs[-4:]
    _, rows, half = grad_buf.shape
    blocks, _, block = active_buf.shape

    def piece_copy(slot, side):
        size = pieces[slot].shape[0]
        there = pl.ds(pl.multiple_of(starts_ref[slot], size), size)
        return pltpu.make_async_copy(
            pieces[slot].at[:, pl.ds(side * half, half)],
            grad_buf.at[side, there, :],
            piece_sems.at[slot, side],
        )

    def active_copy(index):
        return pltpu.make_async_copy(
            columns_of(active, index, block), active_buf.at[index], load_sems.at[index]
        )

    def row_copy(side):
        return pltpu.make_async_copy(
            grad_buf.at[side], rows_out.at[:, pl.ds(side * half, half)], row_sems.at[side]
        )

    dense_copy = pltpu.make_async_copy(dense, dense_buf, load_sems.at[blocks])
    dense_copy.start()
    for slot in range(count):
        for side in range(2):
            piece_copy(slot, side).start()
    for index in range(blocks):
        active_copy(index).start()
    dense_copy.wait()
    for slot in range(count):
        for side in range(2):
            piece_copy(slot, side).wait()
        size = pieces[slot].shape[0]
        chunk = min(512, size)

        @pl.loop(0, size // chunk)
        def _(step, slot=slot, chunk=chunk):
            here = pl.ds(pl.multiple_of(starts_ref[slot] + step * chunk, chunk), chunk)
            mixed_out[here, :] = (
                nt_dot(grad_buf[0, here, :], dense_buf[:, :half])
                + nt_dot(grad_buf[1, here, :], dense_buf[:, half:])
            ).astype(mixed_out.dtype)

    for side in range(2):
        row_copy(side).start()
    for index in range(blocks):
        active_copy(index).wait()
    tile_loop(
        2 * blocks,
        tiles,
        tile_sems,
        lambda step: down_out.at[
            pl.ds(pl.multiple_of(lax.div(step, 2) * block, block), block),
            pl.ds(pl.multiple_of(lax.rem(step, 2) * half, half), half),
        ],
        lambda step: tn_dot(active_buf[lax.div(step, 2)], grad_buf[lax.rem(step, 2)]),
    )
    for side in range(2):
        row_copy(side).wait()


def first_grads(pieces, active, dense):
    low = jnp.bfloat16
    rows, hidden = active.shape
    width, depth = dense.shape
    half, block = depth // 2, min(512, hidden)
    count = len(pieces)
    starts = jnp.stack([jnp.asarray(start, jnp.int32) for start, _ in pieces])
    return whole_call(
        first_grads_kernel,
        [SMEM] + [ANY] * (2 + count),
        [ANY, VMEM, ANY],
        [
            jax.ShapeDtypeStruct((rows, depth), low),
            jax.ShapeDtypeStruct((rows, width), low),
            jax.ShapeDtypeStruct((hidden, depth), low),
        ],
        [
            pltpu.VMEM((2, rows, half), low),
            pltpu.VMEM((hidden // block, rows, block), low),
            pltpu.VMEM((width, depth), low),
            pltpu.VMEM((2, block, half), low),
            pltpu.SemaphoreType.DMA((count, 2)),
            pltpu.SemaphoreType.DMA((hidden // block + 1,)),
            pltpu.SemaphoreType.DMA((2,)),
            pltpu.SemaphoreType.DMA((2,)),
        ],
    )(starts, active, dense, *[piece for _, piece in pieces])


def feed_kernel(starts_ref, active, weight, *refs, halves):
    cuts = refs[:-5]
    active_buf, weight_buf, out_buf, load_sems, cut_sems = refs[-5:]
    owners = len(cuts) // halves
    rows = active_buf.shape[0]
    half = weight_buf.shape[2]
    owner_rows = rows // owners
    piece = owner_rows // halves

    def weight_load(side):
        return pltpu.make_async_copy(
            weight.at[:, pl.ds(side * half, half)], weight_buf.at[side], load_sems.at[side]
        )

    def row_load(owner):
        here = pl.ds(pl.multiple_of(starts_ref[owner], owner_rows), owner_rows)
        return pltpu.make_async_copy(
            active.at[here, :], active_buf.at[here, :], load_sems.at[2 + owner]
        )

    weight_load(0).start()
    row_load(0).start()
    weight_load(1).start()
    for owner in range(1, owners):
        row_load(owner).start()

    def cut_copy(owner, part_of, side):
        return pltpu.make_async_copy(
            out_buf.at[side, pl.ds(owner * owner_rows + part_of * piece, piece), :],
            cuts[owner * halves + part_of].at[:, pl.ds(pl.multiple_of(side * half, half), half)],
            cut_sems.at[side, owner * halves + part_of],
        )

    @pl.loop(0, 2 * owners)
    def _(step):
        owner, side = lax.div(step, 2), lax.rem(step, 2)
        for own in range(owners):
            pl.when(step == 2 * own)(row_load(own).wait)
        for own in range(2):
            pl.when(step == own)(weight_load(own).wait)
        here = pl.ds(pl.multiple_of(starts_ref[owner], owner_rows), owner_rows)
        there = pl.ds(pl.multiple_of(owner * owner_rows, owner_rows), owner_rows)
        out_buf[side, there, :] = jnp.dot(
            active_buf[here, :], weight_buf[side], preferred_element_type=jnp.float32
        ).astype(out_buf.dtype)
        for own in range(owners):

            @pl.when(owner == own)
            def _(own=own):
                for part_of in range(halves):
                    cut_copy(own, part_of, side).start()

    for side in range(2):
        for own in range(owners):
            for part_of in range(halves):
                cut_copy(own, part_of, side).wait()


def feed_rows(active, weight):
    low = jnp.bfloat16
    rows, hidden = active.shape
    depth = weight.shape[1]
    half = depth // 2
    starts, owners, halves = owner_cuts(rows)
    cut = jax.ShapeDtypeStruct((rows // owners // halves, depth), low)
    return tuple(
        whole_call(
            functools.partial(feed_kernel, halves=halves),
            [SMEM] + [ANY] * 2,
            [ANY] * (owners * halves),
            [cut] * (owners * halves),
            [
                pltpu.VMEM((rows, hidden), low),
                pltpu.VMEM((2, hidden, half), low),
                pltpu.VMEM((2, rows, half), low),
                pltpu.SemaphoreType.DMA((2 + owners,)),
                pltpu.SemaphoreType.DMA((2, owners * halves)),
            ],
        )(starts, active, weight)
    )


def hidden_grads_kernel(grad_rows, weight, slope, x, hidden_out, up_out, sum_out, *refs):
    grad_buf, weight_buf, slope_buf, x_buf, hidden_buf, tiles = refs[:6]
    load_sems, slope_sems, hidden_sems, tile_sems = refs[6:]
    rows = grad_buf.shape[0]
    parts, _, part = hidden_buf.shape
    x_blocks, _, x_block = x_buf.shape
    chunk = slope_buf.shape[1]
    chunks = rows // chunk

    def load(source, target, index):
        return pltpu.make_async_copy(source, target, load_sems.at[index])

    def grad_load(index):
        here = pl.ds(pl.multiple_of(index * chunk, chunk), chunk)
        return load(grad_rows.at[here, :], grad_buf.at[here, :], index)

    def weight_load(index):
        here = pl.ds(pl.multiple_of(index * part, part), part)
        return load(weight.at[here, :], weight_buf.at[here, :], chunks + index)

    x_loads = [
        load(columns_of(x, i, x_block), x_buf.at[i], chunks + parts + i) for i in range(x_blocks)
    ]

    def slope_copy(step, slot):
        place = (
            pl.ds(pl.multiple_of(lax.rem(step, chunks) * chunk, chunk), chunk),
            pl.ds(pl.multiple_of(lax.div(step, chunks) * part, part), part),
        )
        return pltpu.make_async_copy(slope.at[place], slope_buf.at[slot], slope_sems.at[slot])

    def hidden_copy(index):
        return pltpu.make_async_copy(
            hidden_buf.at[index],
            hidden_out.at[:, pl.ds(index * part, part)],
            hidden_sems.at[index],
        )

    weight_load(0).start()
    grad_load(0).start()
    slope_copy(0, 0).start()
    for index in range(1, chunks):
        grad_load(index).start()
    for index in range(1, parts):
        weight_load(index).start()
    for copy in x_loads:
        copy.start()
    sum_out[...] = jnp.zeros_like(sum_out)

    @pl.loop(0, parts * chunks)
    def _(step):
        slot = lax.rem(step, 2)
        index = lax.div(step, chunks)

        @pl.when(step + 1 < parts * chunks)
        def _():
            slope_copy(step + 1, 1 - slot).start()

        @pl.when(lax.rem(step, chunks) == 0)
        def _():
            weight_load(index).wait()

        @pl.when(index == 0)
        def _():
            grad_load(step).wait()

        slope_copy(step, slot).wait()
        here = pl.ds(pl.multiple_of(lax.rem(step, chunks) * chunk, chunk), chunk)
        units = pl.ds(pl.multiple_of(index * part, part), part)
        product = nt_dot(grad_buf[here, :], weight_buf[units, :])
        low = (product * wide(slope_buf[slot])).astype(hidden_buf.dtype)
        hidden_buf[index, here, :] = low
        sum_out[index] += jnp.sum(wide(low), axis=0, keepdims=True)

    for index in range(parts):
        hidden_copy(index).start()
    for copy in x_loads:
        copy.wait()
    tile_loop(
        x_blocks * parts,
        tiles,
        tile_sems,
        lambda step: up_out.at[
            pl.ds(pl.multiple_of(lax.div(step, parts) * x_block, x_block), x_block),
            pl.ds(pl.multiple_of(lax.rem(step, parts) * part, part), part),
        ],
        lambda step: tn_dot(x_buf[lax.div(step, parts)], hidden_buf[lax.rem(step, parts)]),
    )
    for index in range(parts):
        hidden_copy(index).wait()


def hidden_grads(grad_rows, weight, slope, x):
    low = jnp.bfloat16
    rows, depth = grad_rows.shape
    hidden = weight.shape[0]
    part, x_block, chunk = min(1024, hidden), min(512, depth), min(512, rows)
    return whole_call(
        hidden_grads_kernel,
        [ANY] * 4,
        [ANY, ANY, VMEM],
        [
            jax.ShapeDtypeStruct((rows, hidden), low),
            jax.ShapeDtypeStruct((depth, hidden), low),
            jax.ShapeDtypeStruct((hidden // part, 1, part), jnp.float32),
        ],
        [
            pltpu.VMEM((rows, depth), low),
            pltpu.VMEM((hidden, depth), low),
            pltpu.VMEM((2, chunk, part), low),
            pltpu.VMEM((depth // x_block, rows, x_block), low),
            pltpu.VMEM((hidden // part, rows, part), low),
            pltpu.VMEM((2, x_block, part), low),
            pltpu.SemaphoreType.DMA((rows // chunk + hidden // part + depth // x_block,)),
            pltpu.SemaphoreType.DMA((2,)),
            pltpu.SemaphoreType.DMA((hidden // part,)),
            pltpu.SemaphoreType.DMA((2,)),
        ],
    )(grad_rows, weight, slope, x)


def qkv_grads_kernel(x, joined, out, x_buf, joined_buf, tiles, x_sems, joined_sems, tile_sems):
    blocks, _, block = x_buf.shape
    x_loads = [
        pltpu.make_async_copy(columns_of(x, i, block), x_buf.at[i], x_sems.at[i])
        for i in range(blocks)
    ]
    joined_loads = [
        pltpu.make_async_copy(joined.at[i], joined_buf.at[i], joined_sems.at[i]) for i in range(3)
    ]
    joined_loads[0].start()
    for copy in x_loads + joined_loads[1:]:
        copy.start()

    def compute(step):
        for index in range(3):
            pl.when(step == index * blocks)(joined_loads[index].wait)
        for index in range(blocks):
            pl.when(step == index)(x_loads[index].wait)
        return tn_dot(x_buf[lax.rem(step, blocks)], joined_buf[lax.div(step, blocks)])

    tile_loop(
        3 * blocks,
        tiles,
        tile_sems,
        lambda step: rows_of(out.at[lax.div(step, blocks)], lax.rem(step, blocks), block),
        compute,
    )


def qkv_grads(x, joined):
    low = jnp.bfloat16
    rows, depth = x.shape
    width = joined.shape[2]
    block = min(1024, depth)
    return whole_call(
        qkv_grads_kernel,
        [ANY] * 2,
        ANY,
        jax.ShapeDtypeStruct((3, depth, width), low),
        [
            pltpu.VMEM((depth // block, rows, block), low),
            pltpu.VMEM((3, rows, width), low),
            pltpu.VMEM((2, block, width), low),
            pltpu.SemaphoreType.DMA((depth // block,)),
            pltpu.SemaphoreType.DMA((3,)),
            pltpu.SemaphoreType.DMA((2,)),
        ],
    )(x, joined)


def normed_grads_kernel(
    starts_ref, joined, qkv, hidden, up, x, mean_ref, root_ref, gain_ref, shift_ref, *refs, halves
):
    cuts = refs[:-8]
    joined_buf, qkv_buf, hidden_buf, up_buf, x_buf, out_buf, load_sems, cut_sems = refs[-8:]
    owners = len(cuts) // halves
    rows = hidden_buf.shape[0]
    owner_rows = rows // owners
    piece = owner_rows // halves

    def load(source, target, index):
        return pltpu.make_async_copy(source, target, load_sems.at[index])

    def row_loads(owner):
        here = pl.ds(pl.multiple_of(starts_ref[owner], owner_rows), owner_rows)
        at = 4 + owner * 3
        return (
            load(hidden.at[here, :], hidden_buf.at[here, :], at),
            load(joined.at[:, here, :], joined_buf.at[:, here, :], at + 1),
            load(x.at[here, :], x_buf.at[here, :], at + 2),
        )

    weights = [load(up, up_buf, 0), load(qkv, qkv_buf, 1)]
    weights[0].start()
    for copy in row_loads(0):
        copy.start()
    weights[1].start()
    for owner in range(1, owners):
        for copy in row_loads(owner):
            copy.start()
    gain_ref[...] = jnp.zeros_like(gain_ref)
    shift_ref[...] = jnp.zeros_like(shift_ref)
    for copy in weights:
        copy.wait()

    def cut_copy(owner, part_of):
        return pltpu.make_async_copy(
            out_buf.at[pl.ds(owner * owner_rows + part_of * piece, piece), :],
            cuts[owner * halves + part_of],
            cut_sems.at[owner * halves + part_of],
        )

    @pl.loop(0, owners)
    def _(owner):
        for copy in row_loads(owner):
            copy.wait()
        here = pl.ds(pl.multiple_of(starts_ref[owner], owner_rows), owner_rows)
        there = pl.ds(pl.multiple_of(owner * owner_rows, owner_rows), owner_rows)
        columns = up_buf.shape[0]
        chunk = min(512, columns)
        for start in range(0, columns, chunk):
            mine = slice(start, start + chunk)
            total = nt_dot(hidden_buf[here, :], up_buf[mine, :])
            for slot in range(3):
                total += nt_dot(joined_buf[slot, here, :], qkv_buf[slot, mine, :])
            out_buf[there, mine] = total.astype(out_buf.dtype)
            hat = (wide(x_buf[here, mine]) - mean_ref[here, :]) * root_ref[here, :]
            gain_ref[:, mine] += jnp.sum(total * hat, axis=0, keepdims=True)
            shift_ref[:, mine] += jnp.sum(total, axis=0, keepdims=True)
        for own in range(owners):

            @pl.when(owner == own)
            def _(own=own):
                for part_of in range(halves):
                    cut_copy(own, part_of).start()

    for own in range(owners):
        for part_of in range(halves):
            cut_copy(own, part_of).wait()


def normed_grads(joined, qkv, hidden, up, x, mean, root, first, last):
    low = jnp.bfloat16
    rows, units = hidden.shape
    width = joined.shape[2]
    columns = last - first
    starts, owners, halves = owner_cuts(rows)
    cut = jax.ShapeDtypeStruct((rows // owners // halves, columns), low)
    line = jax.ShapeDtypeStruct((1, columns), jnp.float32)

    def kernel(starts_ref, joined, qkv, hidden, up, x, *refs):
        mine = pl.ds(first, columns)
        normed_grads_kernel(
            starts_ref,
            joined,
            qkv.at[:, mine, :],
            hidden,
            up.at[mine, :],
            x.at[:, mine],
            *refs,
            halves=halves,
        )

    result = whole_call(
        kernel,
        [SMEM] + [ANY] * 5 + [VMEM] * 2,
        [VMEM, VMEM] + [ANY] * (owners * halves),
        [line, line] + [cut] * (owners * halves),
        [
            pltpu.VMEM((3, rows, width), low),
            pltpu.VMEM((3, columns, width), low),
            pltpu.VMEM((rows, units), low),
            pltpu.VMEM((columns, units), low),
            pltpu.VMEM((rows, columns), low),
            pltpu.VMEM((rows, columns), low),
            pltpu.SemaphoreType.DMA((4 + 3 * owners,)),
            pltpu.SemaphoreType.DMA((owners * halves,)),
        ],
    )(starts, joined, qkv, hidden, up, x, mean, root)
    return result[0], result[1], tuple(result[2:])


def finish_kernel(*refs):
    mixed, dense = refs[:4], refs[4:9]
    token_ref, bias_ref = refs[9:11]
    last_first, last_second, first_near, second_near, low, high = refs[11:17]
    out_ref = refs[17]
    half = low.shape[0]
    far = dense[3].shape[0]
    total = jnp.dot(mixed[0][...], dense[0][...], preferred_element_type=jnp.float32)
    total += jnp.dot(mixed[1][...], dense[1][...], preferred_element_type=jnp.float32)
    total += jnp.dot(mixed[2][...], dense[2][...], preferred_element_type=jnp.float32)
    total += jnp.dot(mixed[3][:, :far], dense[3][...], preferred_element_type=jnp.float32)
    total += jnp.dot(mixed[3][:, far:], dense[4][...], preferred_element_type=jnp.float32)
    total += wide(token_ref[...]) + bias_ref[...]
    for here, parts in (
        (slice(0, half), (low, first_near, last_first)),
        (slice(half, 2 * half), (high, second_near, last_second)),
    ):
        feed = wide(parts[0][...]) + wide(parts[1][...]) + wide(parts[2][...])
        out_ref[here, :] = (total[here] + feed).astype(out_ref.dtype)


def finish_output(mixed_parts, dense_parts, tokens, bias, feed_parts):
    rows, depth = tokens.shape
    if len(feed_parts) == 1:
        attended = jnp.dot(mixed_parts[0], dense_parts[0], preferred_element_type=jnp.float32)
        return (wide(tokens) + attended + feed_parts[0] + bias).astype(tokens.dtype)
    columns = min(512, depth)

    def column_block(piece):
        return pl.BlockSpec((piece.shape[0], columns), lambda j: (0, j))

    return pl.pallas_call(
        finish_kernel,
        grid=(depth // columns,),
        in_specs=[pl.BlockSpec(piece.shape, lambda j: (0, 0)) for piece in mixed_parts]
        + [column_block(piece) for piece in dense_parts]
        + [column_block(tokens), pl.BlockSpec((1, columns), lambda j: (0, j))]
        + [column_block(piece) for piece in feed_parts],
        out_specs=column_block(tokens),
        out_shape=jax.ShapeDtypeStruct(tokens.shape, tokens.dtype),
        compiler_params=pltpu.CompilerParams(vmem_limit_bytes=VMEM_BYTES),
        cost_estimate=SHORT,
    )(*mixed_parts, *dense_parts, tokens, bias.reshape(1, depth), *feed_parts)


def token_grads_kernel(*refs):
    left, right = refs[:6], refs[6:12]
    token_ref, grad_ref, mean_ref, root_ref, gain_ref, out_ref = refs[12:]
    half = left[4].shape[0]
    split = left[4].shape[1]
    chunk = min(32, half)
    for upper in range(2):
        chosen = [(side[4 + upper], side[2 + upper], side[upper]) for side in (left, right)]

        @pl.loop(0, half // chunk)
        def _(step, chosen=chosen, upper=upper):
            there = pl.ds(pl.multiple_of(step * chunk, chunk), chunk)
            here = pl.ds(pl.multiple_of(upper * half + step * chunk, chunk), chunk)
            scaled = []
            hats = []
            for side, parts in enumerate(chosen):
                columns = slice(side * split, (side + 1) * split)
                total = sum(wide(part[there, :]) for part in parts)
                scaled.append(total * gain_ref[:, columns])
                hats.append(
                    (wide(token_ref[here, columns]) - mean_ref[here, :]) * root_ref[here, :]
                )
            count = 2 * split
            mean = sum(jnp.sum(v, axis=-1, keepdims=True) for v in scaled) / count
            slant = (
                sum(jnp.sum(v * h, axis=-1, keepdims=True) for v, h in zip(scaled, hats)) / count
            )
            for side in range(2):
                columns = slice(side * split, (side + 1) * split)
                grad = root_ref[here, :] * (scaled[side] - mean - hats[side] * slant)
                out_ref[here, columns] = (wide(grad_ref[here, columns]) + grad).astype(
                    out_ref.dtype
                )


def token_grads(left_parts, right_parts, tokens, cotangent, mean, root, gain):
    if len(left_parts) == 1:
        grad = jnp.concatenate([left_parts[0], right_parts[0]], axis=1)
        hat = (wide(tokens) - mean) * root
        scaled = grad * gain
        grad_input = root * (
            scaled
            - jnp.mean(scaled, axis=-1, keepdims=True)
            - hat * jnp.mean(scaled * hat, axis=-1, keepdims=True)
        )
        return (wide(cotangent) + grad_input).astype(tokens.dtype)
    return pl.pallas_call(
        token_grads_kernel,
        out_shape=jax.ShapeDtypeStruct(tokens.shape, tokens.dtype),
        compiler_params=pltpu.CompilerParams(vmem_limit_bytes=VMEM_BYTES),
        cost_estimate=SHORT,
    )(*left_parts, *right_parts, tokens, cotangent, mean, root, gain.reshape(1, -1))


def attention_kernel(
    q_ref,
    k_ref,
    v_ref,
    g_ref,
    cos_ref,
    above_ref,
    below_ref,
    mixed_ref,
    grads_ref,
    sums_ref,
    keys_across,
    values_across,
    query_total,
    key_total,
    value_total,
    weight_buf,
    top_buf,
    out_buf,
    across_buf,
    *,
    block,
    block_count,
):
    step = pl.program_id(1)
    scale = HEAD_DIM**-0.5
    rate = scale * 1.4426950408889634

    @pl.when(step == 0)
    def _():
        keys_across[...] = k_ref[...].T
        values_across[...] = v_ref[...].T
        key_total[...] = jnp.zeros_like(key_total)
        value_total[...] = jnp.zeros_like(value_total)

    rows = pl.ds(pl.multiple_of(step * block, block), block)
    queries, grads = q_ref[rows, :], g_ref[rows, :]
    lane = lax.broadcasted_iota(jnp.int32, (block, PAIR), 1)
    own_lanes = [lane // HEAD_DIM == head for head in range(2)]
    query_heads = [jnp.where(own, queries, jnp.zeros_like(queries)) for own in own_lanes]
    grad_heads = [jnp.where(own, grads, jnp.zeros_like(grads)) for own in own_lanes]
    parts = [slice(head * HEAD_DIM, (head + 1) * HEAD_DIM) for head in range(2)]

    def weigh(there, index, first):
        keys = k_ref[there, :]
        score_heads = [
            lax.dot_general(keys, own, ROWS_BY_ROWS, preferred_element_type=jnp.float32)
            for own in query_heads
        ]
        for head in range(2):
            scores = score_heads[head]
            if first:
                key_pos = lax.broadcasted_iota(jnp.int32, (block, block), 0)
                query_pos = lax.broadcasted_iota(jnp.int32, (block, block), 1)
                scores = jnp.where(key_pos <= query_pos, scores, masked_score)
            top = jnp.max(scores, axis=0, keepdims=True) * rate
            if not first:
                before = top_buf[head, 0]
                top = jnp.maximum(top, before)
            weights = jnp.exp2(scores * rate - top)
            weight_buf[head, there, :] = weights
            top_buf[head, 2 + index] = top
            total = jnp.sum(weights, axis=0, keepdims=True)
            out = jnp.dot(
                values_across[parts[head], there],
                weights.astype(jnp.bfloat16),
                preferred_element_type=jnp.float32,
            )
            if not first:
                shrink = jnp.exp2(before - top)
                total += top_buf[head, 1] * shrink
                out += out_buf[parts[head], :] * shrink
            top_buf[head, 0] = top
            top_buf[head, 1] = total
            out_buf[parts[head], :] = out

    weigh(rows, step, True)

    @pl.loop(0, step)
    def _(index):
        weigh(pl.ds(pl.multiple_of(index * block, block), block), index, False)

    grads_across = grads.T.astype(jnp.float32)
    inner, share = [], []
    for head in range(2):
        share.append(1.0 / top_buf[head, 1])
        out = out_buf[parts[head], :] * share[head]
        out_buf[parts[head], :] = out
        inner.append(jnp.sum(out * grads_across[parts[head]], axis=0, keepdims=True))
    mixed_ref[rows, :] = out_buf[...].T.astype(mixed_ref.dtype)

    def differentiate(there, index, first):
        values = v_ref[there, :]
        prob_heads = [
            lax.dot_general(values, own, ROWS_BY_ROWS, preferred_element_type=jnp.float32)
            for own in grad_heads
        ]
        value_parts, key_parts = [], []
        for head in range(2):
            factor = jnp.exp2(top_buf[head, 2 + index] - top_buf[head, 0]) * share[head]
            exact = weight_buf[head, there, :] * factor
            rounded = exact.astype(jnp.bfloat16)
            grad_scores = (exact * (prob_heads[head] - inner[head])).astype(jnp.bfloat16)
            value_parts.append(
                jnp.dot(rounded, grad_heads[head], preferred_element_type=jnp.float32)
            )
            key_parts.append(
                jnp.dot(grad_scores, query_heads[head], preferred_element_type=jnp.float32)
            )
            across = jnp.dot(
                keys_across[parts[head], there], grad_scores, preferred_element_type=jnp.float32
            )
            if first:
                across_buf[parts[head], :] = across
            else:
                across_buf[parts[head], :] += across
        value_total[there, :] += value_parts[0] + value_parts[1]
        key_total[there, :] += key_parts[0] + key_parts[1]

    differentiate(rows, step, True)

    @pl.loop(0, step)
    def _(index):
        differentiate(pl.ds(pl.multiple_of(index * block, block), block), index, False)

    query_total[rows, :] = across_buf[...].T

    @pl.when(step == block_count - 1)
    def _():
        lanes = cos_ref[...], above_ref[...], below_ref[...]
        for slot, field in enumerate(
            (
                turn_back(query_total[...] * scale, *lanes),
                turn_back(key_total[...] * scale, *lanes),
                value_total[...],
            )
        ):
            low = field.astype(grads_ref.dtype)
            grads_ref[slot] = low
            sums_ref[slot] = jnp.sum(low.astype(jnp.float32), axis=0, keepdims=True)


def attention(joined, grad_mixed, lanes, first, last, earlier=None):
    rows, width = grad_mixed.shape
    block = min(512, LENGTH)
    pairs, block_count = width // PAIR, LENGTH // block
    row_block = pl.BlockSpec((LENGTH, PAIR), lambda p, i: (0, first + p))
    table = pl.BlockSpec((LENGTH, PAIR), lambda p, i: (0, 0))
    kept = () if earlier is None else tuple(earlier)
    kernel = functools.partial(attention_kernel, block=block, block_count=block_count)

    def body(*refs):
        kernel(*refs[:7], *refs[7 + len(kept) :])

    return pl.pallas_call(
        body,
        grid=(last - first, block_count),
        in_specs=[
            row_block,
            pl.BlockSpec((LENGTH, PAIR), lambda p, i: (0, pairs + first + p)),
            pl.BlockSpec((LENGTH, PAIR), lambda p, i: (0, 2 * pairs + first + p)),
            row_block,
            table,
            table,
            table,
        ]
        + [pl.BlockSpec(memory_space=pl.ANY)] * len(kept),
        out_specs=[
            row_block,
            pl.BlockSpec((3, LENGTH, PAIR), lambda p, i: (0, 0, first + p)),
            pl.BlockSpec((3, 1, PAIR), lambda p, i: (0, 0, first + p)),
        ],
        out_shape=[
            jax.ShapeDtypeStruct((rows, width), jnp.bfloat16),
            jax.ShapeDtypeStruct((3, rows, width), jnp.bfloat16),
            jax.ShapeDtypeStruct((3, 1, width), jnp.float32),
        ],
        scratch_shapes=[
            pltpu.VMEM((PAIR, LENGTH), jnp.bfloat16),
            pltpu.VMEM((PAIR, LENGTH), jnp.bfloat16),
            pltpu.VMEM((LENGTH, PAIR), jnp.float32),
            pltpu.VMEM((LENGTH, PAIR), jnp.float32),
            pltpu.VMEM((LENGTH, PAIR), jnp.float32),
            pltpu.VMEM((2, LENGTH, block), jnp.float32),
            pltpu.VMEM((2, 2 + block_count, 1, block), jnp.float32),
            pltpu.VMEM((PAIR, block), jnp.float32),
            pltpu.VMEM((PAIR, block), jnp.float32),
        ],
        input_output_aliases={7 + i: i for i in range(len(kept))},
        compiler_params=pltpu.CompilerParams(vmem_limit_bytes=VMEM_BYTES),
        cost_estimate=SHORT,
    )(joined, joined, joined, grad_mixed, *lanes, *kept)


def norm_kernel(starts_ref, gain_ref, shift_ref, following_ref, *refs):
    count = (len(refs) - 6) // 3
    pieces = refs[:count]
    raw, normed, mean_ref, root_ref, following_out = refs[count : count + 5]
    buffers = refs[count + 5 : 2 * count + 5]
    results = refs[2 * count + 5 : 3 * count + 5]
    sems = refs[-1]
    following_out[...] = following_ref[...]
    for slot in range(count):
        pltpu.make_async_copy(pieces[slot], buffers[slot], sems.at[0, slot]).start()
    writes = []
    for slot in range(count):
        buffer, result = buffers[slot], results[slot]
        size = buffer.shape[0]
        where = pl.ds(pl.multiple_of(starts_ref[slot], size), size)
        pltpu.make_async_copy(pieces[slot], buffer, sems.at[0, slot]).wait()
        write = pltpu.make_async_copy(buffer, raw.at[where, :], sems.at[1, slot])
        write.start()
        writes.append(write)
        chunk = min(128, size)

        @pl.loop(0, size // chunk)
        def _(step, buffer=buffer, result=result, slot=slot):
            here = pl.ds(pl.multiple_of(step * chunk, chunk), chunk)
            rows = buffer[here, :].astype(jnp.float32)
            mean = jnp.mean(rows, axis=-1, keepdims=True)
            centred = rows - mean
            variance = jnp.mean(centred * centred, axis=-1, keepdims=True)
            root = lax.rsqrt(variance + epsilon)
            out = centred * root * gain_ref[...] + shift_ref[...]
            result[here, :] = out.astype(result.dtype)
            there = pl.ds(pl.multiple_of(starts_ref[slot] + step * chunk, chunk), chunk)
            mean_ref[there, :] = mean
            root_ref[there, :] = root

        write = pltpu.make_async_copy(result, normed.at[where, :], sems.at[2, slot])
        write.start()
        writes.append(write)
    for write in writes:
        write.wait()


def norm_rows(pieces, gain, shift, following):
    depth = gain.shape[0]
    total = sum(piece.shape[0] for _, piece in pieces)
    count = len(pieces)
    low = jnp.bfloat16
    starts = jnp.stack([jnp.asarray(start, jnp.int32) for start, _ in pieces])
    any_space = pl.BlockSpec(memory_space=pl.ANY)
    vmem = pl.BlockSpec(memory_space=pltpu.VMEM)
    stage = [pltpu.VMEM(piece.shape, low) for _, piece in pieces]
    return pl.pallas_call(
        norm_kernel,
        in_specs=[pl.BlockSpec(memory_space=pltpu.SMEM), vmem, vmem, vmem] + [any_space] * count,
        out_specs=[any_space, any_space, vmem, vmem, vmem],
        out_shape=[
            jax.ShapeDtypeStruct((total, depth), low),
            jax.ShapeDtypeStruct((total, depth), low),
            jax.ShapeDtypeStruct((total, 1), jnp.float32),
            jax.ShapeDtypeStruct((total, 1), jnp.float32),
            jax.ShapeDtypeStruct(following.shape, following.dtype),
        ],
        scratch_shapes=stage + stage + [pltpu.SemaphoreType.DMA((3, count))],
        compiler_params=pltpu.CompilerParams(vmem_limit_bytes=VMEM_BYTES),
        cost_estimate=SHORT,
    )(
        starts,
        gain.reshape(1, depth),
        shift.reshape(1, depth),
        following,
        *[piece for _, piece in pieces],
    )


def on_device(
    tokens,
    norm_gain,
    norm_shift,
    weight_qkv,
    bias_qkv,
    weight_dense,
    weight_up,
    bias_up,
    weight_down,
    bias_out,
    cotangent,
):
    f32, low = jnp.float32, jnp.bfloat16
    depth = tokens.shape[1]
    local_rows = tokens.shape[0]
    tensor_index = lax.axis_index("tensor")

    full_up = lax.all_gather(weight_up, "dp", axis=0, tiled=True)
    token_parts = gather_start(tokens)
    lanes = lane_tables(LENGTH)
    out_part = jnp.sum(cotangent, axis=0, dtype=f32)
    lanes, out_part, token_parts = after((lanes, out_part, token_parts))
    full_qkv = lax.all_gather(
        after(jnp.transpose(weight_qkv, (1, 0, 2)), token_parts), "dp", axis=1, tiled=True
    )
    token_parts = gather_pass(token_parts)
    all_tokens, gathered, mean, root, sent = norm_rows(
        gathered_pieces(token_parts), norm_gain, norm_shift, cotangent
    )
    grad_parts = gather_start(sent)

    full_dense = lax.all_gather(after(weight_dense, gathered), "dp", axis=1, tiled=True)
    active, slope = hidden_rows(gathered, full_up, bias_up)
    grad_parts, active = after((grad_parts, active))
    full_down = lax.all_gather(after(weight_down, grad_parts), "dp", axis=1, tiled=True)
    grad_parts = gather_pass(grad_parts)
    joined = joined_rows(after(gathered, active, grad_parts[:3]), full_qkv, bias_qkv, lanes)
    grad_parts, joined = after((grad_parts, joined))
    grad_rows, grad_mixed, grad_down = first_grads(
        gathered_pieces(grad_parts), active, full_dense
    )
    dense_parts = gather_start(after(full_dense, grad_mixed))
    grad_down_sum = lax.psum_scatter(grad_down, "dp", scatter_dimension=1, tiled=True)

    pairs = grad_mixed.shape[1] // PAIR
    part = attention(joined, grad_mixed, lanes, 0, pairs // 2)
    dense_parts, part = after((dense_parts, part))
    dense_parts = gather_pass(dense_parts)
    feed_cuts = feed_rows(after(active, part[0]), full_down)
    feed_cuts, dense_parts = after((feed_cuts, dense_parts))
    feed_parts = scatter_send(feed_cuts)
    grad_hidden, grad_up, bias_up_part = hidden_grads(
        after(grad_rows, feed_cuts), full_down, slope, gathered
    )
    grad_up, feed_parts = after((grad_up, feed_parts))
    grad_up_sum = lax.psum_scatter(
        after(grad_up, grad_down_sum), "dp", scatter_dimension=0, tiled=True
    )
    feed_parts = scatter_pass(scatter_fold(feed_parts))
    part = attention(after(joined, grad_up), grad_mixed, lanes, pairs // 2, pairs, part)
    mixed, grad_joined, bias_qkv_part = part
    mixed, grad_joined, feed_parts = after((mixed, grad_joined, feed_parts))

    mixed_parts = exchange_start(mixed)
    grad_qkv = qkv_grads(gathered, grad_joined)
    grad_qkv, mixed_parts = after((grad_qkv, mixed_parts))
    grad_dense = jnp.einsum(
        "tk,td->kd", after(mixed, grad_qkv), grad_rows, preferred_element_type=f32
    ).astype(low)
    own_mean = lax.dynamic_slice_in_dim(mean, tensor_index * local_rows, local_rows, 0)
    own_root = lax.dynamic_slice_in_dim(root, tensor_index * local_rows, local_rows, 0)
    own_mean, own_root, grad_dense = after((own_mean, own_root, grad_dense))
    grad_qkv_sum = lax.psum_scatter(
        after(grad_qkv, grad_up_sum, grad_dense), "dp", scatter_dimension=1, tiled=True
    )
    half = depth // 2
    sources = full_qkv, grad_hidden, full_up, all_tokens, mean, root
    *left_sums, left_cuts = normed_grads(after(grad_joined, grad_dense), *sources, 0, half)
    left_parts = scatter_send(left_cuts)
    *right_sums, right_cuts = normed_grads(after(grad_joined, left_cuts), *sources, half, depth)
    right_cuts, right_sums, left_parts = after((right_cuts, right_sums, left_parts))
    sums = jnp.concatenate(
        [left_sums[0][0], right_sums[0][0], left_sums[1][0], right_sums[1][0], out_part]
    ).reshape(-1, PAIR)
    right_parts = scatter_send(right_cuts)
    left_parts, sums = after((scatter_fold(left_parts), sums))
    over_group = exchange_sum(sums, "tensor")
    left_parts = scatter_pass(left_parts)
    block_out = finish_output(
        after(mixed_parts, right_cuts), dense_parts, tokens, bias_out, feed_parts
    )
    block_out, right_parts, left_parts, over_group = after(
        (block_out, right_parts, left_parts, over_group)
    )
    grad_dense_sum = lax.psum_scatter(
        after(grad_dense, grad_qkv_sum, block_out), "dp", scatter_dimension=1, tiled=True
    )
    right_parts = scatter_pass(scatter_fold(right_parts))
    bias_size = bias_qkv.size
    over_dp = jnp.concatenate(
        [over_group.reshape(-1), bias_qkv_part.reshape(-1), bias_up_part.reshape(-1)]
    ).reshape(-1, PAIR)
    over_dp = over_dp + swap(over_dp, "dp", 1)
    over_dp = exchange_sum(over_dp, "dp", 2).reshape(-1)
    grad_gain, grad_shift, grad_bias_out = over_dp[: 3 * depth].reshape(3, depth)
    grad_bias_qkv = over_dp[3 * depth : 3 * depth + bias_size].reshape(bias_qkv.shape)
    grad_bias_up = over_dp[3 * depth + bias_size :]
    grad_tokens = token_grads(
        left_parts, right_parts, tokens, cotangent, own_mean, own_root, norm_gain
    )
    return (
        block_out,
        grad_tokens,
        grad_gain,
        grad_shift,
        jnp.transpose(grad_qkv_sum, (1, 0, 2)).astype(f32),
        grad_bias_qkv,
        grad_dense_sum.astype(f32),
        grad_up_sum.astype(f32),
        grad_bias_up,
        grad_down_sum.astype(f32),
        grad_bias_out,
    )


def solution(mesh):
    in_specs = (
        P(("dp", "tensor"), None),
        P(),
        P(),
        P("dp", None, "tensor"),
        P(None, "tensor"),
        P("tensor", "dp"),
        P("dp", "tensor"),
        P("tensor"),
        P("tensor", "dp"),
        P(),
        P(("dp", "tensor"), None),
    )
    out_specs = (
        P(("dp", "tensor"), None),
        P(("dp", "tensor"), None),
        P(),
        P(),
        P("dp", None, "tensor"),
        P(None, "tensor"),
        P("tensor", "dp"),
        P("dp", "tensor"),
        P("tensor"),
        P("tensor", "dp"),
        P(),
    )
    return jax.shard_map(
        on_device, mesh=mesh, in_specs=in_specs, out_specs=out_specs, check_vma=False
    )
```

```python
import functools

import jax
import jax.numpy as jnp
from jax import lax
from jax.experimental import pallas as pl
from jax.experimental.pallas import tpu as pltpu
from jax.sharding import PartitionSpec as P

HEAD_DIM = 64
ROT = 32
LENGTH = 2048
PAIR = 2 * HEAD_DIM

epsilon = 1e-05
masked_score = -1e30
MIB = 1024 * 1024
VMEM_BYTES = 64 * MIB - 256 * 1024
ROWS_BY_ROWS = (((1,), (1,)), ((), ()))
COLUMNS_BY_COLUMNS = (((0,), (0,)), ((), ()))


SHORT = pl.CostEstimate(flops=1, bytes_accessed=1, transcendentals=0)


def after(value, *earlier):
    return lax.optimization_barrier((value,) + earlier)[0]


def swap(value, axis, bit):
    count = lax.axis_size(axis)
    return lax.ppermute(value, axis, [(i, i ^ bit) for i in range(count)])


def gather_start(block):
    if lax.axis_size("tensor") != 4:
        return (lax.all_gather(block, "tensor", axis=0, tiled=True),)
    return block, swap(block, "tensor", 1), swap(block, "tensor", 2)


def halves_kernel(one_ref, two_ref, low_ref, high_ref):
    half = one_ref.shape[0] // 2
    low_ref[...] = one_ref[:half, :]
    high_ref[...] = two_ref[half:, :]


def gather_pass(parts):
    if len(parts) == 1:
        return parts
    block, one, two = parts
    rows, depth = block.shape
    half = jax.ShapeDtypeStruct((rows // 2, depth), block.dtype)
    low, high = pl.pallas_call(
        halves_kernel,
        out_shape=[half, half],
        compiler_params=pltpu.CompilerParams(vmem_limit_bytes=VMEM_BYTES),
        cost_estimate=SHORT,
    )(one, two)
    return block, one, two, swap(low, "tensor", 2), swap(high, "tensor", 1)


def gathered_pieces(parts):
    if len(parts) == 1:
        return [(0, parts[0])]
    block, one, two, low, high = parts
    rows = block.shape[0]
    me = lax.axis_index("tensor")
    return [
        (me * rows, block),
        ((me ^ 1) * rows, one),
        ((me ^ 2) * rows, two),
        ((me ^ 3) * rows, low),
        ((me ^ 3) * rows + rows // 2, high),
    ]


def wide(piece):
    return piece.astype(jnp.float32)


def owner_cuts(total):
    count = lax.axis_size("tensor")
    rows = total // count
    me = lax.axis_index("tensor")
    order = [me ^ bit for bit in (3, 1, 2, 0)] if count == 4 else list(range(count))
    starts = jnp.stack([jnp.asarray(owner * rows, jnp.int32) for owner in order])
    return starts, count, 2 if count == 4 else 1


def scatter_send(cuts):
    if lax.axis_size("tensor") != 4:
        whole = wide(jnp.concatenate(cuts))
        return (lax.psum_scatter(whole, "tensor", scatter_dimension=0, tiled=True),)
    far_low, far_high, one_low, one_high, two_low, two_high, low, high = cuts
    return (
        swap(far_low, "tensor", 1),
        swap(far_high, "tensor", 2),
        swap(one_low, "tensor", 1),
        swap(two_high, "tensor", 2),
        two_low,
        one_high,
        low,
        high,
    )


def fold_kernel(a_ref, b_ref, c_ref, d_ref, ab_ref, cd_ref):
    ab_ref[...] = (wide(a_ref[...]) + wide(b_ref[...])).astype(ab_ref.dtype)
    cd_ref[...] = (wide(c_ref[...]) + wide(d_ref[...])).astype(cd_ref.dtype)


def scatter_fold(parts):
    if len(parts) == 1:
        return parts
    first_far, second_far, first_near, second_near, two_low, one_high, low, high = parts
    shape = jax.ShapeDtypeStruct(low.shape, low.dtype)
    forward = pl.pallas_call(
        fold_kernel,
        out_shape=[shape, shape],
        compiler_params=pltpu.CompilerParams(vmem_limit_bytes=VMEM_BYTES),
    )(two_low, first_far, one_high, second_far)
    return (*forward, first_near, second_near, low, high)


def scatter_pass(parts):
    if len(parts) == 1:
        return parts
    two_low, one_high, first_near, second_near, low, high = parts
    return (
        swap(two_low, "tensor", 2),
        swap(one_high, "tensor", 1),
        first_near,
        second_near,
        low,
        high,
    )


def exchange_start(columns):
    if lax.axis_size("tensor") != 4:
        return (lax.all_to_all(columns, "tensor", 0, 1, tiled=True),)
    rows = columns.shape[0] // 4
    me = lax.axis_index("tensor")
    pieces = []
    for bit in range(4):
        piece = lax.dynamic_slice_in_dim(columns, (me ^ bit) * rows, rows, 0)
        pieces.append(swap(piece, "tensor", bit) if bit else piece)
    return tuple(pieces)


def exchange_sum(value, axis, step=1):
    parts = [value]
    for bit in range(step, lax.axis_size(axis), step):
        parts.append(swap(value, axis, bit))
    return functools.reduce(lambda a, b: a + b, parts)


def lane_tables(row_total):
    half_rot = ROT // 2
    positions = (jnp.arange(row_total, dtype=jnp.int32) % LENGTH).astype(jnp.float32)
    inverse = 10000.0 ** (-(2.0 * jnp.arange(half_rot, dtype=jnp.float32)) / ROT)
    angles = positions[:, None] * inverse[None, :]
    cosine, sine = jnp.cos(angles), jnp.sin(angles)
    ones = jnp.ones((row_total, HEAD_DIM - ROT), jnp.float32)
    zeros = jnp.zeros((row_total, half_rot), jnp.float32)
    rest = jnp.zeros((row_total, HEAD_DIM - ROT), jnp.float32)
    cos_lanes = jnp.concatenate([cosine, cosine, ones] * 2, axis=1)
    from_above = jnp.concatenate([-sine, zeros, rest] * 2, axis=1)
    from_below = jnp.concatenate([zeros, sine, rest] * 2, axis=1)
    return cos_lanes, from_above, from_below


def turn(field, cos_lanes, from_above, from_below):
    half_rot = ROT // 2
    above = pltpu.roll(field, PAIR - half_rot, 1)
    below = pltpu.roll(field, half_rot, 1)
    return field * cos_lanes + above * from_above + below * from_below


def turn_back(field, cos_lanes, from_above, from_below):
    half_rot = ROT // 2
    above = pltpu.roll(field, PAIR - half_rot, 1)
    below = pltpu.roll(field, half_rot, 1)
    return field * cos_lanes - above * from_above - below * from_below


def joined_kernel(x_ref, w_ref, bias_ref, cos_ref, above_ref, below_ref, out_ref):
    width = out_ref.shape[1]
    chunk = min(256, width)
    slot = pl.program_id(0)

    def product(start):
        columns = slice(start, start + chunk)
        part = jnp.dot(x_ref[...], w_ref[0, :, columns], preferred_element_type=jnp.float32)
        return part + bias_ref[0, :, columns]

    @pl.when(slot < 2)
    def _():
        for start in range(0, width, chunk):
            part = product(start)
            for shift in range(0, chunk, PAIR):
                lanes = part[:, shift : shift + PAIR]
                turned = turn(lanes, cos_ref[...], above_ref[...], below_ref[...])
                columns = slice(start + shift, start + shift + PAIR)
                out_ref[:, columns] = turned.astype(out_ref.dtype)

    @pl.when(slot == 2)
    def _():
        for start in range(0, width, chunk):
            out_ref[:, start : start + chunk] = product(start).astype(out_ref.dtype)


def joined_rows(x, w, bias, lanes):
    rows, depth = x.shape
    width = w.shape[2]
    block = min(1024, rows)
    return pl.pallas_call(
        joined_kernel,
        grid=(3, rows // block),
        in_specs=[
            pl.BlockSpec((block, depth), lambda j, i: (i, 0)),
            pl.BlockSpec((1, depth, width), lambda j, i: (j, 0, 0)),
            pl.BlockSpec((1, 1, width), lambda j, i: (j, 0, 0)),
        ]
        + [pl.BlockSpec((block, PAIR), lambda j, i: (i, 0))] * 3,
        out_specs=pl.BlockSpec((block, width), lambda j, i: (i, j)),
        out_shape=jax.ShapeDtypeStruct((rows, 3 * width), jnp.bfloat16),
        compiler_params=pltpu.CompilerParams(vmem_limit_bytes=VMEM_BYTES),
        cost_estimate=SHORT,
    )(x, w, bias.reshape(3, 1, width), *lanes)


def hidden_kernel(x_ref, w_ref, bias_ref, active_ref, slope_ref):
    hidden = jnp.dot(x_ref[...], w_ref[...], preferred_element_type=jnp.float32) + bias_ref[...]
    scale = (2.0 / jnp.pi) ** 0.5
    square = hidden * hidden
    inner = scale * hidden * (1.0 + 0.044715 * square)
    bent = jnp.tanh(inner)
    half = 0.5 * (1.0 + bent)
    active_ref[...] = (hidden * half).astype(active_ref.dtype)
    growth = scale * (1.0 + (3.0 * 0.044715) * square)
    slope = half + 0.5 * hidden * (1.0 - bent * bent) * growth
    slope_ref[...] = slope.astype(slope_ref.dtype)


def hidden_rows(x, w, bias):
    rows, depth = x.shape
    width = w.shape[1]
    block, columns = min(1024, rows), min(1024, width)
    return pl.pallas_call(
        hidden_kernel,
        grid=(width // columns, rows // block),
        in_specs=[
            pl.BlockSpec((block, depth), lambda j, i: (i, 0)),
            pl.BlockSpec((depth, columns), lambda j, i: (0, j)),
            pl.BlockSpec((1, columns), lambda j, i: (0, j)),
        ],
        out_specs=[pl.BlockSpec((block, columns), lambda j, i: (i, j))] * 2,
        out_shape=[jax.ShapeDtypeStruct((rows, width), jnp.bfloat16)] * 2,
        compiler_params=pltpu.CompilerParams(vmem_limit_bytes=VMEM_BYTES),
        cost_estimate=SHORT,
    )(x, w, bias.reshape(1, width))


def whole_call(kernel, in_specs, out_specs, out_shape, scratch):
    return pl.pallas_call(
        kernel,
        in_specs=in_specs,
        out_specs=out_specs,
        out_shape=out_shape,
        scratch_shapes=scratch,
        compiler_params=pltpu.CompilerParams(vmem_limit_bytes=VMEM_BYTES),
        cost_estimate=SHORT,
    )


def columns_of(ref, index, size):
    return ref.at[:, pl.ds(pl.multiple_of(index * size, size), size)]


def rows_of(ref, index, size):
    return ref.at[pl.ds(pl.multiple_of(index * size, size), size), :]


def nt_dot(a, b):
    return lax.dot_general(a, b, ROWS_BY_ROWS, preferred_element_type=jnp.float32)


def tn_dot(a, b):
    return lax.dot_general(a, b, COLUMNS_BY_COLUMNS, preferred_element_type=jnp.float32)


ANY = pl.BlockSpec(memory_space=pl.ANY)
SMEM = pl.BlockSpec(memory_space=pltpu.SMEM)
VMEM = pl.BlockSpec(memory_space=pltpu.VMEM)


def tile_loop(count, tiles, tile_sems, where, compute):
    def write(step, slot):
        return pltpu.make_async_copy(tiles.at[slot], where(step), tile_sems.at[slot])

    @pl.loop(0, count)
    def _(step):
        slot = lax.rem(step, 2)

        @pl.when(step >= 2)
        def _():
            write(step, slot).wait()

        tiles[slot] = compute(step).astype(tiles.dtype)
        write(step, slot).start()

    for step in range(max(count - 2, 0), count):
        write(step, step % 2).wait()


def first_grads_kernel(starts_ref, active, *refs):
    count = len(refs) - 9
    pieces = refs[:count]
    rows_out, down_out, grad_buf, active_buf, tiles = refs[count:-4]
    piece_sems, load_sems, row_sems, tile_sems = refs[-4:]
    _, rows, half = grad_buf.shape
    blocks, _, block = active_buf.shape

    def piece_copy(slot, side):
        size = pieces[slot].shape[0]
        there = pl.ds(pl.multiple_of(starts_ref[slot], size), size)
        return pltpu.make_async_copy(
            pieces[slot].at[:, pl.ds(side * half, half)],
            grad_buf.at[side, there, :],
            piece_sems.at[slot, side],
        )

    def active_copy(index):
        return pltpu.make_async_copy(
            columns_of(active, index, block), active_buf.at[index], load_sems.at[index]
        )

    def row_copy(side):
        return pltpu.make_async_copy(
            grad_buf.at[side], rows_out.at[:, pl.ds(side * half, half)], row_sems.at[side]
        )

    active_copy(0).start()
    for side in range(2):
        for slot in range(count):
            piece_copy(slot, side).start()
    for index in range(1, blocks):
        active_copy(index).start()

    def compute(step):
        for index in range(blocks):
            pl.when(step == 2 * index)(active_copy(index).wait)
        for side in range(2):

            @pl.when(step == side)
            def _(side=side):
                for slot in range(count):
                    piece_copy(slot, side).wait()
                row_copy(side).start()

        return tn_dot(active_buf[lax.div(step, 2)], grad_buf[lax.rem(step, 2)])

    tile_loop(
        2 * blocks,
        tiles,
        tile_sems,
        lambda step: down_out.at[
            pl.ds(pl.multiple_of(lax.div(step, 2) * block, block), block),
            pl.ds(pl.multiple_of(lax.rem(step, 2) * half, half), half),
        ],
        compute,
    )
    for side in range(2):
        row_copy(side).wait()


def first_grads(pieces, active):
    low = jnp.bfloat16
    rows, hidden = active.shape
    depth = pieces[0][1].shape[1]
    half, block = depth // 2, min(512, hidden)
    count = len(pieces)
    starts = jnp.stack([jnp.asarray(start, jnp.int32) for start, _ in pieces])
    return whole_call(
        first_grads_kernel,
        [SMEM] + [ANY] * (1 + count),
        [ANY, ANY],
        [
            jax.ShapeDtypeStruct((rows, depth), low),
            jax.ShapeDtypeStruct((hidden, depth), low),
        ],
        [
            pltpu.VMEM((2, rows, half), low),
            pltpu.VMEM((hidden // block, rows, block), low),
            pltpu.VMEM((2, block, half), low),
            pltpu.SemaphoreType.DMA((count, 2)),
            pltpu.SemaphoreType.DMA((hidden // block,)),
            pltpu.SemaphoreType.DMA((2,)),
            pltpu.SemaphoreType.DMA((2,)),
        ],
    )(starts, active, *[piece for _, piece in pieces])


def feed_kernel(starts_ref, active, weight, *refs, halves):
    cuts = refs[:-5]
    active_buf, weight_buf, out_buf, load_sems, cut_sems = refs[-5:]
    owners = len(cuts) // halves
    rows = active_buf.shape[0]
    half = weight_buf.shape[2]
    owner_rows = rows // owners
    piece = owner_rows // halves

    def weight_load(side):
        return pltpu.make_async_copy(
            weight.at[:, pl.ds(side * half, half)], weight_buf.at[side], load_sems.at[side]
        )

    def row_load(owner):
        here = pl.ds(pl.multiple_of(starts_ref[owner], owner_rows), owner_rows)
        return pltpu.make_async_copy(
            active.at[here, :], active_buf.at[here, :], load_sems.at[2 + owner]
        )

    weight_load(0).start()
    row_load(0).start()
    weight_load(1).start()
    for owner in range(1, owners):
        row_load(owner).start()

    def cut_copy(owner, part_of, side):
        return pltpu.make_async_copy(
            out_buf.at[side, pl.ds(owner * owner_rows + part_of * piece, piece), :],
            cuts[owner * halves + part_of].at[:, pl.ds(pl.multiple_of(side * half, half), half)],
            cut_sems.at[side, owner * halves + part_of],
        )

    @pl.loop(0, 2 * owners)
    def _(step):
        owner, side = lax.div(step, 2), lax.rem(step, 2)
        for own in range(owners):
            pl.when(step == 2 * own)(row_load(own).wait)
        for own in range(2):
            pl.when(step == own)(weight_load(own).wait)
        here = pl.ds(pl.multiple_of(starts_ref[owner], owner_rows), owner_rows)
        there = pl.ds(pl.multiple_of(owner * owner_rows, owner_rows), owner_rows)
        out_buf[side, there, :] = jnp.dot(
            active_buf[here, :], weight_buf[side], preferred_element_type=jnp.float32
        ).astype(out_buf.dtype)
        for own in range(owners):

            @pl.when(owner == own)
            def _(own=own):
                for part_of in range(halves):
                    cut_copy(own, part_of, side).start()

    for side in range(2):
        for own in range(owners):
            for part_of in range(halves):
                cut_copy(own, part_of, side).wait()


def feed_rows(active, weight):
    low = jnp.bfloat16
    rows, hidden = active.shape
    depth = weight.shape[1]
    half = depth // 2
    starts, owners, halves = owner_cuts(rows)
    cut = jax.ShapeDtypeStruct((rows // owners // halves, depth), low)
    return tuple(
        whole_call(
            functools.partial(feed_kernel, halves=halves),
            [SMEM] + [ANY] * 2,
            [ANY] * (owners * halves),
            [cut] * (owners * halves),
            [
                pltpu.VMEM((rows, hidden), low),
                pltpu.VMEM((2, hidden, half), low),
                pltpu.VMEM((2, rows, half), low),
                pltpu.SemaphoreType.DMA((2 + owners,)),
                pltpu.SemaphoreType.DMA((2, owners * halves)),
            ],
        )(starts, active, weight)
    )


def hidden_grads_kernel(grad_rows, weight, slope, x, hidden_out, up_out, sum_out, *refs):
    grad_buf, weight_buf, slope_buf, x_buf, hidden_buf, tiles = refs[:6]
    load_sems, slope_sems, hidden_sems, tile_sems = refs[6:]
    rows = grad_buf.shape[0]
    parts, _, part = hidden_buf.shape
    x_blocks, _, x_block = x_buf.shape
    chunk = slope_buf.shape[1]
    chunks = rows // chunk

    def load(source, target, index):
        return pltpu.make_async_copy(source, target, load_sems.at[index])

    def grad_load(index):
        here = pl.ds(pl.multiple_of(index * chunk, chunk), chunk)
        return load(grad_rows.at[here, :], grad_buf.at[here, :], index)

    def weight_load(index):
        here = pl.ds(pl.multiple_of(index * part, part), part)
        return load(weight.at[here, :], weight_buf.at[here, :], chunks + index)

    x_loads = [
        load(columns_of(x, i, x_block), x_buf.at[i], chunks + parts + i) for i in range(x_blocks)
    ]

    def slope_copy(step, slot):
        place = (
            pl.ds(pl.multiple_of(lax.rem(step, chunks) * chunk, chunk), chunk),
            pl.ds(pl.multiple_of(lax.div(step, chunks) * part, part), part),
        )
        return pltpu.make_async_copy(slope.at[place], slope_buf.at[slot], slope_sems.at[slot])

    def hidden_copy(index):
        return pltpu.make_async_copy(
            hidden_buf.at[index],
            hidden_out.at[:, pl.ds(index * part, part)],
            hidden_sems.at[index],
        )

    weight_load(0).start()
    grad_load(0).start()
    slope_copy(0, 0).start()
    for index in range(1, chunks):
        grad_load(index).start()
    for index in range(1, parts):
        weight_load(index).start()
    for copy in x_loads:
        copy.start()
    sum_out[...] = jnp.zeros_like(sum_out)

    @pl.loop(0, parts * chunks)
    def _(step):
        slot = lax.rem(step, 2)
        index = lax.div(step, chunks)

        @pl.when(step + 1 < parts * chunks)
        def _():
            slope_copy(step + 1, 1 - slot).start()

        @pl.when(lax.rem(step, chunks) == 0)
        def _():
            weight_load(index).wait()

        @pl.when(index == 0)
        def _():
            grad_load(step).wait()

        slope_copy(step, slot).wait()
        here = pl.ds(pl.multiple_of(lax.rem(step, chunks) * chunk, chunk), chunk)
        units = pl.ds(pl.multiple_of(index * part, part), part)
        product = nt_dot(grad_buf[here, :], weight_buf[units, :])
        low = (product * wide(slope_buf[slot])).astype(hidden_buf.dtype)
        hidden_buf[index, here, :] = low
        sum_out[index] += jnp.sum(wide(low), axis=0, keepdims=True)

    for index in range(parts):
        hidden_copy(index).start()
    for copy in x_loads:
        copy.wait()
    tile_loop(
        x_blocks * parts,
        tiles,
        tile_sems,
        lambda step: up_out.at[
            pl.ds(pl.multiple_of(lax.div(step, parts) * x_block, x_block), x_block),
            pl.ds(pl.multiple_of(lax.rem(step, parts) * part, part), part),
        ],
        lambda step: tn_dot(x_buf[lax.div(step, parts)], hidden_buf[lax.rem(step, parts)]),
    )
    for index in range(parts):
        hidden_copy(index).wait()


def hidden_grads(grad_rows, weight, slope, x):
    low = jnp.bfloat16
    rows, depth = grad_rows.shape
    hidden = weight.shape[0]
    part, x_block, chunk = min(1024, hidden), min(512, depth), min(512, rows)
    return whole_call(
        hidden_grads_kernel,
        [ANY] * 4,
        [ANY, ANY, VMEM],
        [
            jax.ShapeDtypeStruct((rows, hidden), low),
            jax.ShapeDtypeStruct((depth, hidden), low),
            jax.ShapeDtypeStruct((hidden // part, 1, part), jnp.float32),
        ],
        [
            pltpu.VMEM((rows, depth), low),
            pltpu.VMEM((hidden, depth), low),
            pltpu.VMEM((2, chunk, part), low),
            pltpu.VMEM((depth // x_block, rows, x_block), low),
            pltpu.VMEM((hidden // part, rows, part), low),
            pltpu.VMEM((2, x_block, part), low),
            pltpu.SemaphoreType.DMA((rows // chunk + hidden // part + depth // x_block,)),
            pltpu.SemaphoreType.DMA((2,)),
            pltpu.SemaphoreType.DMA((hidden // part,)),
            pltpu.SemaphoreType.DMA((2,)),
        ],
    )(grad_rows, weight, slope, x)


def last_grads_kernel(
    x, joined, grad_rows, mixed, out, x_buf, joined_buf, tiles, x_sems, joined_sems, tile_sems
):
    blocks = x_buf.shape[0] // 2
    block = x_buf.shape[2]

    def x_load(index):
        source = x if index < blocks else grad_rows
        return pltpu.make_async_copy(
            columns_of(source, index % blocks, block), x_buf.at[index], x_sems.at[index]
        )

    def joined_load(slot):
        source = joined.at[slot] if slot < 3 else mixed
        return pltpu.make_async_copy(source, joined_buf.at[slot], joined_sems.at[slot])

    joined_load(0).start()
    for index in range(blocks):
        x_load(index).start()
    for slot in range(1, 4):
        joined_load(slot).start()
    for index in range(blocks, 2 * blocks):
        x_load(index).start()

    def compute(step):
        for slot in range(4):
            pl.when(step == slot * blocks)(joined_load(slot).wait)
        for index in range(blocks):
            pl.when(step == index)(x_load(index).wait)
            pl.when(step == 3 * blocks + index)(x_load(blocks + index).wait)
        slot = lax.div(step, blocks)
        index = lax.rem(step, blocks) + blocks * lax.div(slot, 3)
        return tn_dot(x_buf[index], joined_buf[slot])

    tile_loop(
        4 * blocks,
        tiles,
        tile_sems,
        lambda step: rows_of(out.at[lax.div(step, blocks)], lax.rem(step, blocks), block),
        compute,
    )


def last_grads(x, joined, grad_rows, mixed):
    low = jnp.bfloat16
    rows, depth = x.shape
    width = joined.shape[2]
    block = min(1024, depth)
    return whole_call(
        last_grads_kernel,
        [ANY] * 4,
        ANY,
        jax.ShapeDtypeStruct((4, depth, width), low),
        [
            pltpu.VMEM((2 * depth // block, rows, block), low),
            pltpu.VMEM((4, rows, width), low),
            pltpu.VMEM((2, block, width), low),
            pltpu.SemaphoreType.DMA((2 * depth // block,)),
            pltpu.SemaphoreType.DMA((4,)),
            pltpu.SemaphoreType.DMA((2,)),
        ],
    )(x, joined, grad_rows, mixed)


def normed_grads_kernel(
    starts_ref, joined, qkv, hidden, up, x, mean_ref, root_ref, gain_ref, shift_ref, *refs, halves
):
    cuts = refs[:-8]
    joined_buf, qkv_buf, hidden_buf, up_buf, x_buf, out_buf, load_sems, cut_sems = refs[-8:]
    owners = len(cuts) // halves
    rows = hidden_buf.shape[0]
    owner_rows = rows // owners
    piece = owner_rows // halves

    def load(source, target, index):
        return pltpu.make_async_copy(source, target, load_sems.at[index])

    def row_loads(owner):
        here = pl.ds(pl.multiple_of(starts_ref[owner], owner_rows), owner_rows)
        at = 4 + owner * 3
        return (
            load(hidden.at[here, :], hidden_buf.at[here, :], at),
            load(joined.at[:, here, :], joined_buf.at[:, here, :], at + 1),
            load(x.at[here, :], x_buf.at[here, :], at + 2),
        )

    weights = [load(up, up_buf, 0), load(qkv, qkv_buf, 1)]
    weights[0].start()
    for copy in row_loads(0):
        copy.start()
    weights[1].start()
    for owner in range(1, owners):
        for copy in row_loads(owner):
            copy.start()
    gain_ref[...] = jnp.zeros_like(gain_ref)
    shift_ref[...] = jnp.zeros_like(shift_ref)
    for copy in weights:
        copy.wait()

    def cut_copy(owner, part_of):
        return pltpu.make_async_copy(
            out_buf.at[pl.ds(owner * owner_rows + part_of * piece, piece), :],
            cuts[owner * halves + part_of],
            cut_sems.at[owner * halves + part_of],
        )

    @pl.loop(0, owners)
    def _(owner):
        for copy in row_loads(owner):
            copy.wait()
        here = pl.ds(pl.multiple_of(starts_ref[owner], owner_rows), owner_rows)
        there = pl.ds(pl.multiple_of(owner * owner_rows, owner_rows), owner_rows)
        columns = up_buf.shape[0]
        chunk = min(512, columns)
        for start in range(0, columns, chunk):
            mine = slice(start, start + chunk)
            total = nt_dot(hidden_buf[here, :], up_buf[mine, :])
            for slot in range(3):
                total += nt_dot(joined_buf[slot, here, :], qkv_buf[slot, mine, :])
            out_buf[there, mine] = total.astype(out_buf.dtype)
            hat = (wide(x_buf[here, mine]) - mean_ref[here, :]) * root_ref[here, :]
            gain_ref[:, mine] += jnp.sum(total * hat, axis=0, keepdims=True)
            shift_ref[:, mine] += jnp.sum(total, axis=0, keepdims=True)
        for own in range(owners):

            @pl.when(owner == own)
            def _(own=own):
                for part_of in range(halves):
                    cut_copy(own, part_of).start()

    for own in range(owners):
        for part_of in range(halves):
            cut_copy(own, part_of).wait()


def normed_grads(joined, qkv, hidden, up, x, mean, root, first, last):
    low = jnp.bfloat16
    rows, units = hidden.shape
    width = joined.shape[2]
    columns = last - first
    starts, owners, halves = owner_cuts(rows)
    cut = jax.ShapeDtypeStruct((rows // owners // halves, columns), low)
    line = jax.ShapeDtypeStruct((1, columns), jnp.float32)

    def kernel(starts_ref, joined, qkv, hidden, up, x, *refs):
        mine = pl.ds(first, columns)
        normed_grads_kernel(
            starts_ref,
            joined,
            qkv.at[:, mine, :],
            hidden,
            up.at[mine, :],
            x.at[:, mine],
            *refs,
            halves=halves,
        )

    result = whole_call(
        kernel,
        [SMEM] + [ANY] * 5 + [VMEM] * 2,
        [VMEM, VMEM] + [ANY] * (owners * halves),
        [line, line] + [cut] * (owners * halves),
        [
            pltpu.VMEM((3, rows, width), low),
            pltpu.VMEM((3, columns, width), low),
            pltpu.VMEM((rows, units), low),
            pltpu.VMEM((columns, units), low),
            pltpu.VMEM((rows, columns), low),
            pltpu.VMEM((rows, columns), low),
            pltpu.SemaphoreType.DMA((4 + 3 * owners,)),
            pltpu.SemaphoreType.DMA((owners * halves,)),
        ],
    )(starts, joined, qkv, hidden, up, x, mean, root)
    return result[0], result[1], tuple(result[2:])


def finish_kernel(*refs):
    mixed, dense = refs[:4], refs[4:9]
    token_ref, bias_ref = refs[9:11]
    last_first, last_second, first_near, second_near, low, high = refs[11:17]
    out_ref = refs[17]
    half = low.shape[0]
    far = dense[3].shape[0]
    total = jnp.dot(mixed[0][...], dense[0][...], preferred_element_type=jnp.float32)
    total += jnp.dot(mixed[1][...], dense[1][...], preferred_element_type=jnp.float32)
    total += jnp.dot(mixed[2][...], dense[2][...], preferred_element_type=jnp.float32)
    total += jnp.dot(mixed[3][:, :far], dense[3][...], preferred_element_type=jnp.float32)
    total += jnp.dot(mixed[3][:, far:], dense[4][...], preferred_element_type=jnp.float32)
    total += wide(token_ref[...]) + bias_ref[...]
    for here, parts in (
        (slice(0, half), (low, first_near, last_first)),
        (slice(half, 2 * half), (high, second_near, last_second)),
    ):
        feed = wide(parts[0][...]) + wide(parts[1][...]) + wide(parts[2][...])
        out_ref[here, :] = (total[here] + feed).astype(out_ref.dtype)


def finish_output(mixed_parts, dense_parts, tokens, bias, feed_parts):
    rows, depth = tokens.shape
    if len(feed_parts) == 1:
        attended = jnp.dot(mixed_parts[0], dense_parts[0], preferred_element_type=jnp.float32)
        return (wide(tokens) + attended + feed_parts[0] + bias).astype(tokens.dtype)
    columns = min(512, depth)

    def column_block(piece):
        return pl.BlockSpec((piece.shape[0], columns), lambda j: (0, j))

    return pl.pallas_call(
        finish_kernel,
        grid=(depth // columns,),
        in_specs=[pl.BlockSpec(piece.shape, lambda j: (0, 0)) for piece in mixed_parts]
        + [column_block(piece) for piece in dense_parts]
        + [column_block(tokens), pl.BlockSpec((1, columns), lambda j: (0, j))]
        + [column_block(piece) for piece in feed_parts],
        out_specs=column_block(tokens),
        out_shape=jax.ShapeDtypeStruct(tokens.shape, tokens.dtype),
        compiler_params=pltpu.CompilerParams(vmem_limit_bytes=VMEM_BYTES),
        cost_estimate=SHORT,
    )(*mixed_parts, *dense_parts, tokens, bias.reshape(1, depth), *feed_parts)


def token_grads_kernel(*refs, steps):
    left, right = refs[:6], refs[6:12]
    token_ref, grad_ref, mean_ref, root_ref, gain_ref, out_ref = refs[12:]
    split = left[4].shape[1]
    mean_own, root_own = mean_ref[...], root_ref[...]

    def rows_of_half(upper):
        scaled, hats = [], []
        for side, parts in enumerate((left, right)):
            columns = slice(side * split, (side + 1) * split)
            total = sum(wide(parts[at + upper][...]) for at in (4, 2, 0))
            scaled.append(total * gain_ref[:, columns])
            hats.append((wide(token_ref[:, columns]) - mean_own) * root_own)
        count = 2 * split
        mean = sum(jnp.sum(v, axis=-1, keepdims=True) for v in scaled) / count
        slant = sum(jnp.sum(v * h, axis=-1, keepdims=True) for v, h in zip(scaled, hats)) / count
        for side in range(2):
            columns = slice(side * split, (side + 1) * split)
            grad = root_own * (scaled[side] - mean - hats[side] * slant)
            out_ref[:, columns] = (wide(grad_ref[:, columns]) + grad).astype(out_ref.dtype)

    step = pl.program_id(0)
    pl.when(step < steps)(lambda: rows_of_half(0))
    pl.when(step >= steps)(lambda: rows_of_half(1))


def token_grads(left_parts, right_parts, tokens, cotangent, mean, root, gain):
    if len(left_parts) == 1:
        grad = jnp.concatenate([left_parts[0], right_parts[0]], axis=1)
        hat = (wide(tokens) - mean) * root
        scaled = grad * gain
        grad_input = root * (
            scaled
            - jnp.mean(scaled, axis=-1, keepdims=True)
            - hat * jnp.mean(scaled * hat, axis=-1, keepdims=True)
        )
        return (wide(cotangent) + grad_input).astype(tokens.dtype)
    half, split = left_parts[4].shape
    rows, depth = tokens.shape
    chunk = min(64, half)
    steps = half // chunk
    low_part = pl.BlockSpec((chunk, split), lambda i: (jnp.minimum(i, steps - 1), 0))
    high_part = pl.BlockSpec((chunk, split), lambda i: (jnp.maximum(i - steps, 0), 0))
    row_block = pl.BlockSpec((chunk, depth), lambda i: (i, 0))
    thin = pl.BlockSpec((chunk, 1), lambda i: (i, 0))
    return pl.pallas_call(
        functools.partial(token_grads_kernel, steps=steps),
        grid=(rows // chunk,),
        in_specs=[low_part, high_part] * 6
        + [row_block, row_block, thin, thin, pl.BlockSpec((1, depth), lambda i: (0, 0))],
        out_specs=row_block,
        out_shape=jax.ShapeDtypeStruct(tokens.shape, tokens.dtype),
        compiler_params=pltpu.CompilerParams(vmem_limit_bytes=VMEM_BYTES),
        cost_estimate=SHORT,
    )(*left_parts, *right_parts, tokens, cotangent, mean, root, gain.reshape(1, -1))


def attention_kernel(
    q_ref,
    k_ref,
    v_ref,
    g_ref,
    cos_ref,
    above_ref,
    below_ref,
    mixed_ref,
    grads_ref,
    sums_ref,
    keys_across,
    values_across,
    query_total,
    key_total,
    value_total,
    weight_buf,
    top_buf,
    out_buf,
    across_buf,
    *,
    block,
    block_count,
):
    step = pl.program_id(1)
    scale = HEAD_DIM**-0.5
    rate = scale * 1.4426950408889634

    @pl.when(step == 0)
    def _():
        keys_across[...] = k_ref[...].T
        values_across[...] = v_ref[...].T
        key_total[...] = jnp.zeros_like(key_total)
        value_total[...] = jnp.zeros_like(value_total)

    rows = pl.ds(pl.multiple_of(step * block, block), block)
    queries, grads = q_ref[rows, :], g_ref[rows, :]
    lane = lax.broadcasted_iota(jnp.int32, (block, PAIR), 1)
    own_lanes = [lane // HEAD_DIM == head for head in range(2)]
    query_heads = [jnp.where(own, queries, jnp.zeros_like(queries)) for own in own_lanes]
    grad_heads = [jnp.where(own, grads, jnp.zeros_like(grads)) for own in own_lanes]
    parts = [slice(head * HEAD_DIM, (head + 1) * HEAD_DIM) for head in range(2)]

    def weigh(there, index, first):
        keys = k_ref[there, :]
        score_heads = [
            lax.dot_general(keys, own, ROWS_BY_ROWS, preferred_element_type=jnp.float32)
            for own in query_heads
        ]
        for head in range(2):
            scores = score_heads[head]
            if first:
                key_pos = lax.broadcasted_iota(jnp.int32, (block, block), 0)
                query_pos = lax.broadcasted_iota(jnp.int32, (block, block), 1)
                scores = jnp.where(key_pos <= query_pos, scores, masked_score)
            top = jnp.max(scores, axis=0, keepdims=True) * rate
            if not first:
                before = top_buf[head, 0]
                top = jnp.maximum(top, before)
            weights = jnp.exp2(scores * rate - top)
            weight_buf[head, there, :] = weights
            top_buf[head, 2 + index] = top
            total = jnp.sum(weights, axis=0, keepdims=True)
            out = jnp.dot(
                values_across[parts[head], there],
                weights.astype(jnp.bfloat16),
                preferred_element_type=jnp.float32,
            )
            if not first:
                shrink = jnp.exp2(before - top)
                total += top_buf[head, 1] * shrink
                out += out_buf[parts[head], :] * shrink
            top_buf[head, 0] = top
            top_buf[head, 1] = total
            out_buf[parts[head], :] = out

    def over_blocks(act):
        act(rows, step, True)

        @pl.when(lax.rem(step, 2) == 1)
        def _():
            act(pl.ds(pl.multiple_of((step - 1) * block, block), block), step - 1, False)

        @pl.loop(0, lax.div(step, 2))
        def _(index):
            start = pl.multiple_of(index * 2 * block, 2 * block)
            act(pl.ds(start, 2 * block), 2 * index, False)

    over_blocks(weigh)

    grads_across = grads.T.astype(jnp.float32)
    inner, share = [], []
    for head in range(2):
        share.append(1.0 / top_buf[head, 1])
        out = out_buf[parts[head], :] * share[head]
        out_buf[parts[head], :] = out
        inner.append(jnp.sum(out * grads_across[parts[head]], axis=0, keepdims=True))
    mixed_ref[rows, :] = out_buf[...].T.astype(mixed_ref.dtype)

    def differentiate(there, index, first):
        values = v_ref[there, :]
        prob_heads = [
            lax.dot_general(values, own, ROWS_BY_ROWS, preferred_element_type=jnp.float32)
            for own in grad_heads
        ]
        value_parts, key_parts = [], []
        for head in range(2):
            factor = jnp.exp2(top_buf[head, 2 + index] - top_buf[head, 0]) * share[head]
            exact = weight_buf[head, there, :] * factor
            rounded = exact.astype(jnp.bfloat16)
            grad_scores = (exact * (prob_heads[head] - inner[head])).astype(jnp.bfloat16)
            value_parts.append(
                jnp.dot(rounded, grad_heads[head], preferred_element_type=jnp.float32)
            )
            key_parts.append(
                jnp.dot(grad_scores, query_heads[head], preferred_element_type=jnp.float32)
            )
            across = jnp.dot(
                keys_across[parts[head], there], grad_scores, preferred_element_type=jnp.float32
            )
            if first:
                across_buf[parts[head], :] = across
            else:
                across_buf[parts[head], :] += across
        value_total[there, :] += value_parts[0] + value_parts[1]
        key_total[there, :] += key_parts[0] + key_parts[1]

    over_blocks(differentiate)
    query_total[rows, :] = across_buf[...].T

    @pl.when(step == block_count - 1)
    def _():
        lanes = cos_ref[...], above_ref[...], below_ref[...]
        for slot, field in enumerate(
            (
                turn_back(query_total[...] * scale, *lanes),
                turn_back(key_total[...] * scale, *lanes),
                value_total[...],
            )
        ):
            low = field.astype(grads_ref.dtype)
            grads_ref[slot] = low
            sums_ref[slot] = jnp.sum(low.astype(jnp.float32), axis=0, keepdims=True)


def attention(joined, grad_mixed, lanes, first, last, earlier=None):
    rows, width = grad_mixed.shape
    block = min(512, LENGTH)
    pairs, block_count = width // PAIR, LENGTH // block
    row_block = pl.BlockSpec((LENGTH, PAIR), lambda p, i: (0, first + p))
    table = pl.BlockSpec((LENGTH, PAIR), lambda p, i: (0, 0))
    kept = () if earlier is None else tuple(earlier)
    kernel = functools.partial(attention_kernel, block=block, block_count=block_count)

    def body(*refs):
        kernel(*refs[:7], *refs[7 + len(kept) :])

    return pl.pallas_call(
        body,
        grid=(last - first, block_count),
        in_specs=[
            row_block,
            pl.BlockSpec((LENGTH, PAIR), lambda p, i: (0, pairs + first + p)),
            pl.BlockSpec((LENGTH, PAIR), lambda p, i: (0, 2 * pairs + first + p)),
            row_block,
            table,
            table,
            table,
        ]
        + [pl.BlockSpec(memory_space=pl.ANY)] * len(kept),
        out_specs=[
            row_block,
            pl.BlockSpec((3, LENGTH, PAIR), lambda p, i: (0, 0, first + p)),
            pl.BlockSpec((3, 1, PAIR), lambda p, i: (0, 0, first + p)),
        ],
        out_shape=[
            jax.ShapeDtypeStruct((rows, width), jnp.bfloat16),
            jax.ShapeDtypeStruct((3, rows, width), jnp.bfloat16),
            jax.ShapeDtypeStruct((3, 1, width), jnp.float32),
        ],
        scratch_shapes=[
            pltpu.VMEM((PAIR, LENGTH), jnp.bfloat16),
            pltpu.VMEM((PAIR, LENGTH), jnp.bfloat16),
            pltpu.VMEM((LENGTH, PAIR), jnp.float32),
            pltpu.VMEM((LENGTH, PAIR), jnp.float32),
            pltpu.VMEM((LENGTH, PAIR), jnp.float32),
            pltpu.VMEM((2, LENGTH, block), jnp.float32),
            pltpu.VMEM((2, 2 + block_count, 1, block), jnp.float32),
            pltpu.VMEM((PAIR, block), jnp.float32),
            pltpu.VMEM((PAIR, block), jnp.float32),
        ],
        input_output_aliases={7 + i: i for i in range(len(kept))},
        compiler_params=pltpu.CompilerParams(vmem_limit_bytes=VMEM_BYTES),
        cost_estimate=SHORT,
    )(joined, joined, joined, grad_mixed, *lanes, *kept)


def norm_kernel(starts_ref, gain_ref, shift_ref, following_ref, *refs):
    count = (len(refs) - 6) // 3
    pieces = refs[:count]
    raw, normed, mean_ref, root_ref, following_out = refs[count : count + 5]
    buffers = refs[count + 5 : 2 * count + 5]
    results = refs[2 * count + 5 : 3 * count + 5]
    sems = refs[-1]
    following_out[...] = following_ref[...]
    for slot in range(count):
        pltpu.make_async_copy(pieces[slot], buffers[slot], sems.at[0, slot]).start()
    writes = []
    for slot in range(count):
        buffer, result = buffers[slot], results[slot]
        size = buffer.shape[0]
        where = pl.ds(pl.multiple_of(starts_ref[slot], size), size)
        pltpu.make_async_copy(pieces[slot], buffer, sems.at[0, slot]).wait()
        write = pltpu.make_async_copy(buffer, raw.at[where, :], sems.at[1, slot])
        write.start()
        writes.append(write)
        chunk = min(128, size)

        @pl.loop(0, size // chunk)
        def _(step, buffer=buffer, result=result, slot=slot):
            here = pl.ds(pl.multiple_of(step * chunk, chunk), chunk)
            rows = buffer[here, :].astype(jnp.float32)
            mean = jnp.mean(rows, axis=-1, keepdims=True)
            centred = rows - mean
            variance = jnp.mean(centred * centred, axis=-1, keepdims=True)
            root = lax.rsqrt(variance + epsilon)
            out = centred * root * gain_ref[...] + shift_ref[...]
            result[here, :] = out.astype(result.dtype)
            there = pl.ds(pl.multiple_of(starts_ref[slot] + step * chunk, chunk), chunk)
            mean_ref[there, :] = mean
            root_ref[there, :] = root

        write = pltpu.make_async_copy(result, normed.at[where, :], sems.at[2, slot])
        write.start()
        writes.append(write)
    for write in writes:
        write.wait()


def norm_rows(pieces, gain, shift, following):
    depth = gain.shape[0]
    total = sum(piece.shape[0] for _, piece in pieces)
    count = len(pieces)
    low = jnp.bfloat16
    starts = jnp.stack([jnp.asarray(start, jnp.int32) for start, _ in pieces])
    any_space = pl.BlockSpec(memory_space=pl.ANY)
    vmem = pl.BlockSpec(memory_space=pltpu.VMEM)
    stage = [pltpu.VMEM(piece.shape, low) for _, piece in pieces]
    return pl.pallas_call(
        norm_kernel,
        in_specs=[pl.BlockSpec(memory_space=pltpu.SMEM), vmem, vmem, vmem] + [any_space] * count,
        out_specs=[any_space, any_space, vmem, vmem, vmem],
        out_shape=[
            jax.ShapeDtypeStruct((total, depth), low),
            jax.ShapeDtypeStruct((total, depth), low),
            jax.ShapeDtypeStruct((total, 1), jnp.float32),
            jax.ShapeDtypeStruct((total, 1), jnp.float32),
            jax.ShapeDtypeStruct(following.shape, following.dtype),
        ],
        scratch_shapes=stage + stage + [pltpu.SemaphoreType.DMA((3, count))],
        compiler_params=pltpu.CompilerParams(vmem_limit_bytes=VMEM_BYTES),
        cost_estimate=SHORT,
    )(
        starts,
        gain.reshape(1, depth),
        shift.reshape(1, depth),
        following,
        *[piece for _, piece in pieces],
    )


def on_device(
    tokens,
    norm_gain,
    norm_shift,
    weight_qkv,
    bias_qkv,
    weight_dense,
    weight_up,
    bias_up,
    weight_down,
    bias_out,
    cotangent,
):
    f32, low = jnp.float32, jnp.bfloat16
    depth = tokens.shape[1]
    local_rows = tokens.shape[0]
    tensor_index = lax.axis_index("tensor")

    full_up = lax.all_gather(weight_up, "dp", axis=0, tiled=True)
    token_parts = gather_start(tokens)
    lanes = lane_tables(LENGTH)
    out_part = jnp.sum(cotangent, axis=0, dtype=f32)
    lanes, out_part, token_parts = after((lanes, out_part, token_parts))
    full_qkv = lax.all_gather(
        after(jnp.transpose(weight_qkv, (1, 0, 2)), token_parts), "dp", axis=1, tiled=True
    )
    token_parts = gather_pass(token_parts)
    all_tokens, gathered, mean, root, sent = norm_rows(
        gathered_pieces(token_parts), norm_gain, norm_shift, cotangent
    )
    grad_parts = gather_start(sent)

    full_dense = lax.all_gather(after(weight_dense, gathered), "dp", axis=1, tiled=True)
    own_mean = lax.dynamic_slice_in_dim(mean, tensor_index * local_rows, local_rows, 0)
    own_root = lax.dynamic_slice_in_dim(root, tensor_index * local_rows, local_rows, 0)
    active, slope = hidden_rows(gathered, full_up, bias_up)
    own_mean, own_root, active = after((own_mean, own_root, active))
    grad_parts, active = after((grad_parts, active))
    full_down = lax.all_gather(after(weight_down, grad_parts), "dp", axis=1, tiled=True)
    grad_parts = gather_pass(grad_parts)
    joined = joined_rows(after(gathered, active, grad_parts[:3]), full_qkv, bias_qkv, lanes)
    grad_parts, joined = after((grad_parts, joined))
    grad_rows, grad_down = first_grads(gathered_pieces(grad_parts), active)
    grad_mixed = jnp.einsum(
        "td,kd->tk", grad_rows, after(full_dense, grad_down), preferred_element_type=f32
    ).astype(low)
    dense_parts = gather_start(after(full_dense, grad_mixed))
    grad_down_sum = lax.psum_scatter(grad_down, "dp", scatter_dimension=1, tiled=True)

    pairs = grad_mixed.shape[1] // PAIR
    part = attention(joined, grad_mixed, lanes, 0, pairs // 2)
    dense_parts, part = after((dense_parts, part))
    dense_parts = gather_pass(dense_parts)
    feed_cuts = feed_rows(after(active, part[0]), full_down)
    feed_cuts, dense_parts = after((feed_cuts, dense_parts))
    feed_parts = scatter_send(feed_cuts)
    grad_hidden, grad_up, bias_up_part = hidden_grads(
        after(grad_rows, feed_cuts), full_down, slope, gathered
    )
    grad_up, feed_parts = after((grad_up, feed_parts))
    feed_parts = scatter_fold(feed_parts)
    grad_up_sum = lax.psum_scatter(
        after(grad_up, grad_down_sum, feed_parts[:2]), "dp", scatter_dimension=0, tiled=True
    )
    feed_parts = scatter_pass(feed_parts)
    part = attention(after(joined, grad_up), grad_mixed, lanes, pairs // 2, pairs, part)
    mixed, grad_joined, bias_qkv_part = part
    mixed, grad_joined, feed_parts = after((mixed, grad_joined, feed_parts))

    mixed_parts = exchange_start(mixed)
    grad_last = last_grads(gathered, grad_joined, grad_rows, mixed)
    grad_last, mixed_parts = after((grad_last, mixed_parts))
    grad_last_sum = lax.psum_scatter(
        after(grad_last, grad_up_sum), "dp", scatter_dimension=1, tiled=True
    )
    half = depth // 2
    sources = full_qkv, grad_hidden, full_up, all_tokens, mean, root
    *left_sums, left_cuts = normed_grads(after(grad_joined, grad_last), *sources, 0, half)
    left_parts = scatter_send(left_cuts)
    *right_sums, right_cuts = normed_grads(after(grad_joined, left_cuts), *sources, half, depth)
    right_cuts, right_sums, left_parts = after((right_cuts, right_sums, left_parts))
    sums = jnp.concatenate(
        [left_sums[0][0], right_sums[0][0], left_sums[1][0], right_sums[1][0], out_part]
    ).reshape(-1, PAIR)
    right_parts = scatter_send(right_cuts)
    left_parts, sums = after((scatter_fold(left_parts), sums))
    over_group = exchange_sum(sums, "tensor")
    left_parts = scatter_pass(left_parts)
    block_out = finish_output(
        after(mixed_parts, right_cuts), dense_parts, tokens, bias_out, feed_parts
    )
    block_out, right_parts, left_parts, over_group = after(
        (block_out, right_parts, left_parts, over_group)
    )
    right_parts = scatter_pass(scatter_fold(right_parts))
    bias_size = bias_qkv.size
    over_dp = jnp.concatenate(
        [over_group.reshape(-1), bias_qkv_part.reshape(-1), bias_up_part.reshape(-1)]
    ).reshape(-1, PAIR)
    over_dp = over_dp + swap(over_dp, "dp", 1)
    over_dp = exchange_sum(over_dp, "dp", 2).reshape(-1)
    grad_gain, grad_shift, grad_bias_out = over_dp[: 3 * depth].reshape(3, depth)
    grad_bias_qkv = over_dp[3 * depth : 3 * depth + bias_size].reshape(bias_qkv.shape)
    grad_bias_up = over_dp[3 * depth + bias_size :]
    last = jnp.transpose(grad_last_sum, (1, 0, 2)).astype(f32)
    ready = grad_up_sum.astype(f32), grad_down_sum.astype(f32), last
    ready, left_parts = after((ready, left_parts))
    grad_up_sum, grad_down_sum, last = ready
    grad_tokens = token_grads(
        left_parts, right_parts, tokens, cotangent, own_mean, own_root, norm_gain
    )
    return (
        block_out,
        grad_tokens,
        grad_gain,
        grad_shift,
        last[:, :3],
        grad_bias_qkv,
        jnp.transpose(last[:, 3]),
        grad_up_sum,
        grad_bias_up,
        grad_down_sum,
        grad_bias_out,
    )


def solution(mesh):
    in_specs = (
        P(("dp", "tensor"), None),
        P(),
        P(),
        P("dp", None, "tensor"),
        P(None, "tensor"),
        P("tensor", "dp"),
        P("dp", "tensor"),
        P("tensor"),
        P("tensor", "dp"),
        P(),
        P(("dp", "tensor"), None),
    )
    out_specs = (
        P(("dp", "tensor"), None),
        P(("dp", "tensor"), None),
        P(),
        P(),
        P("dp", None, "tensor"),
        P(None, "tensor"),
        P("tensor", "dp"),
        P("dp", "tensor"),
        P("tensor"),
        P("tensor", "dp"),
        P(),
    )
    return jax.shard_map(
        on_device, mesh=mesh, in_specs=in_specs, out_specs=out_specs, check_vma=False
    )
```

```python
import functools

import jax
import jax.numpy as jnp
from jax import lax
from jax.experimental import pallas as pl
from jax.experimental.pallas import tpu as pltpu
from jax.sharding import PartitionSpec as P

HEAD_DIM = 64
ROT = 32
LENGTH = 2048
PAIR = 2 * HEAD_DIM

epsilon = 1e-05
masked_score = -1e30
MIB = 1024 * 1024
VMEM_BYTES = 64 * MIB - 256 * 1024
ROWS_BY_ROWS = (((1,), (1,)), ((), ()))
COLUMNS_BY_COLUMNS = (((0,), (0,)), ((), ()))


SHORT = pl.CostEstimate(flops=1, bytes_accessed=1, transcendentals=0)


def after(value, *earlier):
    return lax.optimization_barrier((value,) + earlier)[0]


def swap(value, axis, bit):
    count = lax.axis_size(axis)
    return lax.ppermute(value, axis, [(i, i ^ bit) for i in range(count)])


def gather_start(block):
    if lax.axis_size("tensor") != 4:
        return (lax.all_gather(block, "tensor", axis=0, tiled=True),)
    return block, swap(block, "tensor", 1), swap(block, "tensor", 2)


def halves_kernel(one_ref, two_ref, low_ref, high_ref):
    half = one_ref.shape[0] // 2
    low_ref[...] = one_ref[:half, :]
    high_ref[...] = two_ref[half:, :]


def gather_pass(parts):
    if len(parts) == 1:
        return parts
    block, one, two = parts
    rows, depth = block.shape
    half = jax.ShapeDtypeStruct((rows // 2, depth), block.dtype)
    low, high = pl.pallas_call(
        halves_kernel,
        out_shape=[half, half],
        compiler_params=pltpu.CompilerParams(vmem_limit_bytes=VMEM_BYTES),
        cost_estimate=SHORT,
    )(one, two)
    return block, one, two, swap(low, "tensor", 2), swap(high, "tensor", 1)


def gathered_pieces(parts):
    if len(parts) == 1:
        return [(0, parts[0])]
    block, one, two, low, high = parts
    rows = block.shape[0]
    me = lax.axis_index("tensor")
    return [
        (me * rows, block),
        ((me ^ 1) * rows, one),
        ((me ^ 2) * rows, two),
        ((me ^ 3) * rows, low),
        ((me ^ 3) * rows + rows // 2, high),
    ]


def wide(piece):
    return piece.astype(jnp.float32)


def owner_cuts(total):
    count = lax.axis_size("tensor")
    rows = total // count
    me = lax.axis_index("tensor")
    if count == 4:
        order = [me ^ bit for bit in (3, 1, 2, 0)]
        half = rows // 2
        places = (((0, 0), (1, 0)), ((0, half), (3, 0)), ((2, 0), (1, half)), ((4, 0), (5, 0)))
        sizes = (rows, rows, half, half, half, half)
    else:
        order = list(range(count))
        places = tuple(((owner, 0),) for owner in range(count))
        sizes = (rows,) * count
    starts = jnp.stack([jnp.asarray(owner * rows, jnp.int32) for owner in order])
    return starts, places, sizes


def scatter_send(cuts):
    if lax.axis_size("tensor") != 4:
        whole = wide(jnp.concatenate(cuts))
        return (lax.psum_scatter(whole, "tensor", scatter_dimension=0, tiled=True),)
    for_one, for_two, two_low, one_high, low, high = cuts
    return swap(for_one, "tensor", 1), swap(for_two, "tensor", 2), two_low, one_high, low, high


def fold_kernel(a_ref, b_ref, c_ref, d_ref, ab_ref, cd_ref):
    half = a_ref.shape[0]
    ab_ref[...] = (wide(a_ref[...]) + wide(b_ref[:half, :])).astype(ab_ref.dtype)
    cd_ref[...] = (wide(c_ref[...]) + wide(d_ref[:half, :])).astype(cd_ref.dtype)


def scatter_fold(parts):
    if len(parts) == 1:
        return parts
    first, second, two_low, one_high, low, high = parts
    shape = jax.ShapeDtypeStruct(low.shape, low.dtype)
    forward = pl.pallas_call(
        fold_kernel,
        out_shape=[shape, shape],
        compiler_params=pltpu.CompilerParams(vmem_limit_bytes=VMEM_BYTES),
        cost_estimate=SHORT,
    )(two_low, first, one_high, second)
    return (*forward, first, second, low, high)


def scatter_pass(parts):
    if len(parts) == 1:
        return parts
    two_low, one_high, first_near, second_near, low, high = parts
    return (
        swap(two_low, "tensor", 2),
        swap(one_high, "tensor", 1),
        first_near,
        second_near,
        low,
        high,
    )


def exchange_start(columns):
    if lax.axis_size("tensor") != 4:
        return (lax.all_to_all(columns, "tensor", 0, 1, tiled=True),)
    rows = columns.shape[0] // 4
    me = lax.axis_index("tensor")
    pieces = []
    for bit in range(4):
        piece = lax.dynamic_slice_in_dim(columns, (me ^ bit) * rows, rows, 0)
        pieces.append(swap(piece, "tensor", bit) if bit else piece)
    return tuple(pieces)


def exchange_sum(value, axis, step=1):
    parts = [value]
    for bit in range(step, lax.axis_size(axis), step):
        parts.append(swap(value, axis, bit))
    return functools.reduce(lambda a, b: a + b, parts)


def lane_tables(row_total):
    half_rot = ROT // 2
    positions = (jnp.arange(row_total, dtype=jnp.int32) % LENGTH).astype(jnp.float32)
    inverse = 10000.0 ** (-(2.0 * jnp.arange(half_rot, dtype=jnp.float32)) / ROT)
    angles = positions[:, None] * inverse[None, :]
    cosine, sine = jnp.cos(angles), jnp.sin(angles)
    ones = jnp.ones((row_total, HEAD_DIM - ROT), jnp.float32)
    zeros = jnp.zeros((row_total, half_rot), jnp.float32)
    rest = jnp.zeros((row_total, HEAD_DIM - ROT), jnp.float32)
    cos_lanes = jnp.concatenate([cosine, cosine, ones] * 2, axis=1)
    from_above = jnp.concatenate([-sine, zeros, rest] * 2, axis=1)
    from_below = jnp.concatenate([zeros, sine, rest] * 2, axis=1)
    return cos_lanes, from_above, from_below


def turn(field, cos_lanes, from_above, from_below):
    half_rot = ROT // 2
    above = pltpu.roll(field, PAIR - half_rot, 1)
    below = pltpu.roll(field, half_rot, 1)
    return field * cos_lanes + above * from_above + below * from_below


def turn_back(field, cos_lanes, from_above, from_below):
    half_rot = ROT // 2
    above = pltpu.roll(field, PAIR - half_rot, 1)
    below = pltpu.roll(field, half_rot, 1)
    return field * cos_lanes - above * from_above - below * from_below


def joined_kernel(x_ref, w_ref, bias_ref, cos_ref, above_ref, below_ref, out_ref):
    width = out_ref.shape[1]
    chunk = min(256, width)
    slot = pl.program_id(0)

    def product(start):
        columns = slice(start, start + chunk)
        part = jnp.dot(x_ref[...], w_ref[0, :, columns], preferred_element_type=jnp.float32)
        return part + bias_ref[0, :, columns]

    @pl.when(slot < 2)
    def _():
        for start in range(0, width, chunk):
            part = product(start)
            for shift in range(0, chunk, PAIR):
                lanes = part[:, shift : shift + PAIR]
                turned = turn(lanes, cos_ref[...], above_ref[...], below_ref[...])
                columns = slice(start + shift, start + shift + PAIR)
                out_ref[:, columns] = turned.astype(out_ref.dtype)

    @pl.when(slot == 2)
    def _():
        for start in range(0, width, chunk):
            out_ref[:, start : start + chunk] = product(start).astype(out_ref.dtype)


def joined_rows(x, w, bias, lanes):
    rows, depth = x.shape
    width = w.shape[2]
    block = min(1024, rows)
    return pl.pallas_call(
        joined_kernel,
        grid=(3, rows // block),
        in_specs=[
            pl.BlockSpec((block, depth), lambda j, i: (i, 0)),
            pl.BlockSpec((1, depth, width), lambda j, i: (j, 0, 0)),
            pl.BlockSpec((1, 1, width), lambda j, i: (j, 0, 0)),
        ]
        + [pl.BlockSpec((block, PAIR), lambda j, i: (i, 0))] * 3,
        out_specs=pl.BlockSpec((block, width), lambda j, i: (i, j)),
        out_shape=jax.ShapeDtypeStruct((rows, 3 * width), jnp.bfloat16),
        compiler_params=pltpu.CompilerParams(vmem_limit_bytes=VMEM_BYTES),
        cost_estimate=SHORT,
    )(x, w, bias.reshape(3, 1, width), *lanes)


def hidden_kernel(x_ref, w_ref, bias_ref, active_ref, slope_ref):
    hidden = jnp.dot(x_ref[...], w_ref[...], preferred_element_type=jnp.float32) + bias_ref[...]
    scale = (2.0 / jnp.pi) ** 0.5
    square = hidden * hidden
    inner = scale * hidden * (1.0 + 0.044715 * square)
    bent = jnp.tanh(inner)
    half = 0.5 * (1.0 + bent)
    active_ref[...] = (hidden * half).astype(active_ref.dtype)
    growth = scale * (1.0 + (3.0 * 0.044715) * square)
    slope = half + 0.5 * hidden * (1.0 - bent * bent) * growth
    slope_ref[...] = slope.astype(slope_ref.dtype)


def hidden_rows(x, w, bias):
    rows, depth = x.shape
    width = w.shape[1]
    block, columns = min(1024, rows), min(1024, width)
    return pl.pallas_call(
        hidden_kernel,
        grid=(width // columns, rows // block),
        in_specs=[
            pl.BlockSpec((block, depth), lambda j, i: (i, 0)),
            pl.BlockSpec((depth, columns), lambda j, i: (0, j)),
            pl.BlockSpec((1, columns), lambda j, i: (0, j)),
        ],
        out_specs=[pl.BlockSpec((block, columns), lambda j, i: (i, j))] * 2,
        out_shape=[jax.ShapeDtypeStruct((rows, width), jnp.bfloat16)] * 2,
        compiler_params=pltpu.CompilerParams(vmem_limit_bytes=VMEM_BYTES),
        cost_estimate=SHORT,
    )(x, w, bias.reshape(1, width))


def whole_call(kernel, in_specs, out_specs, out_shape, scratch):
    return pl.pallas_call(
        kernel,
        in_specs=in_specs,
        out_specs=out_specs,
        out_shape=out_shape,
        scratch_shapes=scratch,
        compiler_params=pltpu.CompilerParams(vmem_limit_bytes=VMEM_BYTES),
        cost_estimate=SHORT,
    )


def columns_of(ref, index, size):
    return ref.at[:, pl.ds(pl.multiple_of(index * size, size), size)]


def rows_of(ref, index, size):
    return ref.at[pl.ds(pl.multiple_of(index * size, size), size), :]


def nt_dot(a, b):
    return lax.dot_general(a, b, ROWS_BY_ROWS, preferred_element_type=jnp.float32)


def tn_dot(a, b):
    return lax.dot_general(a, b, COLUMNS_BY_COLUMNS, preferred_element_type=jnp.float32)


ANY = pl.BlockSpec(memory_space=pl.ANY)
SMEM = pl.BlockSpec(memory_space=pltpu.SMEM)
VMEM = pl.BlockSpec(memory_space=pltpu.VMEM)


def tile_loop(count, tiles, tile_sems, where, compute):
    def write(step, slot):
        return pltpu.make_async_copy(tiles.at[slot], where(step), tile_sems.at[slot])

    @pl.loop(0, count)
    def _(step):
        slot = lax.rem(step, 2)

        @pl.when(step >= 2)
        def _():
            write(step, slot).wait()

        tiles[slot] = compute(step).astype(tiles.dtype)
        write(step, slot).start()

    for step in range(max(count - 2, 0), count):
        write(step, step % 2).wait()


def first_grads_kernel(starts_ref, active, *refs):
    count = len(refs) - 9
    pieces = refs[:count]
    rows_out, down_out, grad_buf, active_buf, tiles = refs[count:-4]
    piece_sems, load_sems, row_sems, tile_sems = refs[-4:]
    _, rows, half = grad_buf.shape
    blocks, _, block = active_buf.shape

    def piece_copy(slot, side):
        size = pieces[slot].shape[0]
        there = pl.ds(pl.multiple_of(starts_ref[slot], size), size)
        return pltpu.make_async_copy(
            pieces[slot].at[:, pl.ds(side * half, half)],
            grad_buf.at[side, there, :],
            piece_sems.at[slot, side],
        )

    def active_copy(index):
        return pltpu.make_async_copy(
            columns_of(active, index, block), active_buf.at[index], load_sems.at[index]
        )

    def row_copy(side):
        return pltpu.make_async_copy(
            grad_buf.at[side], rows_out.at[:, pl.ds(side * half, half)], row_sems.at[side]
        )

    active_copy(0).start()
    for side in range(2):
        for slot in range(count):
            piece_copy(slot, side).start()
    for index in range(1, blocks):
        active_copy(index).start()

    def compute(step):
        for index in range(blocks):
            pl.when(step == 2 * index)(active_copy(index).wait)
        for side in range(2):

            @pl.when(step == side)
            def _(side=side):
                for slot in range(count):
                    piece_copy(slot, side).wait()
                row_copy(side).start()

        return tn_dot(active_buf[lax.div(step, 2)], grad_buf[lax.rem(step, 2)])

    tile_loop(
        2 * blocks,
        tiles,
        tile_sems,
        lambda step: down_out.at[
            pl.ds(pl.multiple_of(lax.div(step, 2) * block, block), block),
            pl.ds(pl.multiple_of(lax.rem(step, 2) * half, half), half),
        ],
        compute,
    )
    for side in range(2):
        row_copy(side).wait()


def first_grads(pieces, active):
    low = jnp.bfloat16
    rows, hidden = active.shape
    depth = pieces[0][1].shape[1]
    half, block = depth // 2, min(512, hidden)
    count = len(pieces)
    starts = jnp.stack([jnp.asarray(start, jnp.int32) for start, _ in pieces])
    return whole_call(
        first_grads_kernel,
        [SMEM] + [ANY] * (1 + count),
        [ANY, ANY],
        [
            jax.ShapeDtypeStruct((rows, depth), low),
            jax.ShapeDtypeStruct((hidden, depth), low),
        ],
        [
            pltpu.VMEM((2, rows, half), low),
            pltpu.VMEM((hidden // block, rows, block), low),
            pltpu.VMEM((2, block, half), low),
            pltpu.SemaphoreType.DMA((count, 2)),
            pltpu.SemaphoreType.DMA((hidden // block,)),
            pltpu.SemaphoreType.DMA((2,)),
            pltpu.SemaphoreType.DMA((2,)),
        ],
    )(starts, active, *[piece for _, piece in pieces])


def feed_kernel(starts_ref, active, weight, *refs, places):
    cuts = refs[:-5]
    active_buf, weight_buf, out_buf, load_sems, cut_sems = refs[-5:]
    owners, halves = len(places), len(places[0])
    rows = active_buf.shape[0]
    half = weight_buf.shape[2]
    owner_rows = rows // owners
    piece = owner_rows // halves

    def weight_load(side):
        return pltpu.make_async_copy(
            weight.at[:, pl.ds(side * half, half)], weight_buf.at[side], load_sems.at[side]
        )

    def row_load(owner):
        here = pl.ds(pl.multiple_of(starts_ref[owner], owner_rows), owner_rows)
        return pltpu.make_async_copy(
            active.at[here, :], active_buf.at[here, :], load_sems.at[2 + owner]
        )

    weight_load(0).start()
    row_load(0).start()
    weight_load(1).start()
    for owner in range(1, owners):
        row_load(owner).start()

    def cut_copy(owner, part_of, side):
        return pltpu.make_async_copy(
            out_buf.at[side, pl.ds(owner * owner_rows + part_of * piece, piece), :],
            cuts[places[owner][part_of][0]].at[
                pl.ds(places[owner][part_of][1], piece),
                pl.ds(pl.multiple_of(side * half, half), half),
            ],
            cut_sems.at[side, owner * halves + part_of],
        )

    @pl.loop(0, 2 * owners)
    def _(step):
        owner, side = lax.div(step, 2), lax.rem(step, 2)
        for own in range(owners):
            pl.when(step == 2 * own)(row_load(own).wait)
        for own in range(2):
            pl.when(step == own)(weight_load(own).wait)
        here = pl.ds(pl.multiple_of(starts_ref[owner], owner_rows), owner_rows)
        there = pl.ds(pl.multiple_of(owner * owner_rows, owner_rows), owner_rows)
        out_buf[side, there, :] = jnp.dot(
            active_buf[here, :], weight_buf[side], preferred_element_type=jnp.float32
        ).astype(out_buf.dtype)
        for own in range(owners):

            @pl.when(owner == own)
            def _(own=own):
                for part_of in range(halves):
                    cut_copy(own, part_of, side).start()

    for side in range(2):
        for own in range(owners):
            for part_of in range(halves):
                cut_copy(own, part_of, side).wait()


def feed_rows(active, weight):
    low = jnp.bfloat16
    rows, hidden = active.shape
    depth = weight.shape[1]
    half = depth // 2
    starts, places, sizes = owner_cuts(rows)
    owners, halves = len(places), len(places[0])
    return tuple(
        whole_call(
            functools.partial(feed_kernel, places=places),
            [SMEM] + [ANY] * 2,
            [ANY] * len(sizes),
            [jax.ShapeDtypeStruct((size, depth), low) for size in sizes],
            [
                pltpu.VMEM((rows, hidden), low),
                pltpu.VMEM((2, hidden, half), low),
                pltpu.VMEM((2, rows, half), low),
                pltpu.SemaphoreType.DMA((2 + owners,)),
                pltpu.SemaphoreType.DMA((2, owners * halves)),
            ],
        )(starts, active, weight)
    )


def hidden_grads_kernel(grad_rows, weight, slope, x, hidden_out, up_out, sum_out, *refs):
    grad_buf, weight_buf, slope_buf, x_buf, hidden_buf, tiles = refs[:6]
    load_sems, slope_sems, hidden_sems, tile_sems = refs[6:]
    rows = grad_buf.shape[0]
    parts, _, part = hidden_buf.shape
    x_blocks, _, x_block = x_buf.shape
    chunk = slope_buf.shape[1]
    chunks = rows // chunk

    def load(source, target, index):
        return pltpu.make_async_copy(source, target, load_sems.at[index])

    def grad_load(index):
        here = pl.ds(pl.multiple_of(index * chunk, chunk), chunk)
        return load(grad_rows.at[here, :], grad_buf.at[here, :], index)

    def weight_load(index):
        here = pl.ds(pl.multiple_of(index * part, part), part)
        return load(weight.at[here, :], weight_buf.at[here, :], chunks + index)

    x_loads = [
        load(columns_of(x, i, x_block), x_buf.at[i], chunks + parts + i) for i in range(x_blocks)
    ]

    def slope_copy(step, slot):
        place = (
            pl.ds(pl.multiple_of(lax.rem(step, chunks) * chunk, chunk), chunk),
            pl.ds(pl.multiple_of(lax.div(step, chunks) * part, part), part),
        )
        return pltpu.make_async_copy(slope.at[place], slope_buf.at[slot], slope_sems.at[slot])

    def hidden_copy(index):
        return pltpu.make_async_copy(
            hidden_buf.at[index],
            hidden_out.at[:, pl.ds(index * part, part)],
            hidden_sems.at[index],
        )

    weight_load(0).start()
    grad_load(0).start()
    slope_copy(0, 0).start()
    for index in range(1, chunks):
        grad_load(index).start()
    for index in range(1, parts):
        weight_load(index).start()
    for copy in x_loads:
        copy.start()
    sum_out[...] = jnp.zeros_like(sum_out)

    @pl.loop(0, parts * chunks)
    def _(step):
        slot = lax.rem(step, 2)
        index = lax.div(step, chunks)

        @pl.when(step + 1 < parts * chunks)
        def _():
            slope_copy(step + 1, 1 - slot).start()

        @pl.when(lax.rem(step, chunks) == 0)
        def _():
            weight_load(index).wait()

        @pl.when(index == 0)
        def _():
            grad_load(step).wait()

        slope_copy(step, slot).wait()
        here = pl.ds(pl.multiple_of(lax.rem(step, chunks) * chunk, chunk), chunk)
        units = pl.ds(pl.multiple_of(index * part, part), part)
        product = nt_dot(grad_buf[here, :], weight_buf[units, :])
        low = (product * wide(slope_buf[slot])).astype(hidden_buf.dtype)
        hidden_buf[index, here, :] = low
        sum_out[index] += jnp.sum(wide(low), axis=0, keepdims=True)

    for index in range(parts):
        hidden_copy(index).start()
    for copy in x_loads:
        copy.wait()
    tile_loop(
        x_blocks * parts,
        tiles,
        tile_sems,
        lambda step: up_out.at[
            pl.ds(pl.multiple_of(lax.div(step, parts) * x_block, x_block), x_block),
            pl.ds(pl.multiple_of(lax.rem(step, parts) * part, part), part),
        ],
        lambda step: tn_dot(x_buf[lax.div(step, parts)], hidden_buf[lax.rem(step, parts)]),
    )
    for index in range(parts):
        hidden_copy(index).wait()


def hidden_grads(grad_rows, weight, slope, x):
    low = jnp.bfloat16
    rows, depth = grad_rows.shape
    hidden = weight.shape[0]
    part, x_block, chunk = min(1024, hidden), min(512, depth), min(512, rows)
    return whole_call(
        hidden_grads_kernel,
        [ANY] * 4,
        [ANY, ANY, VMEM],
        [
            jax.ShapeDtypeStruct((rows, hidden), low),
            jax.ShapeDtypeStruct((depth, hidden), low),
            jax.ShapeDtypeStruct((hidden // part, 1, part), jnp.float32),
        ],
        [
            pltpu.VMEM((rows, depth), low),
            pltpu.VMEM((hidden, depth), low),
            pltpu.VMEM((2, chunk, part), low),
            pltpu.VMEM((depth // x_block, rows, x_block), low),
            pltpu.VMEM((hidden // part, rows, part), low),
            pltpu.VMEM((2, x_block, part), low),
            pltpu.SemaphoreType.DMA((rows // chunk + hidden // part + depth // x_block,)),
            pltpu.SemaphoreType.DMA((2,)),
            pltpu.SemaphoreType.DMA((hidden // part,)),
            pltpu.SemaphoreType.DMA((2,)),
        ],
    )(grad_rows, weight, slope, x)


def last_grads_kernel(
    x, joined, grad_rows, mixed, out, x_buf, joined_buf, tiles, x_sems, joined_sems, tile_sems
):
    blocks = x_buf.shape[0] // 2
    block = x_buf.shape[2]

    def x_load(index):
        source = x if index < blocks else grad_rows
        return pltpu.make_async_copy(
            columns_of(source, index % blocks, block), x_buf.at[index], x_sems.at[index]
        )

    def joined_load(slot):
        source = joined.at[slot] if slot < 3 else mixed
        return pltpu.make_async_copy(source, joined_buf.at[slot], joined_sems.at[slot])

    joined_load(0).start()
    for index in range(blocks):
        x_load(index).start()
    for slot in range(1, 4):
        joined_load(slot).start()
    for index in range(blocks, 2 * blocks):
        x_load(index).start()

    def compute(step):
        for slot in range(4):
            pl.when(step == slot * blocks)(joined_load(slot).wait)
        for index in range(blocks):
            pl.when(step == index)(x_load(index).wait)
            pl.when(step == 3 * blocks + index)(x_load(blocks + index).wait)
        slot = lax.div(step, blocks)
        index = lax.rem(step, blocks) + blocks * lax.div(slot, 3)
        return tn_dot(x_buf[index], joined_buf[slot])

    tile_loop(
        4 * blocks,
        tiles,
        tile_sems,
        lambda step: rows_of(out.at[lax.div(step, blocks)], lax.rem(step, blocks), block),
        compute,
    )


def last_grads(x, joined, grad_rows, mixed):
    low = jnp.bfloat16
    rows, depth = x.shape
    width = joined.shape[2]
    block = min(1024, depth)
    return whole_call(
        last_grads_kernel,
        [ANY] * 4,
        ANY,
        jax.ShapeDtypeStruct((4, depth, width), low),
        [
            pltpu.VMEM((2 * depth // block, rows, block), low),
            pltpu.VMEM((4, rows, width), low),
            pltpu.VMEM((2, block, width), low),
            pltpu.SemaphoreType.DMA((2 * depth // block,)),
            pltpu.SemaphoreType.DMA((4,)),
            pltpu.SemaphoreType.DMA((2,)),
        ],
    )(x, joined, grad_rows, mixed)


def normed_grads_kernel(
    starts_ref, joined, qkv, hidden, up, x, mean_ref, root_ref, gain_ref, shift_ref, *refs, places
):
    cuts = refs[:-8]
    joined_buf, qkv_buf, hidden_buf, up_buf, x_buf, out_buf, load_sems, cut_sems = refs[-8:]
    owners, halves = len(places), len(places[0])
    rows = hidden_buf.shape[0]
    owner_rows = rows // owners
    piece = owner_rows // halves
    columns = up_buf.shape[0]
    chunk = min(512, columns)
    chunks = columns // chunk

    def load(source, target, index):
        return pltpu.make_async_copy(source, target, load_sems.at[index])

    def row_loads(owner):
        here = pl.ds(pl.multiple_of(starts_ref[owner], owner_rows), owner_rows)
        at = 2 + owner * 3
        return (
            load(hidden.at[here, :], hidden_buf.at[here, :], at),
            load(joined.at[:, here, :], joined_buf.at[:, here, :], at + 1),
            load(x.at[here, :], x_buf.at[here, :], at + 2),
        )

    weights = [load(up, up_buf, 0), load(qkv, qkv_buf, 1)]
    weights[0].start()
    for copy in row_loads(0):
        copy.start()
    weights[1].start()
    for owner in range(1, owners):
        for copy in row_loads(owner):
            copy.start()
    gain_ref[...] = jnp.zeros_like(gain_ref)
    shift_ref[...] = jnp.zeros_like(shift_ref)
    for copy in weights:
        copy.wait()

    def cut_copy(owner, part_of):
        array, row = places[owner][part_of]
        return pltpu.make_async_copy(
            out_buf.at[pl.ds(owner * owner_rows + part_of * piece, piece), :],
            cuts[array].at[pl.ds(row, piece), :],
            cut_sems.at[owner * halves + part_of],
        )

    @pl.loop(0, owners)
    def _(owner):
        here = pl.ds(pl.multiple_of(starts_ref[owner], owner_rows), owner_rows)
        there = pl.ds(pl.multiple_of(owner * owner_rows, owner_rows), owner_rows)
        for copy in row_loads(owner):
            copy.wait()
        for index in range(chunks):
            mine = slice(index * chunk, (index + 1) * chunk)
            total = nt_dot(hidden_buf[here, :], up_buf[mine, :])
            for slot in range(3):
                total += nt_dot(joined_buf[slot, here, :], qkv_buf[slot, mine, :])
            out_buf[there, mine] = total.astype(out_buf.dtype)
            hat = (wide(x_buf[here, mine]) - mean_ref[here, :]) * root_ref[here, :]
            gain_ref[:, mine] += jnp.sum(total * hat, axis=0, keepdims=True)
            shift_ref[:, mine] += jnp.sum(total, axis=0, keepdims=True)
        for own in range(owners):

            @pl.when(owner == own)
            def _(own=own):
                for part_of in range(halves):
                    cut_copy(own, part_of).start()

    for own in range(owners):
        for part_of in range(halves):
            cut_copy(own, part_of).wait()


def normed_grads(joined, qkv, hidden, up, x, mean, root, first, last):
    low = jnp.bfloat16
    rows, units = hidden.shape
    width = joined.shape[2]
    columns = last - first
    starts, places, sizes = owner_cuts(rows)
    owners, halves = len(places), len(places[0])
    line = jax.ShapeDtypeStruct((1, columns), jnp.float32)

    def kernel(starts_ref, joined, qkv, hidden, up, x, *refs):
        mine = pl.ds(first, columns)
        normed_grads_kernel(
            starts_ref,
            joined,
            qkv.at[:, mine, :],
            hidden,
            up.at[mine, :],
            x.at[:, mine],
            *refs,
            places=places,
        )

    result = whole_call(
        kernel,
        [SMEM] + [ANY] * 5 + [VMEM] * 2,
        [VMEM, VMEM] + [ANY] * len(sizes),
        [line, line] + [jax.ShapeDtypeStruct((size, columns), low) for size in sizes],
        [
            pltpu.VMEM((3, rows, width), low),
            pltpu.VMEM((3, columns, width), low),
            pltpu.VMEM((rows, units), low),
            pltpu.VMEM((columns, units), low),
            pltpu.VMEM((rows, columns), low),
            pltpu.VMEM((rows, columns), low),
            pltpu.SemaphoreType.DMA((2 + 3 * owners,)),
            pltpu.SemaphoreType.DMA((owners * halves,)),
        ],
    )(starts, joined, qkv, hidden, up, x, mean, root)
    return result[0], result[1], tuple(result[2:])


def finish_kernel(*refs):
    mixed, dense = refs[:4], refs[4:9]
    token_ref, bias_ref = refs[9:11]
    last_first, last_second, first_near, second_near, low, high = refs[11:17]
    out_ref = refs[17]
    half = low.shape[0]
    far = dense[3].shape[0]
    total = jnp.dot(mixed[0][...], dense[0][...], preferred_element_type=jnp.float32)
    total += jnp.dot(mixed[1][...], dense[1][...], preferred_element_type=jnp.float32)
    total += jnp.dot(mixed[2][...], dense[2][...], preferred_element_type=jnp.float32)
    total += jnp.dot(mixed[3][:, :far], dense[3][...], preferred_element_type=jnp.float32)
    total += jnp.dot(mixed[3][:, far:], dense[4][...], preferred_element_type=jnp.float32)
    total += wide(token_ref[...]) + bias_ref[...]
    for here, parts in (
        (slice(0, half), (low, first_near, last_first)),
        (slice(half, 2 * half), (high, second_near, last_second)),
    ):
        feed = wide(parts[0][...]) + wide(parts[1][...]) + wide(parts[2][...])
        out_ref[here, :] = (total[here] + feed).astype(out_ref.dtype)


def finish_output(mixed_parts, dense_parts, tokens, bias, feed_parts):
    rows, depth = tokens.shape
    if len(feed_parts) == 1:
        attended = jnp.dot(mixed_parts[0], dense_parts[0], preferred_element_type=jnp.float32)
        return (wide(tokens) + attended + feed_parts[0] + bias).astype(tokens.dtype)
    columns = min(512, depth)

    def column_block(piece):
        return pl.BlockSpec((piece.shape[0], columns), lambda j: (0, j))

    return pl.pallas_call(
        finish_kernel,
        grid=(depth // columns,),
        in_specs=[pl.BlockSpec(piece.shape, lambda j: (0, 0)) for piece in mixed_parts]
        + [column_block(piece) for piece in dense_parts]
        + [column_block(tokens), pl.BlockSpec((1, columns), lambda j: (0, j))]
        + [column_block(piece) for piece in feed_parts[:2]]
        + [pl.BlockSpec((rows // 2, columns), lambda j: (1, j))] * 2
        + [column_block(piece) for piece in feed_parts[4:]],
        out_specs=column_block(tokens),
        out_shape=jax.ShapeDtypeStruct(tokens.shape, tokens.dtype),
        compiler_params=pltpu.CompilerParams(vmem_limit_bytes=VMEM_BYTES),
        cost_estimate=SHORT,
    )(*mixed_parts, *dense_parts, tokens, bias.reshape(1, depth), *feed_parts)


def token_grads_kernel(*refs, steps):
    left, right = refs[:6], refs[6:12]
    token_ref, grad_ref, mean_ref, root_ref, gain_ref, out_ref = refs[12:]
    split = left[4].shape[1]
    mean_own, root_own = mean_ref[...], root_ref[...]

    def rows_of_half(upper):
        scaled, hats = [], []
        for side, parts in enumerate((left, right)):
            columns = slice(side * split, (side + 1) * split)
            total = sum(wide(parts[at + upper][...]) for at in (4, 2, 0))
            scaled.append(total * gain_ref[:, columns])
            hats.append((wide(token_ref[:, columns]) - mean_own) * root_own)
        count = 2 * split
        mean = sum(jnp.sum(v, axis=-1, keepdims=True) for v in scaled) / count
        slant = sum(jnp.sum(v * h, axis=-1, keepdims=True) for v, h in zip(scaled, hats)) / count
        for side in range(2):
            columns = slice(side * split, (side + 1) * split)
            grad = root_own * (scaled[side] - mean - hats[side] * slant)
            out_ref[:, columns] = (wide(grad_ref[:, columns]) + grad).astype(out_ref.dtype)

    step = pl.program_id(0)
    pl.when(step < steps)(lambda: rows_of_half(0))
    pl.when(step >= steps)(lambda: rows_of_half(1))


def token_grads(left_parts, right_parts, tokens, cotangent, mean, root, gain):
    if len(left_parts) == 1:
        grad = jnp.concatenate([left_parts[0], right_parts[0]], axis=1)
        hat = (wide(tokens) - mean) * root
        scaled = grad * gain
        grad_input = root * (
            scaled
            - jnp.mean(scaled, axis=-1, keepdims=True)
            - hat * jnp.mean(scaled * hat, axis=-1, keepdims=True)
        )
        return (wide(cotangent) + grad_input).astype(tokens.dtype)
    half, split = left_parts[4].shape
    rows, depth = tokens.shape
    chunk = min(64, half)
    steps = half // chunk
    low_part = pl.BlockSpec((chunk, split), lambda i: (jnp.minimum(i, steps - 1), 0))
    high_part = pl.BlockSpec((chunk, split), lambda i: (jnp.maximum(i - steps, 0), 0))
    low_near = pl.BlockSpec((chunk, split), lambda i: (steps + jnp.minimum(i, steps - 1), 0))
    high_near = pl.BlockSpec((chunk, split), lambda i: (jnp.maximum(i, steps), 0))
    row_block = pl.BlockSpec((chunk, depth), lambda i: (i, 0))
    thin = pl.BlockSpec((chunk, 1), lambda i: (i, 0))
    return pl.pallas_call(
        functools.partial(token_grads_kernel, steps=steps),
        grid=(rows // chunk,),
        in_specs=[low_part, high_part, low_near, high_near, low_part, high_part] * 2
        + [row_block, row_block, thin, thin, pl.BlockSpec((1, depth), lambda i: (0, 0))],
        out_specs=row_block,
        out_shape=jax.ShapeDtypeStruct(tokens.shape, tokens.dtype),
        compiler_params=pltpu.CompilerParams(vmem_limit_bytes=VMEM_BYTES),
        cost_estimate=SHORT,
    )(*left_parts, *right_parts, tokens, cotangent, mean, root, gain.reshape(1, -1))


def attention_kernel(
    q_ref,
    k_ref,
    v_ref,
    g_ref,
    cos_ref,
    above_ref,
    below_ref,
    mixed_ref,
    grads_ref,
    sums_ref,
    keys_across,
    values_across,
    query_total,
    key_total,
    value_total,
    weight_buf,
    top_buf,
    out_buf,
    across_buf,
    *,
    block,
    block_count,
):
    step = pl.program_id(1)
    scale = HEAD_DIM**-0.5
    rate = scale * 1.4426950408889634

    @pl.when(step == 0)
    def _():
        keys_across[...] = k_ref[...].T
        values_across[...] = v_ref[...].T
        key_total[...] = jnp.zeros_like(key_total)
        value_total[...] = jnp.zeros_like(value_total)

    rows = pl.ds(pl.multiple_of(step * block, block), block)
    queries, grads = q_ref[rows, :], g_ref[rows, :]
    lane = lax.broadcasted_iota(jnp.int32, (block, PAIR), 1)
    own_lanes = [lane // HEAD_DIM == head for head in range(2)]
    query_heads = [jnp.where(own, queries, jnp.zeros_like(queries)) for own in own_lanes]
    grad_heads = [jnp.where(own, grads, jnp.zeros_like(grads)) for own in own_lanes]
    parts = [slice(head * HEAD_DIM, (head + 1) * HEAD_DIM) for head in range(2)]

    def weigh(there, index, first):
        keys = k_ref[there, :]
        score_heads = [
            lax.dot_general(keys, own, ROWS_BY_ROWS, preferred_element_type=jnp.float32)
            for own in query_heads
        ]
        for head in range(2):
            scores = score_heads[head]
            if first:
                key_pos = lax.broadcasted_iota(jnp.int32, (block, block), 0)
                query_pos = lax.broadcasted_iota(jnp.int32, (block, block), 1)
                scores = jnp.where(key_pos <= query_pos, scores, masked_score)
            top = jnp.max(scores, axis=0, keepdims=True) * rate
            if not first:
                before = top_buf[head, 0]
                top = jnp.maximum(top, before)
            weights = jnp.exp2(scores * rate - top)
            weight_buf[head, there, :] = weights
            top_buf[head, 2 + index] = top
            total = jnp.sum(weights, axis=0, keepdims=True)
            out = jnp.dot(
                values_across[parts[head], there],
                weights.astype(jnp.bfloat16),
                preferred_element_type=jnp.float32,
            )
            if not first:
                shrink = jnp.exp2(before - top)
                total += top_buf[head, 1] * shrink
                out += out_buf[parts[head], :] * shrink
            top_buf[head, 0] = top
            top_buf[head, 1] = total
            out_buf[parts[head], :] = out

    def over_blocks(act):
        act(rows, step, True)

        @pl.when(lax.rem(step, 2) == 1)
        def _():
            act(pl.ds(pl.multiple_of((step - 1) * block, block), block), step - 1, False)

        @pl.loop(0, lax.div(step, 2))
        def _(index):
            start = pl.multiple_of(index * 2 * block, 2 * block)
            act(pl.ds(start, 2 * block), 2 * index, False)

    over_blocks(weigh)

    grads_across = grads.T.astype(jnp.float32)
    inner, share = [], []
    for head in range(2):
        share.append(1.0 / top_buf[head, 1])
        out = out_buf[parts[head], :] * share[head]
        out_buf[parts[head], :] = out
        inner.append(jnp.sum(out * grads_across[parts[head]], axis=0, keepdims=True))
    mixed_ref[rows, :] = out_buf[...].T.astype(mixed_ref.dtype)

    def differentiate(there, index, first):
        values = v_ref[there, :]
        prob_heads = [
            lax.dot_general(values, own, ROWS_BY_ROWS, preferred_element_type=jnp.float32)
            for own in grad_heads
        ]
        value_parts, key_parts = [], []
        for head in range(2):
            factor = jnp.exp2(top_buf[head, 2 + index] - top_buf[head, 0]) * share[head]
            exact = weight_buf[head, there, :] * factor
            rounded = exact.astype(jnp.bfloat16)
            grad_scores = (exact * (prob_heads[head] - inner[head])).astype(jnp.bfloat16)
            value_parts.append(
                jnp.dot(rounded, grad_heads[head], preferred_element_type=jnp.float32)
            )
            key_parts.append(
                jnp.dot(grad_scores, query_heads[head], preferred_element_type=jnp.float32)
            )
            across = jnp.dot(
                keys_across[parts[head], there], grad_scores, preferred_element_type=jnp.float32
            )
            if first:
                across_buf[parts[head], :] = across
            else:
                across_buf[parts[head], :] += across
        value_total[there, :] += value_parts[0] + value_parts[1]
        key_total[there, :] += key_parts[0] + key_parts[1]

    over_blocks(differentiate)
    query_total[rows, :] = across_buf[...].T

    @pl.when(step == block_count - 1)
    def _():
        lanes = cos_ref[...], above_ref[...], below_ref[...]
        for slot, field in enumerate(
            (
                turn_back(query_total[...] * scale, *lanes),
                turn_back(key_total[...] * scale, *lanes),
                value_total[...],
            )
        ):
            low = field.astype(grads_ref.dtype)
            grads_ref[slot] = low
            sums_ref[slot] = jnp.sum(low.astype(jnp.float32), axis=0, keepdims=True)


def attention(joined, grad_mixed, lanes, first, last, earlier=None):
    rows, width = grad_mixed.shape
    block = min(512, LENGTH)
    pairs, block_count = width // PAIR, LENGTH // block
    row_block = pl.BlockSpec((LENGTH, PAIR), lambda p, i: (0, first + p))
    table = pl.BlockSpec((LENGTH, PAIR), lambda p, i: (0, 0))
    kept = () if earlier is None else tuple(earlier)
    kernel = functools.partial(attention_kernel, block=block, block_count=block_count)

    def body(*refs):
        kernel(*refs[:7], *refs[7 + len(kept) :])

    return pl.pallas_call(
        body,
        grid=(last - first, block_count),
        in_specs=[
            row_block,
            pl.BlockSpec((LENGTH, PAIR), lambda p, i: (0, pairs + first + p)),
            pl.BlockSpec((LENGTH, PAIR), lambda p, i: (0, 2 * pairs + first + p)),
            row_block,
            table,
            table,
            table,
        ]
        + [pl.BlockSpec(memory_space=pl.ANY)] * len(kept),
        out_specs=[
            row_block,
            pl.BlockSpec((3, LENGTH, PAIR), lambda p, i: (0, 0, first + p)),
            pl.BlockSpec((3, 1, PAIR), lambda p, i: (0, 0, first + p)),
        ],
        out_shape=[
            jax.ShapeDtypeStruct((rows, width), jnp.bfloat16),
            jax.ShapeDtypeStruct((3, rows, width), jnp.bfloat16),
            jax.ShapeDtypeStruct((3, 1, width), jnp.float32),
        ],
        scratch_shapes=[
            pltpu.VMEM((PAIR, LENGTH), jnp.bfloat16),
            pltpu.VMEM((PAIR, LENGTH), jnp.bfloat16),
            pltpu.VMEM((LENGTH, PAIR), jnp.float32),
            pltpu.VMEM((LENGTH, PAIR), jnp.float32),
            pltpu.VMEM((LENGTH, PAIR), jnp.float32),
            pltpu.VMEM((2, LENGTH, block), jnp.float32),
            pltpu.VMEM((2, 2 + block_count, 1, block), jnp.float32),
            pltpu.VMEM((PAIR, block), jnp.float32),
            pltpu.VMEM((PAIR, block), jnp.float32),
        ],
        input_output_aliases={7 + i: i for i in range(len(kept))},
        compiler_params=pltpu.CompilerParams(vmem_limit_bytes=VMEM_BYTES),
        cost_estimate=SHORT,
    )(joined, joined, joined, grad_mixed, *lanes, *kept)


def norm_kernel(starts_ref, gain_ref, shift_ref, following_ref, *refs):
    count = (len(refs) - 6) // 3
    pieces = refs[:count]
    raw, normed, mean_ref, root_ref, following_out = refs[count : count + 5]
    buffers = refs[count + 5 : 2 * count + 5]
    results = refs[2 * count + 5 : 3 * count + 5]
    sems = refs[-1]
    following_out[...] = following_ref[...]
    for slot in range(count):
        pltpu.make_async_copy(pieces[slot], buffers[slot], sems.at[0, slot]).start()
    writes = []
    for slot in range(count):
        buffer, result = buffers[slot], results[slot]
        size = buffer.shape[0]
        where = pl.ds(pl.multiple_of(starts_ref[slot], size), size)
        pltpu.make_async_copy(pieces[slot], buffer, sems.at[0, slot]).wait()
        write = pltpu.make_async_copy(buffer, raw.at[where, :], sems.at[1, slot])
        write.start()
        writes.append(write)
        chunk = min(128, size)

        @pl.loop(0, size // chunk)
        def _(step, buffer=buffer, result=result, slot=slot):
            here = pl.ds(pl.multiple_of(step * chunk, chunk), chunk)
            rows = buffer[here, :].astype(jnp.float32)
            mean = jnp.mean(rows, axis=-1, keepdims=True)
            centred = rows - mean
            variance = jnp.mean(centred * centred, axis=-1, keepdims=True)
            root = lax.rsqrt(variance + epsilon)
            out = centred * root * gain_ref[...] + shift_ref[...]
            result[here, :] = out.astype(result.dtype)
            there = pl.ds(pl.multiple_of(starts_ref[slot] + step * chunk, chunk), chunk)
            mean_ref[there, :] = mean
            root_ref[there, :] = root

        write = pltpu.make_async_copy(result, normed.at[where, :], sems.at[2, slot])
        write.start()
        writes.append(write)
    for write in writes:
        write.wait()


def norm_rows(pieces, gain, shift, following):
    depth = gain.shape[0]
    total = sum(piece.shape[0] for _, piece in pieces)
    count = len(pieces)
    low = jnp.bfloat16
    starts = jnp.stack([jnp.asarray(start, jnp.int32) for start, _ in pieces])
    any_space = pl.BlockSpec(memory_space=pl.ANY)
    vmem = pl.BlockSpec(memory_space=pltpu.VMEM)
    stage = [pltpu.VMEM(piece.shape, low) for _, piece in pieces]
    return pl.pallas_call(
        norm_kernel,
        in_specs=[pl.BlockSpec(memory_space=pltpu.SMEM), vmem, vmem, vmem] + [any_space] * count,
        out_specs=[any_space, any_space, vmem, vmem, vmem],
        out_shape=[
            jax.ShapeDtypeStruct((total, depth), low),
            jax.ShapeDtypeStruct((total, depth), low),
            jax.ShapeDtypeStruct((total, 1), jnp.float32),
            jax.ShapeDtypeStruct((total, 1), jnp.float32),
            jax.ShapeDtypeStruct(following.shape, following.dtype),
        ],
        scratch_shapes=stage + stage + [pltpu.SemaphoreType.DMA((3, count))],
        compiler_params=pltpu.CompilerParams(vmem_limit_bytes=VMEM_BYTES),
        cost_estimate=SHORT,
    )(
        starts,
        gain.reshape(1, depth),
        shift.reshape(1, depth),
        following,
        *[piece for _, piece in pieces],
    )


def on_device(
    tokens,
    norm_gain,
    norm_shift,
    weight_qkv,
    bias_qkv,
    weight_dense,
    weight_up,
    bias_up,
    weight_down,
    bias_out,
    cotangent,
):
    f32, low = jnp.float32, jnp.bfloat16
    depth = tokens.shape[1]
    local_rows = tokens.shape[0]
    tensor_index = lax.axis_index("tensor")

    full_up = lax.all_gather(weight_up, "dp", axis=0, tiled=True)
    token_parts = gather_start(tokens)
    lanes = lane_tables(LENGTH)
    out_part = jnp.sum(cotangent, axis=0, dtype=f32)
    lanes, out_part, token_parts = after((lanes, out_part, token_parts))
    full_qkv = lax.all_gather(
        after(jnp.transpose(weight_qkv, (1, 0, 2)), token_parts), "dp", axis=1, tiled=True
    )
    token_parts = gather_pass(token_parts)
    all_tokens, gathered, mean, root, sent = norm_rows(
        gathered_pieces(token_parts), norm_gain, norm_shift, cotangent
    )
    grad_parts = gather_start(sent)

    full_dense = lax.all_gather(after(weight_dense, gathered), "dp", axis=1, tiled=True)
    own_mean = lax.dynamic_slice_in_dim(mean, tensor_index * local_rows, local_rows, 0)
    own_root = lax.dynamic_slice_in_dim(root, tensor_index * local_rows, local_rows, 0)
    active, slope = hidden_rows(gathered, full_up, bias_up)
    own_mean, own_root, active = after((own_mean, own_root, active))
    grad_parts, active = after((grad_parts, active))
    full_down = lax.all_gather(after(weight_down, grad_parts), "dp", axis=1, tiled=True)
    grad_parts = gather_pass(grad_parts)
    joined = joined_rows(after(gathered, active, grad_parts[:3]), full_qkv, bias_qkv, lanes)
    grad_parts, joined = after((grad_parts, joined))
    grad_rows, grad_down = first_grads(gathered_pieces(grad_parts), active)
    grad_mixed = jnp.einsum(
        "td,kd->tk", grad_rows, after(full_dense, grad_down), preferred_element_type=f32
    ).astype(low)
    dense_parts = gather_start(after(full_dense, grad_mixed))
    grad_down_sum = lax.psum_scatter(grad_down, "dp", scatter_dimension=1, tiled=True)

    pairs = grad_mixed.shape[1] // PAIR
    part = attention(joined, grad_mixed, lanes, 0, pairs // 2)
    dense_parts, part = after((dense_parts, part))
    dense_parts = gather_pass(dense_parts)
    feed_cuts = feed_rows(after(active, part[0]), full_down)
    feed_cuts, dense_parts = after((feed_cuts, dense_parts))
    feed_parts = scatter_send(feed_cuts)
    grad_hidden, grad_up, bias_up_part = hidden_grads(
        after(grad_rows, feed_cuts), full_down, slope, gathered
    )
    grad_up, feed_parts = after((grad_up, feed_parts))
    feed_parts = scatter_fold(feed_parts)
    grad_up_sum = lax.psum_scatter(
        after(grad_up, grad_down_sum, feed_parts[:2]), "dp", scatter_dimension=0, tiled=True
    )
    feed_parts = scatter_pass(feed_parts)
    part = attention(after(joined, grad_up), grad_mixed, lanes, pairs // 2, pairs, part)
    mixed, grad_joined, bias_qkv_part = part
    mixed, grad_joined, feed_parts = after((mixed, grad_joined, feed_parts))

    mixed_parts = exchange_start(mixed)
    grad_last = last_grads(gathered, grad_joined, grad_rows, mixed)
    grad_last, mixed_parts = after((grad_last, mixed_parts))
    grad_last_sum = lax.psum_scatter(
        after(grad_last, grad_up_sum), "dp", scatter_dimension=1, tiled=True
    )
    half = depth // 2
    sources = full_qkv, grad_hidden, full_up, all_tokens, mean, root
    *left_sums, left_cuts = normed_grads(after(grad_joined, grad_last), *sources, 0, half)
    left_parts = scatter_send(left_cuts)
    *right_sums, right_cuts = normed_grads(after(grad_joined, left_cuts), *sources, half, depth)
    right_cuts, right_sums, left_parts = after((right_cuts, right_sums, left_parts))
    sums = jnp.concatenate(
        [left_sums[0][0], right_sums[0][0], left_sums[1][0], right_sums[1][0], out_part]
    ).reshape(-1, PAIR)
    right_parts = scatter_send(right_cuts)
    left_parts = scatter_pass(scatter_fold(left_parts))
    block_out = finish_output(
        after(mixed_parts, right_cuts), dense_parts, tokens, bias_out, feed_parts
    )
    small = jnp.concatenate(
        [sums.reshape(-1), bias_qkv_part.reshape(-1), bias_up_part.reshape(-1)]
    ).reshape(-1, PAIR)
    block_out, small = after((block_out, small))
    small = jnp.sum(lax.all_gather(small, "dp", axis=0), axis=0)
    block_out, right_parts, left_parts, small = after(
        (block_out, right_parts, left_parts, small)
    )
    right_parts = scatter_fold(right_parts)
    right_parts, small, grad_up_sum, grad_down_sum = after(
        (right_parts, small, grad_up_sum, grad_down_sum)
    )
    right_parts = scatter_pass(right_parts)
    small = small.reshape(-1)
    over_all = exchange_sum(small[: 3 * depth].reshape(-1, PAIR), "tensor")
    grad_gain, grad_shift, grad_bias_out = over_all.reshape(3, depth)
    bias_size = bias_qkv.size
    grad_bias_qkv = small[3 * depth : 3 * depth + bias_size].reshape(bias_qkv.shape)
    grad_bias_up = small[3 * depth + bias_size :]
    last = jnp.transpose(grad_last_sum, (1, 0, 2)).astype(f32)
    ready = grad_up_sum.astype(f32), grad_down_sum.astype(f32), last
    ready, left_parts = after((ready, left_parts))
    grad_up_sum, grad_down_sum, last = ready
    grad_tokens = token_grads(
        left_parts, right_parts, tokens, cotangent, own_mean, own_root, norm_gain
    )
    return (
        block_out,
        grad_tokens,
        grad_gain,
        grad_shift,
        last[:, :3],
        grad_bias_qkv,
        jnp.transpose(last[:, 3]),
        grad_up_sum,
        grad_bias_up,
        grad_down_sum,
        grad_bias_out,
    )


def solution(mesh):
    in_specs = (
        P(("dp", "tensor"), None),
        P(),
        P(),
        P("dp", None, "tensor"),
        P(None, "tensor"),
        P("tensor", "dp"),
        P("dp", "tensor"),
        P("tensor"),
        P("tensor", "dp"),
        P(),
        P(("dp", "tensor"), None),
    )
    out_specs = (
        P(("dp", "tensor"), None),
        P(("dp", "tensor"), None),
        P(),
        P(),
        P("dp", None, "tensor"),
        P(None, "tensor"),
        P("tensor", "dp"),
        P("dp", "tensor"),
        P("tensor"),
        P("tensor", "dp"),
        P(),
    )
    return jax.shard_map(
        on_device, mesh=mesh, in_specs=in_specs, out_specs=out_specs, check_vma=False
    )
```

```python
import functools

import jax
import jax.numpy as jnp
from jax import lax
from jax.experimental import pallas as pl
from jax.experimental.pallas import tpu as pltpu
from jax.sharding import PartitionSpec as P

HEAD_DIM = 64
ROT = 32
LENGTH = 2048
PAIR = 2 * HEAD_DIM

epsilon = 1e-05
masked_score = -1e30
MIB = 1024 * 1024
VMEM_BYTES = 64 * MIB - 256 * 1024
ROWS_BY_ROWS = (((1,), (1,)), ((), ()))
COLUMNS_BY_COLUMNS = (((0,), (0,)), ((), ()))


SHORT = pl.CostEstimate(flops=1, bytes_accessed=1, transcendentals=0)


def after(value, *earlier):
    return lax.optimization_barrier((value,) + earlier)[0]


def swap(value, axis, bit):
    count = lax.axis_size(axis)
    return lax.ppermute(value, axis, [(i, i ^ bit) for i in range(count)])


def gather_start(block):
    if lax.axis_size("tensor") != 4:
        return (lax.all_gather(block, "tensor", axis=0, tiled=True),)
    return block, swap(block, "tensor", 1), swap(block, "tensor", 2)


def halves_kernel(one_ref, two_ref, low_ref, high_ref):
    half = one_ref.shape[0] // 2
    low_ref[...] = one_ref[:half, :]
    high_ref[...] = two_ref[half:, :]


def gather_pass(parts):
    if len(parts) == 1:
        return parts
    block, one, two = parts
    rows, depth = block.shape
    half = jax.ShapeDtypeStruct((rows // 2, depth), block.dtype)
    low, high = pl.pallas_call(
        halves_kernel,
        out_shape=[half, half],
        compiler_params=pltpu.CompilerParams(vmem_limit_bytes=VMEM_BYTES),
        cost_estimate=SHORT,
    )(one, two)
    return block, one, two, swap(low, "tensor", 2), swap(high, "tensor", 1)


def gathered_pieces(parts):
    if len(parts) == 1:
        return [(0, parts[0])]
    block, one, two, low, high = parts
    rows = block.shape[0]
    me = lax.axis_index("tensor")
    return [
        (me * rows, block),
        ((me ^ 1) * rows, one),
        ((me ^ 2) * rows, two),
        ((me ^ 3) * rows, low),
        ((me ^ 3) * rows + rows // 2, high),
    ]


def wide(piece):
    return piece.astype(jnp.float32)


def owner_cuts(total):
    count = lax.axis_size("tensor")
    rows = total // count
    me = lax.axis_index("tensor")
    if count == 4:
        order = [me ^ bit for bit in (3, 1, 2, 0)]
        half = rows // 2
        places = (((0, 0), (1, 0)), ((0, half), (3, 0)), ((2, 0), (1, half)), ((4, 0), (5, 0)))
        sizes = (rows, rows, half, half, half, half)
    else:
        order = list(range(count))
        places = tuple(((owner, 0),) for owner in range(count))
        sizes = (rows,) * count
    starts = jnp.stack([jnp.asarray(owner * rows, jnp.int32) for owner in order])
    return starts, places, sizes


def scatter_send(cuts):
    if lax.axis_size("tensor") != 4:
        whole = wide(jnp.concatenate(cuts))
        return (lax.psum_scatter(whole, "tensor", scatter_dimension=0, tiled=True),)
    for_one, for_two, two_low, one_high, low, high = cuts
    return swap(for_one, "tensor", 1), swap(for_two, "tensor", 2), two_low, one_high, low, high


def fold_kernel(a_ref, b_ref, c_ref, d_ref, ab_ref, cd_ref):
    half = a_ref.shape[0]
    ab_ref[...] = (wide(a_ref[...]) + wide(b_ref[:half, :])).astype(ab_ref.dtype)
    cd_ref[...] = (wide(c_ref[...]) + wide(d_ref[:half, :])).astype(cd_ref.dtype)


def scatter_fold(parts):
    if len(parts) == 1:
        return parts
    first, second, two_low, one_high, low, high = parts
    shape = jax.ShapeDtypeStruct(low.shape, low.dtype)
    forward = pl.pallas_call(
        fold_kernel,
        out_shape=[shape, shape],
        compiler_params=pltpu.CompilerParams(vmem_limit_bytes=VMEM_BYTES),
        cost_estimate=SHORT,
    )(two_low, first, one_high, second)
    return (*forward, first, second, low, high)


def scatter_pass(parts):
    if len(parts) == 1:
        return parts
    two_low, one_high, first_near, second_near, low, high = parts
    return (
        swap(two_low, "tensor", 2),
        swap(one_high, "tensor", 1),
        first_near,
        second_near,
        low,
        high,
    )


def exchange_start(columns):
    if lax.axis_size("tensor") != 4:
        return (lax.all_to_all(columns, "tensor", 0, 1, tiled=True),)
    rows = columns.shape[0] // 4
    me = lax.axis_index("tensor")
    pieces = []
    for bit in range(4):
        piece = lax.dynamic_slice_in_dim(columns, (me ^ bit) * rows, rows, 0)
        pieces.append(swap(piece, "tensor", bit) if bit else piece)
    return tuple(pieces)


def exchange_sum(value, axis, step=1):
    parts = [value]
    for bit in range(step, lax.axis_size(axis), step):
        parts.append(swap(value, axis, bit))
    return functools.reduce(lambda a, b: a + b, parts)


def lane_tables(row_total):
    half_rot = ROT // 2
    positions = (jnp.arange(row_total, dtype=jnp.int32) % LENGTH).astype(jnp.float32)
    inverse = 10000.0 ** (-(2.0 * jnp.arange(half_rot, dtype=jnp.float32)) / ROT)
    angles = positions[:, None] * inverse[None, :]
    cosine, sine = jnp.cos(angles), jnp.sin(angles)
    ones = jnp.ones((row_total, HEAD_DIM - ROT), jnp.float32)
    zeros = jnp.zeros((row_total, half_rot), jnp.float32)
    rest = jnp.zeros((row_total, HEAD_DIM - ROT), jnp.float32)
    cos_lanes = jnp.concatenate([cosine, cosine, ones] * 2, axis=1)
    from_above = jnp.concatenate([-sine, zeros, rest] * 2, axis=1)
    from_below = jnp.concatenate([zeros, sine, rest] * 2, axis=1)
    return cos_lanes, from_above, from_below


def turn(field, cos_lanes, from_above, from_below):
    half_rot = ROT // 2
    above = pltpu.roll(field, PAIR - half_rot, 1)
    below = pltpu.roll(field, half_rot, 1)
    return field * cos_lanes + above * from_above + below * from_below


def turn_back(field, cos_lanes, from_above, from_below):
    half_rot = ROT // 2
    above = pltpu.roll(field, PAIR - half_rot, 1)
    below = pltpu.roll(field, half_rot, 1)
    return field * cos_lanes - above * from_above - below * from_below


def joined_kernel(x_ref, w_ref, bias_ref, cos_ref, above_ref, below_ref, out_ref):
    width = out_ref.shape[1]
    chunk = min(256, width)
    slot = pl.program_id(0)

    def product(start):
        columns = slice(start, start + chunk)
        part = jnp.dot(x_ref[...], w_ref[0, :, columns], preferred_element_type=jnp.float32)
        return part + bias_ref[0, :, columns]

    @pl.when(slot < 2)
    def _():
        for start in range(0, width, chunk):
            part = product(start)
            for shift in range(0, chunk, PAIR):
                lanes = part[:, shift : shift + PAIR]
                turned = turn(lanes, cos_ref[...], above_ref[...], below_ref[...])
                columns = slice(start + shift, start + shift + PAIR)
                out_ref[:, columns] = turned.astype(out_ref.dtype)

    @pl.when(slot == 2)
    def _():
        for start in range(0, width, chunk):
            out_ref[:, start : start + chunk] = product(start).astype(out_ref.dtype)


def joined_rows(x, w, bias, lanes):
    rows, depth = x.shape
    width = w.shape[2]
    block = min(1024, rows)
    return pl.pallas_call(
        joined_kernel,
        grid=(3, rows // block),
        in_specs=[
            pl.BlockSpec((block, depth), lambda j, i: (i, 0)),
            pl.BlockSpec((1, depth, width), lambda j, i: (j, 0, 0)),
            pl.BlockSpec((1, 1, width), lambda j, i: (j, 0, 0)),
        ]
        + [pl.BlockSpec((block, PAIR), lambda j, i: (i, 0))] * 3,
        out_specs=pl.BlockSpec((block, width), lambda j, i: (i, j)),
        out_shape=jax.ShapeDtypeStruct((rows, 3 * width), jnp.bfloat16),
        compiler_params=pltpu.CompilerParams(vmem_limit_bytes=VMEM_BYTES),
        cost_estimate=SHORT,
    )(x, w, bias.reshape(3, 1, width), *lanes)


def hidden_kernel(x_ref, w_ref, bias_ref, active_ref, slope_ref):
    hidden = jnp.dot(x_ref[...], w_ref[...], preferred_element_type=jnp.float32) + bias_ref[...]
    scale = (2.0 / jnp.pi) ** 0.5
    square = hidden * hidden
    inner = scale * hidden * (1.0 + 0.044715 * square)
    bent = jnp.tanh(inner)
    half = 0.5 * (1.0 + bent)
    active_ref[...] = (hidden * half).astype(active_ref.dtype)
    growth = scale * (1.0 + (3.0 * 0.044715) * square)
    slope = half + 0.5 * hidden * (1.0 - bent * bent) * growth
    slope_ref[...] = slope.astype(slope_ref.dtype)


def hidden_rows(x, w, bias):
    rows, depth = x.shape
    width = w.shape[1]
    block, columns = min(1024, rows), min(1024, width)
    return pl.pallas_call(
        hidden_kernel,
        grid=(width // columns, rows // block),
        in_specs=[
            pl.BlockSpec((block, depth), lambda j, i: (i, 0)),
            pl.BlockSpec((depth, columns), lambda j, i: (0, j)),
            pl.BlockSpec((1, columns), lambda j, i: (0, j)),
        ],
        out_specs=[pl.BlockSpec((block, columns), lambda j, i: (i, j))] * 2,
        out_shape=[jax.ShapeDtypeStruct((rows, width), jnp.bfloat16)] * 2,
        compiler_params=pltpu.CompilerParams(vmem_limit_bytes=VMEM_BYTES),
        cost_estimate=SHORT,
    )(x, w, bias.reshape(1, width))


def whole_call(kernel, in_specs, out_specs, out_shape, scratch):
    return pl.pallas_call(
        kernel,
        in_specs=in_specs,
        out_specs=out_specs,
        out_shape=out_shape,
        scratch_shapes=scratch,
        compiler_params=pltpu.CompilerParams(vmem_limit_bytes=VMEM_BYTES),
        cost_estimate=SHORT,
    )


def columns_of(ref, index, size):
    return ref.at[:, pl.ds(pl.multiple_of(index * size, size), size)]


def rows_of(ref, index, size):
    return ref.at[pl.ds(pl.multiple_of(index * size, size), size), :]


def nt_dot(a, b):
    return lax.dot_general(a, b, ROWS_BY_ROWS, preferred_element_type=jnp.float32)


def tn_dot(a, b):
    return lax.dot_general(a, b, COLUMNS_BY_COLUMNS, preferred_element_type=jnp.float32)


ANY = pl.BlockSpec(memory_space=pl.ANY)
SMEM = pl.BlockSpec(memory_space=pltpu.SMEM)
VMEM = pl.BlockSpec(memory_space=pltpu.VMEM)


def tile_loop(count, tiles, tile_sems, where, compute):
    def write(step, slot):
        return pltpu.make_async_copy(tiles.at[slot], where(step), tile_sems.at[slot])

    @pl.loop(0, count)
    def _(step):
        slot = lax.rem(step, 2)

        @pl.when(step >= 2)
        def _():
            write(step, slot).wait()

        tiles[slot] = compute(step).astype(tiles.dtype)
        write(step, slot).start()

    for step in range(max(count - 2, 0), count):
        write(step, step % 2).wait()


def first_grads_kernel(starts_ref, active, *refs):
    count = len(refs) - 9
    pieces = refs[:count]
    rows_out, down_out, grad_buf, active_buf, tiles = refs[count:-4]
    piece_sems, load_sems, row_sems, tile_sems = refs[-4:]
    _, rows, half = grad_buf.shape
    blocks, _, block = active_buf.shape

    def piece_copy(slot, side):
        size = pieces[slot].shape[0]
        there = pl.ds(pl.multiple_of(starts_ref[slot], size), size)
        return pltpu.make_async_copy(
            pieces[slot].at[:, pl.ds(side * half, half)],
            grad_buf.at[side, there, :],
            piece_sems.at[slot, side],
        )

    def active_copy(index):
        return pltpu.make_async_copy(
            columns_of(active, index, block), active_buf.at[index], load_sems.at[index]
        )

    def row_copy(side):
        return pltpu.make_async_copy(
            grad_buf.at[side], rows_out.at[:, pl.ds(side * half, half)], row_sems.at[side]
        )

    active_copy(0).start()
    for side in range(2):
        for slot in range(count):
            piece_copy(slot, side).start()
    for index in range(1, blocks):
        active_copy(index).start()

    def compute(step):
        for index in range(blocks):
            pl.when(step == 2 * index)(active_copy(index).wait)
        for side in range(2):

            @pl.when(step == side)
            def _(side=side):
                for slot in range(count):
                    piece_copy(slot, side).wait()
                row_copy(side).start()

        return tn_dot(active_buf[lax.div(step, 2)], grad_buf[lax.rem(step, 2)])

    tile_loop(
        2 * blocks,
        tiles,
        tile_sems,
        lambda step: down_out.at[
            pl.ds(pl.multiple_of(lax.div(step, 2) * block, block), block),
            pl.ds(pl.multiple_of(lax.rem(step, 2) * half, half), half),
        ],
        compute,
    )
    for side in range(2):
        row_copy(side).wait()


def first_grads(pieces, active):
    low = jnp.bfloat16
    rows, hidden = active.shape
    depth = pieces[0][1].shape[1]
    half, block = depth // 2, min(512, hidden)
    count = len(pieces)
    starts = jnp.stack([jnp.asarray(start, jnp.int32) for start, _ in pieces])
    return whole_call(
        first_grads_kernel,
        [SMEM] + [ANY] * (1 + count),
        [ANY, ANY],
        [
            jax.ShapeDtypeStruct((rows, depth), low),
            jax.ShapeDtypeStruct((hidden, depth), low),
        ],
        [
            pltpu.VMEM((2, rows, half), low),
            pltpu.VMEM((hidden // block, rows, block), low),
            pltpu.VMEM((2, block, half), low),
            pltpu.SemaphoreType.DMA((count, 2)),
            pltpu.SemaphoreType.DMA((hidden // block,)),
            pltpu.SemaphoreType.DMA((2,)),
            pltpu.SemaphoreType.DMA((2,)),
        ],
    )(starts, active, *[piece for _, piece in pieces])


def feed_kernel(starts_ref, active, weight, *refs, places):
    cuts = refs[:-5]
    active_buf, weight_buf, out_buf, load_sems, cut_sems = refs[-5:]
    owners, halves = len(places), len(places[0])
    rows = active_buf.shape[0]
    half = weight_buf.shape[2]
    owner_rows = rows // owners
    piece = owner_rows // halves

    def weight_load(side):
        return pltpu.make_async_copy(
            weight.at[:, pl.ds(side * half, half)], weight_buf.at[side], load_sems.at[side]
        )

    def row_load(owner):
        here = pl.ds(pl.multiple_of(starts_ref[owner], owner_rows), owner_rows)
        return pltpu.make_async_copy(
            active.at[here, :], active_buf.at[here, :], load_sems.at[2 + owner]
        )

    weight_load(0).start()
    row_load(0).start()
    weight_load(1).start()
    for owner in range(1, owners):
        row_load(owner).start()

    def cut_copy(owner, part_of, side):
        return pltpu.make_async_copy(
            out_buf.at[side, pl.ds(owner * owner_rows + part_of * piece, piece), :],
            cuts[places[owner][part_of][0]].at[
                pl.ds(places[owner][part_of][1], piece),
                pl.ds(pl.multiple_of(side * half, half), half),
            ],
            cut_sems.at[side, owner * halves + part_of],
        )

    @pl.loop(0, 2 * owners)
    def _(step):
        owner, side = lax.div(step, 2), lax.rem(step, 2)
        for own in range(owners):
            pl.when(step == 2 * own)(row_load(own).wait)
        for own in range(2):
            pl.when(step == own)(weight_load(own).wait)
        here = pl.ds(pl.multiple_of(starts_ref[owner], owner_rows), owner_rows)
        there = pl.ds(pl.multiple_of(owner * owner_rows, owner_rows), owner_rows)
        out_buf[side, there, :] = jnp.dot(
            active_buf[here, :], weight_buf[side], preferred_element_type=jnp.float32
        ).astype(out_buf.dtype)
        for own in range(owners):

            @pl.when(owner == own)
            def _(own=own):
                for part_of in range(halves):
                    cut_copy(own, part_of, side).start()

    for side in range(2):
        for own in range(owners):
            for part_of in range(halves):
                cut_copy(own, part_of, side).wait()


def feed_rows(active, weight):
    low = jnp.bfloat16
    rows, hidden = active.shape
    depth = weight.shape[1]
    half = depth // 2
    starts, places, sizes = owner_cuts(rows)
    owners, halves = len(places), len(places[0])
    return tuple(
        whole_call(
            functools.partial(feed_kernel, places=places),
            [SMEM] + [ANY] * 2,
            [ANY] * len(sizes),
            [jax.ShapeDtypeStruct((size, depth), low) for size in sizes],
            [
                pltpu.VMEM((rows, hidden), low),
                pltpu.VMEM((2, hidden, half), low),
                pltpu.VMEM((2, rows, half), low),
                pltpu.SemaphoreType.DMA((2 + owners,)),
                pltpu.SemaphoreType.DMA((2, owners * halves)),
            ],
        )(starts, active, weight)
    )


def hidden_grads_kernel(grad_rows, weight, slope, x, hidden_out, up_out, sum_out, *refs):
    grad_buf, weight_buf, slope_buf, x_buf, hidden_buf, tiles = refs[:6]
    load_sems, slope_sems, hidden_sems, tile_sems = refs[6:]
    rows = grad_buf.shape[0]
    parts, _, part = hidden_buf.shape
    x_blocks, _, x_block = x_buf.shape
    chunk = slope_buf.shape[1]
    chunks = rows // chunk

    def load(source, target, index):
        return pltpu.make_async_copy(source, target, load_sems.at[index])

    def grad_load(index):
        here = pl.ds(pl.multiple_of(index * chunk, chunk), chunk)
        return load(grad_rows.at[here, :], grad_buf.at[here, :], index)

    def weight_load(index):
        here = pl.ds(pl.multiple_of(index * part, part), part)
        return load(weight.at[here, :], weight_buf.at[here, :], chunks + index)

    x_loads = [
        load(columns_of(x, i, x_block), x_buf.at[i], chunks + parts + i) for i in range(x_blocks)
    ]

    def slope_copy(step, slot):
        place = (
            pl.ds(pl.multiple_of(lax.rem(step, chunks) * chunk, chunk), chunk),
            pl.ds(pl.multiple_of(lax.div(step, chunks) * part, part), part),
        )
        return pltpu.make_async_copy(slope.at[place], slope_buf.at[slot], slope_sems.at[slot])

    def hidden_copy(index):
        return pltpu.make_async_copy(
            hidden_buf.at[index],
            hidden_out.at[:, pl.ds(index * part, part)],
            hidden_sems.at[index],
        )

    weight_load(0).start()
    grad_load(0).start()
    slope_copy(0, 0).start()
    for index in range(1, chunks):
        grad_load(index).start()
    for index in range(1, parts):
        weight_load(index).start()
    for copy in x_loads:
        copy.start()
    sum_out[...] = jnp.zeros_like(sum_out)

    @pl.loop(0, parts * chunks)
    def _(step):
        slot = lax.rem(step, 2)
        index = lax.div(step, chunks)

        @pl.when(step + 1 < parts * chunks)
        def _():
            slope_copy(step + 1, 1 - slot).start()

        @pl.when(lax.rem(step, chunks) == 0)
        def _():
            weight_load(index).wait()

        @pl.when(index == 0)
        def _():
            grad_load(step).wait()

        slope_copy(step, slot).wait()
        here = pl.ds(pl.multiple_of(lax.rem(step, chunks) * chunk, chunk), chunk)
        units = pl.ds(pl.multiple_of(index * part, part), part)
        product = nt_dot(grad_buf[here, :], weight_buf[units, :])
        low = (product * wide(slope_buf[slot])).astype(hidden_buf.dtype)
        hidden_buf[index, here, :] = low
        sum_out[index] += jnp.sum(wide(low), axis=0, keepdims=True)

    for index in range(parts):
        hidden_copy(index).start()
    for copy in x_loads:
        copy.wait()
    tile_loop(
        x_blocks * parts,
        tiles,
        tile_sems,
        lambda step: up_out.at[
            pl.ds(pl.multiple_of(lax.div(step, parts) * x_block, x_block), x_block),
            pl.ds(pl.multiple_of(lax.rem(step, parts) * part, part), part),
        ],
        lambda step: tn_dot(x_buf[lax.div(step, parts)], hidden_buf[lax.rem(step, parts)]),
    )
    for index in range(parts):
        hidden_copy(index).wait()


def hidden_grads(grad_rows, weight, slope, x):
    low = jnp.bfloat16
    rows, depth = grad_rows.shape
    hidden = weight.shape[0]
    part, x_block, chunk = min(1024, hidden), min(512, depth), min(512, rows)
    return whole_call(
        hidden_grads_kernel,
        [ANY] * 4,
        [ANY, ANY, VMEM],
        [
            jax.ShapeDtypeStruct((rows, hidden), low),
            jax.ShapeDtypeStruct((depth, hidden), low),
            jax.ShapeDtypeStruct((hidden // part, 1, part), jnp.float32),
        ],
        [
            pltpu.VMEM((rows, depth), low),
            pltpu.VMEM((hidden, depth), low),
            pltpu.VMEM((2, chunk, part), low),
            pltpu.VMEM((depth // x_block, rows, x_block), low),
            pltpu.VMEM((hidden // part, rows, part), low),
            pltpu.VMEM((2, x_block, part), low),
            pltpu.SemaphoreType.DMA((rows // chunk + hidden // part + depth // x_block,)),
            pltpu.SemaphoreType.DMA((2,)),
            pltpu.SemaphoreType.DMA((hidden // part,)),
            pltpu.SemaphoreType.DMA((2,)),
        ],
    )(grad_rows, weight, slope, x)


def last_grads_kernel(
    x, joined, grad_rows, mixed, out, x_buf, joined_buf, tiles, x_sems, joined_sems, tile_sems
):
    blocks = x_buf.shape[0] // 2
    block = x_buf.shape[2]

    def x_load(index):
        source = x if index < blocks else grad_rows
        return pltpu.make_async_copy(
            columns_of(source, index % blocks, block), x_buf.at[index], x_sems.at[index]
        )

    def joined_load(slot):
        source = joined.at[slot] if slot < 3 else mixed
        return pltpu.make_async_copy(source, joined_buf.at[slot], joined_sems.at[slot])

    joined_load(0).start()
    for index in range(blocks):
        x_load(index).start()
    for slot in range(1, 4):
        joined_load(slot).start()
    for index in range(blocks, 2 * blocks):
        x_load(index).start()

    def compute(step):
        for slot in range(4):
            pl.when(step == slot * blocks)(joined_load(slot).wait)
        for index in range(blocks):
            pl.when(step == index)(x_load(index).wait)
            pl.when(step == 3 * blocks + index)(x_load(blocks + index).wait)
        slot = lax.div(step, blocks)
        index = lax.rem(step, blocks) + blocks * lax.div(slot, 3)
        return tn_dot(x_buf[index], joined_buf[slot])

    tile_loop(
        4 * blocks,
        tiles,
        tile_sems,
        lambda step: rows_of(out.at[lax.div(step, blocks)], lax.rem(step, blocks), block),
        compute,
    )


def last_grads(x, joined, grad_rows, mixed):
    low = jnp.bfloat16
    rows, depth = x.shape
    width = joined.shape[2]
    block = min(1024, depth)
    return whole_call(
        last_grads_kernel,
        [ANY] * 4,
        ANY,
        jax.ShapeDtypeStruct((4, depth, width), low),
        [
            pltpu.VMEM((2 * depth // block, rows, block), low),
            pltpu.VMEM((4, rows, width), low),
            pltpu.VMEM((2, block, width), low),
            pltpu.SemaphoreType.DMA((2 * depth // block,)),
            pltpu.SemaphoreType.DMA((4,)),
            pltpu.SemaphoreType.DMA((2,)),
        ],
    )(x, joined, grad_rows, mixed)


def normed_grads_kernel(
    starts_ref, joined, qkv, hidden, up, x, mean_ref, root_ref, gain_ref, shift_ref, *refs, places
):
    cuts = refs[:-8]
    joined_buf, qkv_buf, hidden_buf, up_buf, x_buf, out_buf, load_sems, cut_sems = refs[-8:]
    owners, halves = len(places), len(places[0])
    rows = hidden_buf.shape[0]
    owner_rows = rows // owners
    piece = owner_rows // halves
    columns = up_buf.shape[0]
    chunk = min(512, columns)
    chunks = columns // chunk

    def load(source, target, index):
        return pltpu.make_async_copy(source, target, load_sems.at[index])

    def row_loads(owner):
        here = pl.ds(pl.multiple_of(starts_ref[owner], owner_rows), owner_rows)
        at = 2 + owner * 3
        return (
            load(hidden.at[here, :], hidden_buf.at[here, :], at),
            load(joined.at[:, here, :], joined_buf.at[:, here, :], at + 1),
            load(x.at[here, :], x_buf.at[here, :], at + 2),
        )

    weights = [load(up, up_buf, 0), load(qkv, qkv_buf, 1)]
    weights[0].start()
    for copy in row_loads(0):
        copy.start()
    weights[1].start()
    for owner in range(1, owners):
        for copy in row_loads(owner):
            copy.start()
    gain_ref[...] = jnp.zeros_like(gain_ref)
    shift_ref[...] = jnp.zeros_like(shift_ref)
    for copy in weights:
        copy.wait()

    def cut_copy(owner, part_of):
        array, row = places[owner][part_of]
        return pltpu.make_async_copy(
            out_buf.at[pl.ds(owner * owner_rows + part_of * piece, piece), :],
            cuts[array].at[pl.ds(row, piece), :],
            cut_sems.at[owner * halves + part_of],
        )

    @pl.loop(0, owners)
    def _(owner):
        here = pl.ds(pl.multiple_of(starts_ref[owner], owner_rows), owner_rows)
        there = pl.ds(pl.multiple_of(owner * owner_rows, owner_rows), owner_rows)
        for copy in row_loads(owner):
            copy.wait()
        for index in range(chunks):
            mine = slice(index * chunk, (index + 1) * chunk)
            total = nt_dot(hidden_buf[here, :], up_buf[mine, :])
            for slot in range(3):
                total += nt_dot(joined_buf[slot, here, :], qkv_buf[slot, mine, :])
            out_buf[there, mine] = total.astype(out_buf.dtype)
            hat = (wide(x_buf[here, mine]) - mean_ref[here, :]) * root_ref[here, :]
            gain_ref[:, mine] += jnp.sum(total * hat, axis=0, keepdims=True)
            shift_ref[:, mine] += jnp.sum(total, axis=0, keepdims=True)
        for own in range(owners):

            @pl.when(owner == own)
            def _(own=own):
                for part_of in range(halves):
                    cut_copy(own, part_of).start()

    for own in range(owners):
        for part_of in range(halves):
            cut_copy(own, part_of).wait()


def normed_grads(joined, qkv, hidden, up, x, mean, root, first, last):
    low = jnp.bfloat16
    rows, units = hidden.shape
    width = joined.shape[2]
    columns = last - first
    starts, places, sizes = owner_cuts(rows)
    owners, halves = len(places), len(places[0])
    line = jax.ShapeDtypeStruct((1, columns), jnp.float32)

    def kernel(starts_ref, joined, qkv, hidden, up, x, *refs):
        mine = pl.ds(first, columns)
        normed_grads_kernel(
            starts_ref,
            joined,
            qkv.at[:, mine, :],
            hidden,
            up.at[mine, :],
            x.at[:, mine],
            *refs,
            places=places,
        )

    result = whole_call(
        kernel,
        [SMEM] + [ANY] * 5 + [VMEM] * 2,
        [VMEM, VMEM] + [ANY] * len(sizes),
        [line, line] + [jax.ShapeDtypeStruct((size, columns), low) for size in sizes],
        [
            pltpu.VMEM((3, rows, width), low),
            pltpu.VMEM((3, columns, width), low),
            pltpu.VMEM((rows, units), low),
            pltpu.VMEM((columns, units), low),
            pltpu.VMEM((rows, columns), low),
            pltpu.VMEM((rows, columns), low),
            pltpu.SemaphoreType.DMA((2 + 3 * owners,)),
            pltpu.SemaphoreType.DMA((owners * halves,)),
        ],
    )(starts, joined, qkv, hidden, up, x, mean, root)
    return result[0], result[1], tuple(result[2:])


def finish_kernel(*refs):
    mixed, dense = refs[:4], refs[4:9]
    token_ref, bias_ref = refs[9:11]
    last_first, last_second, first_near, second_near, low, high = refs[11:17]
    out_ref = refs[17]
    half = low.shape[0]
    far = dense[3].shape[0]
    total = jnp.dot(mixed[0][...], dense[0][...], preferred_element_type=jnp.float32)
    total += jnp.dot(mixed[1][...], dense[1][...], preferred_element_type=jnp.float32)
    total += jnp.dot(mixed[2][...], dense[2][...], preferred_element_type=jnp.float32)
    total += jnp.dot(mixed[3][:, :far], dense[3][...], preferred_element_type=jnp.float32)
    total += jnp.dot(mixed[3][:, far:], dense[4][...], preferred_element_type=jnp.float32)
    total += wide(token_ref[...]) + bias_ref[...]
    for here, parts in (
        (slice(0, half), (low, first_near, last_first)),
        (slice(half, 2 * half), (high, second_near, last_second)),
    ):
        feed = wide(parts[0][...]) + wide(parts[1][...]) + wide(parts[2][...])
        out_ref[here, :] = (total[here] + feed).astype(out_ref.dtype)


def finish_output(mixed_parts, dense_parts, tokens, bias, feed_parts):
    rows, depth = tokens.shape
    if len(feed_parts) == 1:
        attended = jnp.dot(mixed_parts[0], dense_parts[0], preferred_element_type=jnp.float32)
        return (wide(tokens) + attended + feed_parts[0] + bias).astype(tokens.dtype)
    columns = min(512, depth)

    def column_block(piece):
        return pl.BlockSpec((piece.shape[0], columns), lambda j: (0, j))

    return pl.pallas_call(
        finish_kernel,
        grid=(depth // columns,),
        in_specs=[pl.BlockSpec(piece.shape, lambda j: (0, 0)) for piece in mixed_parts]
        + [column_block(piece) for piece in dense_parts]
        + [column_block(tokens), pl.BlockSpec((1, columns), lambda j: (0, j))]
        + [column_block(piece) for piece in feed_parts[:2]]
        + [pl.BlockSpec((rows // 2, columns), lambda j: (1, j))] * 2
        + [column_block(piece) for piece in feed_parts[4:]],
        out_specs=column_block(tokens),
        out_shape=jax.ShapeDtypeStruct(tokens.shape, tokens.dtype),
        compiler_params=pltpu.CompilerParams(vmem_limit_bytes=VMEM_BYTES),
        cost_estimate=SHORT,
    )(*mixed_parts, *dense_parts, tokens, bias.reshape(1, depth), *feed_parts)


def token_grads_kernel(*refs, steps):
    left, right = refs[:6], refs[6:12]
    token_ref, grad_ref, mean_ref, root_ref, gain_ref, out_ref = refs[12:]
    split = left[4].shape[1]
    mean_own, root_own = mean_ref[...], root_ref[...]

    def rows_of_half(upper):
        scaled, hats = [], []
        for side, parts in enumerate((left, right)):
            columns = slice(side * split, (side + 1) * split)
            total = sum(wide(parts[at + upper][...]) for at in (4, 2, 0))
            scaled.append(total * gain_ref[:, columns])
            hats.append((wide(token_ref[:, columns]) - mean_own) * root_own)
        count = 2 * split
        mean = sum(jnp.sum(v, axis=-1, keepdims=True) for v in scaled) / count
        slant = sum(jnp.sum(v * h, axis=-1, keepdims=True) for v, h in zip(scaled, hats)) / count
        for side in range(2):
            columns = slice(side * split, (side + 1) * split)
            grad = root_own * (scaled[side] - mean - hats[side] * slant)
            out_ref[:, columns] = (wide(grad_ref[:, columns]) + grad).astype(out_ref.dtype)

    step = pl.program_id(0)
    pl.when(step < steps)(lambda: rows_of_half(0))
    pl.when(step >= steps)(lambda: rows_of_half(1))


def token_grads(left_parts, right_parts, tokens, cotangent, mean, root, gain):
    if len(left_parts) == 1:
        grad = jnp.concatenate([left_parts[0], right_parts[0]], axis=1)
        hat = (wide(tokens) - mean) * root
        scaled = grad * gain
        grad_input = root * (
            scaled
            - jnp.mean(scaled, axis=-1, keepdims=True)
            - hat * jnp.mean(scaled * hat, axis=-1, keepdims=True)
        )
        return (wide(cotangent) + grad_input).astype(tokens.dtype)
    half, split = left_parts[4].shape
    rows, depth = tokens.shape
    chunk = min(128, half)
    steps = half // chunk
    low_part = pl.BlockSpec((chunk, split), lambda i: (jnp.minimum(i, steps - 1), 0))
    high_part = pl.BlockSpec((chunk, split), lambda i: (jnp.maximum(i - steps, 0), 0))
    low_near = pl.BlockSpec((chunk, split), lambda i: (steps + jnp.minimum(i, steps - 1), 0))
    high_near = pl.BlockSpec((chunk, split), lambda i: (jnp.maximum(i, steps), 0))
    row_block = pl.BlockSpec((chunk, depth), lambda i: (i, 0))
    thin = pl.BlockSpec((chunk, 1), lambda i: (i, 0))
    return pl.pallas_call(
        functools.partial(token_grads_kernel, steps=steps),
        grid=(rows // chunk,),
        in_specs=[low_part, high_part, low_near, high_near, low_part, high_part] * 2
        + [row_block, row_block, thin, thin, pl.BlockSpec((1, depth), lambda i: (0, 0))],
        out_specs=row_block,
        out_shape=jax.ShapeDtypeStruct(tokens.shape, tokens.dtype),
        compiler_params=pltpu.CompilerParams(vmem_limit_bytes=VMEM_BYTES),
        cost_estimate=SHORT,
    )(*left_parts, *right_parts, tokens, cotangent, mean, root, gain.reshape(1, -1))


def attention_kernel(
    q_ref,
    k_ref,
    v_ref,
    g_ref,
    cos_ref,
    above_ref,
    below_ref,
    mixed_ref,
    grads_ref,
    sums_ref,
    keys_across,
    values_across,
    query_total,
    key_total,
    value_total,
    weight_buf,
    top_buf,
    out_buf,
    across_buf,
    *,
    block,
    block_count,
):
    step = pl.program_id(1)
    scale = HEAD_DIM**-0.5
    rate = scale * 1.4426950408889634

    @pl.when(step == 0)
    def _():
        keys_across[...] = k_ref[...].T
        values_across[...] = v_ref[...].T
        key_total[...] = jnp.zeros_like(key_total)
        value_total[...] = jnp.zeros_like(value_total)

    rows = pl.ds(pl.multiple_of(step * block, block), block)
    queries, grads = q_ref[rows, :], g_ref[rows, :]
    lane = lax.broadcasted_iota(jnp.int32, (block, PAIR), 1)
    own_lanes = [lane // HEAD_DIM == head for head in range(2)]
    query_heads = [jnp.where(own, queries, jnp.zeros_like(queries)) for own in own_lanes]
    grad_heads = [jnp.where(own, grads, jnp.zeros_like(grads)) for own in own_lanes]
    parts = [slice(head * HEAD_DIM, (head + 1) * HEAD_DIM) for head in range(2)]

    def weigh(there, index, first):
        keys = k_ref[there, :]
        score_heads = [
            lax.dot_general(keys, own, ROWS_BY_ROWS, preferred_element_type=jnp.float32)
            for own in query_heads
        ]
        for head in range(2):
            scores = score_heads[head]
            if first:
                key_pos = lax.broadcasted_iota(jnp.int32, (block, block), 0)
                query_pos = lax.broadcasted_iota(jnp.int32, (block, block), 1)
                scores = jnp.where(key_pos <= query_pos, scores, masked_score)
            top = jnp.max(scores, axis=0, keepdims=True) * rate
            if not first:
                before = top_buf[head, 0]
                top = jnp.maximum(top, before)
            weights = jnp.exp2(scores * rate - top)
            weight_buf[head, there, :] = weights
            top_buf[head, 2 + index] = top
            total = jnp.sum(weights, axis=0, keepdims=True)
            out = jnp.dot(
                values_across[parts[head], there],
                weights.astype(jnp.bfloat16),
                preferred_element_type=jnp.float32,
            )
            if not first:
                shrink = jnp.exp2(before - top)
                total += top_buf[head, 1] * shrink
                out += out_buf[parts[head], :] * shrink
            top_buf[head, 0] = top
            top_buf[head, 1] = total
            out_buf[parts[head], :] = out

    def over_blocks(act):
        act(rows, step, True)

        @pl.when(lax.rem(step, 2) == 1)
        def _():
            act(pl.ds(pl.multiple_of((step - 1) * block, block), block), step - 1, False)

        @pl.loop(0, lax.div(step, 2))
        def _(index):
            start = pl.multiple_of(index * 2 * block, 2 * block)
            act(pl.ds(start, 2 * block), 2 * index, False)

    over_blocks(weigh)

    grads_across = grads.T.astype(jnp.float32)
    inner, share = [], []
    for head in range(2):
        share.append(1.0 / top_buf[head, 1])
        out = out_buf[parts[head], :] * share[head]
        out_buf[parts[head], :] = out
        inner.append(jnp.sum(out * grads_across[parts[head]], axis=0, keepdims=True))
    mixed_ref[rows, :] = out_buf[...].T.astype(mixed_ref.dtype)

    def differentiate(there, index, first):
        values = v_ref[there, :]
        prob_heads = [
            lax.dot_general(values, own, ROWS_BY_ROWS, preferred_element_type=jnp.float32)
            for own in grad_heads
        ]
        value_parts, key_parts = [], []
        for head in range(2):
            factor = jnp.exp2(top_buf[head, 2 + index] - top_buf[head, 0]) * share[head]
            exact = weight_buf[head, there, :] * factor
            rounded = exact.astype(jnp.bfloat16)
            grad_scores = (exact * (prob_heads[head] - inner[head])).astype(jnp.bfloat16)
            value_parts.append(
                jnp.dot(rounded, grad_heads[head], preferred_element_type=jnp.float32)
            )
            key_parts.append(
                jnp.dot(grad_scores, query_heads[head], preferred_element_type=jnp.float32)
            )
            across = jnp.dot(
                keys_across[parts[head], there], grad_scores, preferred_element_type=jnp.float32
            )
            if first:
                across_buf[parts[head], :] = across
            else:
                across_buf[parts[head], :] += across
        value_total[there, :] += value_parts[0] + value_parts[1]
        key_total[there, :] += key_parts[0] + key_parts[1]

    over_blocks(differentiate)
    query_total[rows, :] = across_buf[...].T

    @pl.when(step == block_count - 1)
    def _():
        lanes = cos_ref[...], above_ref[...], below_ref[...]
        for slot, field in enumerate(
            (
                turn_back(query_total[...] * scale, *lanes),
                turn_back(key_total[...] * scale, *lanes),
                value_total[...],
            )
        ):
            low = field.astype(grads_ref.dtype)
            grads_ref[slot] = low
            sums_ref[slot] = jnp.sum(low.astype(jnp.float32), axis=0, keepdims=True)


def attention(joined, grad_mixed, lanes, first, last, earlier=None):
    rows, width = grad_mixed.shape
    block = min(512, LENGTH)
    pairs, block_count = width // PAIR, LENGTH // block
    row_block = pl.BlockSpec((LENGTH, PAIR), lambda p, i: (0, first + p))
    table = pl.BlockSpec((LENGTH, PAIR), lambda p, i: (0, 0))
    kept = () if earlier is None else tuple(earlier)
    kernel = functools.partial(attention_kernel, block=block, block_count=block_count)

    def body(*refs):
        kernel(*refs[:7], *refs[7 + len(kept) :])

    return pl.pallas_call(
        body,
        grid=(last - first, block_count),
        in_specs=[
            row_block,
            pl.BlockSpec((LENGTH, PAIR), lambda p, i: (0, pairs + first + p)),
            pl.BlockSpec((LENGTH, PAIR), lambda p, i: (0, 2 * pairs + first + p)),
            row_block,
            table,
            table,
            table,
        ]
        + [pl.BlockSpec(memory_space=pl.ANY)] * len(kept),
        out_specs=[
            row_block,
            pl.BlockSpec((3, LENGTH, PAIR), lambda p, i: (0, 0, first + p)),
            pl.BlockSpec((3, 1, PAIR), lambda p, i: (0, 0, first + p)),
        ],
        out_shape=[
            jax.ShapeDtypeStruct((rows, width), jnp.bfloat16),
            jax.ShapeDtypeStruct((3, rows, width), jnp.bfloat16),
            jax.ShapeDtypeStruct((3, 1, width), jnp.float32),
        ],
        scratch_shapes=[
            pltpu.VMEM((PAIR, LENGTH), jnp.bfloat16),
            pltpu.VMEM((PAIR, LENGTH), jnp.bfloat16),
            pltpu.VMEM((LENGTH, PAIR), jnp.float32),
            pltpu.VMEM((LENGTH, PAIR), jnp.float32),
            pltpu.VMEM((LENGTH, PAIR), jnp.float32),
            pltpu.VMEM((2, LENGTH, block), jnp.float32),
            pltpu.VMEM((2, 2 + block_count, 1, block), jnp.float32),
            pltpu.VMEM((PAIR, block), jnp.float32),
            pltpu.VMEM((PAIR, block), jnp.float32),
        ],
        input_output_aliases={7 + i: i for i in range(len(kept))},
        compiler_params=pltpu.CompilerParams(vmem_limit_bytes=VMEM_BYTES),
        cost_estimate=SHORT,
    )(joined, joined, joined, grad_mixed, *lanes, *kept)


def norm_kernel(starts_ref, gain_ref, shift_ref, following_ref, *refs):
    count = (len(refs) - 6) // 3
    pieces = refs[:count]
    raw, normed, mean_ref, root_ref, following_out = refs[count : count + 5]
    buffers = refs[count + 5 : 2 * count + 5]
    results = refs[2 * count + 5 : 3 * count + 5]
    sems = refs[-1]
    following_out[...] = following_ref[...]
    for slot in range(count):
        pltpu.make_async_copy(pieces[slot], buffers[slot], sems.at[0, slot]).start()
    writes = []
    for slot in range(count):
        buffer, result = buffers[slot], results[slot]
        size = buffer.shape[0]
        where = pl.ds(pl.multiple_of(starts_ref[slot], size), size)
        pltpu.make_async_copy(pieces[slot], buffer, sems.at[0, slot]).wait()
        write = pltpu.make_async_copy(buffer, raw.at[where, :], sems.at[1, slot])
        write.start()
        writes.append(write)
        chunk = min(128, size)

        @pl.loop(0, size // chunk)
        def _(step, buffer=buffer, result=result, slot=slot):
            here = pl.ds(pl.multiple_of(step * chunk, chunk), chunk)
            rows = buffer[here, :].astype(jnp.float32)
            mean = jnp.mean(rows, axis=-1, keepdims=True)
            centred = rows - mean
            variance = jnp.mean(centred * centred, axis=-1, keepdims=True)
            root = lax.rsqrt(variance + epsilon)
            out = centred * root * gain_ref[...] + shift_ref[...]
            result[here, :] = out.astype(result.dtype)
            there = pl.ds(pl.multiple_of(starts_ref[slot] + step * chunk, chunk), chunk)
            mean_ref[there, :] = mean
            root_ref[there, :] = root

        write = pltpu.make_async_copy(result, normed.at[where, :], sems.at[2, slot])
        write.start()
        writes.append(write)
    for write in writes:
        write.wait()


def norm_rows(pieces, gain, shift, following):
    depth = gain.shape[0]
    total = sum(piece.shape[0] for _, piece in pieces)
    count = len(pieces)
    low = jnp.bfloat16
    starts = jnp.stack([jnp.asarray(start, jnp.int32) for start, _ in pieces])
    any_space = pl.BlockSpec(memory_space=pl.ANY)
    vmem = pl.BlockSpec(memory_space=pltpu.VMEM)
    stage = [pltpu.VMEM(piece.shape, low) for _, piece in pieces]
    return pl.pallas_call(
        norm_kernel,
        in_specs=[pl.BlockSpec(memory_space=pltpu.SMEM), vmem, vmem, vmem] + [any_space] * count,
        out_specs=[any_space, any_space, vmem, vmem, vmem],
        out_shape=[
            jax.ShapeDtypeStruct((total, depth), low),
            jax.ShapeDtypeStruct((total, depth), low),
            jax.ShapeDtypeStruct((total, 1), jnp.float32),
            jax.ShapeDtypeStruct((total, 1), jnp.float32),
            jax.ShapeDtypeStruct(following.shape, following.dtype),
        ],
        scratch_shapes=stage + stage + [pltpu.SemaphoreType.DMA((3, count))],
        compiler_params=pltpu.CompilerParams(vmem_limit_bytes=VMEM_BYTES),
        cost_estimate=SHORT,
    )(
        starts,
        gain.reshape(1, depth),
        shift.reshape(1, depth),
        following,
        *[piece for _, piece in pieces],
    )


def on_device(
    tokens,
    norm_gain,
    norm_shift,
    weight_qkv,
    bias_qkv,
    weight_dense,
    weight_up,
    bias_up,
    weight_down,
    bias_out,
    cotangent,
):
    f32, low = jnp.float32, jnp.bfloat16
    depth = tokens.shape[1]
    local_rows = tokens.shape[0]
    tensor_index = lax.axis_index("tensor")

    full_up = lax.all_gather(weight_up, "dp", axis=0, tiled=True)
    token_parts = gather_start(tokens)
    lanes = lane_tables(LENGTH)
    out_part = jnp.sum(cotangent, axis=0, dtype=f32)
    lanes, out_part, token_parts = after((lanes, out_part, token_parts))
    full_qkv = lax.all_gather(
        after(jnp.transpose(weight_qkv, (1, 0, 2)), token_parts), "dp", axis=1, tiled=True
    )
    token_parts = gather_pass(token_parts)
    all_tokens, gathered, mean, root, sent = norm_rows(
        gathered_pieces(token_parts), norm_gain, norm_shift, cotangent
    )
    grad_parts = gather_start(sent)

    full_dense = lax.all_gather(after(weight_dense, gathered), "dp", axis=1, tiled=True)
    own_mean = lax.dynamic_slice_in_dim(mean, tensor_index * local_rows, local_rows, 0)
    own_root = lax.dynamic_slice_in_dim(root, tensor_index * local_rows, local_rows, 0)
    active, slope = hidden_rows(gathered, full_up, bias_up)
    own_mean, own_root, active = after((own_mean, own_root, active))
    grad_parts, active = after((grad_parts, active))
    full_down = lax.all_gather(after(weight_down, grad_parts), "dp", axis=1, tiled=True)
    grad_parts = gather_pass(grad_parts)
    joined = joined_rows(after(gathered, active, grad_parts[:3]), full_qkv, bias_qkv, lanes)
    grad_parts, joined = after((grad_parts, joined))
    grad_rows, grad_down = first_grads(gathered_pieces(grad_parts), active)
    grad_mixed = jnp.einsum(
        "td,kd->tk", grad_rows, after(full_dense, grad_down), preferred_element_type=f32
    ).astype(low)
    dense_parts = gather_start(after(full_dense, grad_mixed))
    grad_down_sum = lax.psum_scatter(grad_down, "dp", scatter_dimension=1, tiled=True)

    pairs = grad_mixed.shape[1] // PAIR
    part = attention(joined, grad_mixed, lanes, 0, pairs // 2)
    dense_parts, part = after((dense_parts, part))
    dense_parts = gather_pass(dense_parts)
    feed_cuts = feed_rows(after(active, part[0]), full_down)
    feed_cuts, dense_parts = after((feed_cuts, dense_parts))
    feed_parts = scatter_send(feed_cuts)
    grad_hidden, grad_up, bias_up_part = hidden_grads(
        after(grad_rows, feed_cuts), full_down, slope, gathered
    )
    grad_up, feed_parts = after((grad_up, feed_parts))
    feed_parts = scatter_fold(feed_parts)
    grad_up_sum = lax.psum_scatter(
        after(grad_up, feed_parts[:2]), "dp", scatter_dimension=0, tiled=True
    )
    feed_parts = scatter_pass(feed_parts)
    part = attention(after(joined, grad_up), grad_mixed, lanes, pairs // 2, pairs, part)
    mixed, grad_joined, bias_qkv_part = part
    mixed, grad_joined, feed_parts = after((mixed, grad_joined, feed_parts))

    mixed_parts = exchange_start(mixed)
    grad_last = last_grads(gathered, grad_joined, grad_rows, mixed)
    grad_last, mixed_parts = after((grad_last, mixed_parts))
    grad_last_sum = lax.psum_scatter(
        grad_last, "dp", scatter_dimension=1, tiled=True
    )
    half = depth // 2
    sources = full_qkv, grad_hidden, full_up, all_tokens, mean, root
    *left_sums, left_cuts = normed_grads(after(grad_joined, grad_last), *sources, 0, half)
    left_parts = scatter_send(left_cuts)
    *right_sums, right_cuts = normed_grads(after(grad_joined, left_cuts), *sources, half, depth)
    right_cuts, right_sums, left_parts = after((right_cuts, right_sums, left_parts))
    sums = jnp.concatenate(
        [left_sums[0][0], right_sums[0][0], left_sums[1][0], right_sums[1][0], out_part]
    ).reshape(-1, PAIR)
    right_parts = scatter_send(right_cuts)
    left_parts = scatter_pass(scatter_fold(left_parts))
    block_out = finish_output(
        after(mixed_parts, right_cuts), dense_parts, tokens, bias_out, feed_parts
    )
    small = jnp.concatenate(
        [sums.reshape(-1), bias_qkv_part.reshape(-1), bias_up_part.reshape(-1)]
    ).reshape(-1, PAIR)
    block_out, small = after((block_out, small))
    small = jnp.sum(lax.all_gather(small, "dp", axis=0), axis=0)
    block_out, right_parts, left_parts, small = after(
        (block_out, right_parts, left_parts, small)
    )
    right_parts = scatter_fold(right_parts)
    right_parts, small, grad_up_sum, grad_down_sum = after(
        (right_parts, small, grad_up_sum, grad_down_sum)
    )
    right_parts = scatter_pass(right_parts)
    small = small.reshape(-1)
    over_all = exchange_sum(small[: 3 * depth].reshape(-1, PAIR), "tensor")
    grad_gain, grad_shift, grad_bias_out = over_all.reshape(3, depth)
    bias_size = bias_qkv.size
    grad_bias_qkv = small[3 * depth : 3 * depth + bias_size].reshape(bias_qkv.shape)
    grad_bias_up = small[3 * depth + bias_size :]
    last = jnp.transpose(grad_last_sum, (1, 0, 2)).astype(f32)
    ready = grad_up_sum.astype(f32), grad_down_sum.astype(f32), last
    ready, left_parts = after((ready, left_parts))
    grad_up_sum, grad_down_sum, last = ready
    grad_tokens = token_grads(
        left_parts, right_parts, tokens, cotangent, own_mean, own_root, norm_gain
    )
    return (
        block_out,
        grad_tokens,
        grad_gain,
        grad_shift,
        last[:, :3],
        grad_bias_qkv,
        jnp.transpose(last[:, 3]),
        grad_up_sum,
        grad_bias_up,
        grad_down_sum,
        grad_bias_out,
    )


def solution(mesh):
    in_specs = (
        P(("dp", "tensor"), None),
        P(),
        P(),
        P("dp", None, "tensor"),
        P(None, "tensor"),
        P("tensor", "dp"),
        P("dp", "tensor"),
        P("tensor"),
        P("tensor", "dp"),
        P(),
        P(("dp", "tensor"), None),
    )
    out_specs = (
        P(("dp", "tensor"), None),
        P(("dp", "tensor"), None),
        P(),
        P(),
        P("dp", None, "tensor"),
        P(None, "tensor"),
        P("tensor", "dp"),
        P("dp", "tensor"),
        P("tensor"),
        P("tensor", "dp"),
        P(),
    )
    return jax.shard_map(
        on_device, mesh=mesh, in_specs=in_specs, out_specs=out_specs, check_vma=False
    )
```

```python
import functools

import jax
import jax.numpy as jnp
from jax import lax
from jax.experimental import pallas as pl
from jax.experimental.pallas import tpu as pltpu
from jax.sharding import PartitionSpec as P

HEAD_DIM = 64
ROT = 32
LENGTH = 2048
PAIR = 2 * HEAD_DIM

epsilon = 1e-05
masked_score = -1e30
MIB = 1024 * 1024
VMEM_BYTES = 64 * MIB - 256 * 1024
ROWS_BY_ROWS = (((1,), (1,)), ((), ()))
COLUMNS_BY_COLUMNS = (((0,), (0,)), ((), ()))


SHORT = pl.CostEstimate(flops=1, bytes_accessed=1, transcendentals=0)


def after(value, *earlier):
    return lax.optimization_barrier((value,) + earlier)[0]


def swap(value, axis, bit):
    count = lax.axis_size(axis)
    return lax.ppermute(value, axis, [(i, i ^ bit) for i in range(count)])


def gather_start(block):
    if lax.axis_size("tensor") != 4:
        return (lax.all_gather(block, "tensor", axis=0, tiled=True),)
    return block, swap(block, "tensor", 1), swap(block, "tensor", 2)


def halves_kernel(one_ref, two_ref, low_ref, high_ref):
    half = one_ref.shape[0] // 2
    low_ref[...] = one_ref[:half, :]
    high_ref[...] = two_ref[half:, :]


def gather_pass(parts):
    if len(parts) == 1:
        return parts
    block, one, two = parts
    rows, depth = block.shape
    half = jax.ShapeDtypeStruct((rows // 2, depth), block.dtype)
    low, high = pl.pallas_call(
        halves_kernel,
        out_shape=[half, half],
        compiler_params=pltpu.CompilerParams(vmem_limit_bytes=VMEM_BYTES),
        cost_estimate=SHORT,
    )(one, two)
    return block, one, two, swap(low, "tensor", 2), swap(high, "tensor", 1)


def gathered_pieces(parts):
    if len(parts) == 1:
        return [(0, parts[0])]
    block, one, two, low, high = parts
    rows = block.shape[0]
    me = lax.axis_index("tensor")
    return [
        (me * rows, block),
        ((me ^ 1) * rows, one),
        ((me ^ 2) * rows, two),
        ((me ^ 3) * rows, low),
        ((me ^ 3) * rows + rows // 2, high),
    ]


def wide(piece):
    return piece.astype(jnp.float32)


def owner_cuts(total):
    count = lax.axis_size("tensor")
    rows = total // count
    me = lax.axis_index("tensor")
    if count == 4:
        order = [me ^ bit for bit in (3, 1, 2, 0)]
        half = rows // 2
        places = (((0, 0), (1, 0)), ((0, half), (3, 0)), ((2, 0), (1, half)), ((4, 0), (5, 0)))
        sizes = (rows, rows, half, half, half, half)
    else:
        order = list(range(count))
        places = tuple(((owner, 0),) for owner in range(count))
        sizes = (rows,) * count
    starts = jnp.stack([jnp.asarray(owner * rows, jnp.int32) for owner in order])
    return starts, places, sizes


def scatter_send(cuts):
    if lax.axis_size("tensor") != 4:
        whole = wide(jnp.concatenate(cuts))
        return (lax.psum_scatter(whole, "tensor", scatter_dimension=0, tiled=True),)
    for_one, for_two, two_low, one_high, low, high = cuts
    return swap(for_one, "tensor", 1), swap(for_two, "tensor", 2), two_low, one_high, low, high


def fold_kernel(a_ref, b_ref, c_ref, d_ref, ab_ref, cd_ref):
    half = a_ref.shape[0]
    ab_ref[...] = (wide(a_ref[...]) + wide(b_ref[:half, :])).astype(ab_ref.dtype)
    cd_ref[...] = (wide(c_ref[...]) + wide(d_ref[:half, :])).astype(cd_ref.dtype)


def scatter_fold(parts):
    if len(parts) == 1:
        return parts
    first, second, two_low, one_high, low, high = parts
    shape = jax.ShapeDtypeStruct(low.shape, low.dtype)
    forward = pl.pallas_call(
        fold_kernel,
        out_shape=[shape, shape],
        compiler_params=pltpu.CompilerParams(vmem_limit_bytes=VMEM_BYTES),
        cost_estimate=SHORT,
    )(two_low, first, one_high, second)
    return (*forward, first, second, low, high)


def scatter_pass(parts):
    if len(parts) == 1:
        return parts
    two_low, one_high, first_near, second_near, low, high = parts
    return (
        swap(two_low, "tensor", 2),
        swap(one_high, "tensor", 1),
        first_near,
        second_near,
        low,
        high,
    )


def exchange_start(columns):
    if lax.axis_size("tensor") != 4:
        return (lax.all_to_all(columns, "tensor", 0, 1, tiled=True),)
    rows = columns.shape[0] // 4
    me = lax.axis_index("tensor")
    pieces = []
    for bit in range(4):
        piece = lax.dynamic_slice_in_dim(columns, (me ^ bit) * rows, rows, 0)
        pieces.append(swap(piece, "tensor", bit) if bit else piece)
    return tuple(pieces)


def exchange_sum(value, axis, step=1):
    parts = [value]
    for bit in range(step, lax.axis_size(axis), step):
        parts.append(swap(value, axis, bit))
    return functools.reduce(lambda a, b: a + b, parts)


def lane_tables(row_total):
    half_rot = ROT // 2
    positions = (jnp.arange(row_total, dtype=jnp.int32) % LENGTH).astype(jnp.float32)
    inverse = 10000.0 ** (-(2.0 * jnp.arange(half_rot, dtype=jnp.float32)) / ROT)
    angles = positions[:, None] * inverse[None, :]
    cosine, sine = jnp.cos(angles), jnp.sin(angles)
    ones = jnp.ones((row_total, HEAD_DIM - ROT), jnp.float32)
    zeros = jnp.zeros((row_total, half_rot), jnp.float32)
    rest = jnp.zeros((row_total, HEAD_DIM - ROT), jnp.float32)
    cos_lanes = jnp.concatenate([cosine, cosine, ones] * 2, axis=1)
    from_above = jnp.concatenate([-sine, zeros, rest] * 2, axis=1)
    from_below = jnp.concatenate([zeros, sine, rest] * 2, axis=1)
    return cos_lanes, from_above, from_below


def turn(field, cos_lanes, from_above, from_below):
    half_rot = ROT // 2
    above = pltpu.roll(field, PAIR - half_rot, 1)
    below = pltpu.roll(field, half_rot, 1)
    return field * cos_lanes + above * from_above + below * from_below


def turn_back(field, cos_lanes, from_above, from_below):
    half_rot = ROT // 2
    above = pltpu.roll(field, PAIR - half_rot, 1)
    below = pltpu.roll(field, half_rot, 1)
    return field * cos_lanes - above * from_above - below * from_below


def joined_kernel(x_ref, w_ref, bias_ref, cos_ref, above_ref, below_ref, out_ref):
    width = out_ref.shape[1]
    chunk = min(256, width)
    slot = pl.program_id(0)

    def product(start):
        columns = slice(start, start + chunk)
        part = jnp.dot(x_ref[...], w_ref[0, :, columns], preferred_element_type=jnp.float32)
        return part + bias_ref[0, :, columns]

    @pl.when(slot < 2)
    def _():
        for start in range(0, width, chunk):
            part = product(start)
            for shift in range(0, chunk, PAIR):
                lanes = part[:, shift : shift + PAIR]
                turned = turn(lanes, cos_ref[...], above_ref[...], below_ref[...])
                columns = slice(start + shift, start + shift + PAIR)
                out_ref[:, columns] = turned.astype(out_ref.dtype)

    @pl.when(slot == 2)
    def _():
        for start in range(0, width, chunk):
            out_ref[:, start : start + chunk] = product(start).astype(out_ref.dtype)


def joined_rows(x, w, bias, lanes):
    rows, depth = x.shape
    width = w.shape[2]
    block = min(1024, rows)
    return pl.pallas_call(
        joined_kernel,
        grid=(3, rows // block),
        in_specs=[
            pl.BlockSpec((block, depth), lambda j, i: (i, 0)),
            pl.BlockSpec((1, depth, width), lambda j, i: (j, 0, 0)),
            pl.BlockSpec((1, 1, width), lambda j, i: (j, 0, 0)),
        ]
        + [pl.BlockSpec((block, PAIR), lambda j, i: (i, 0))] * 3,
        out_specs=pl.BlockSpec((block, width), lambda j, i: (i, j)),
        out_shape=jax.ShapeDtypeStruct((rows, 3 * width), jnp.bfloat16),
        compiler_params=pltpu.CompilerParams(vmem_limit_bytes=VMEM_BYTES),
        cost_estimate=SHORT,
    )(x, w, bias.reshape(3, 1, width), *lanes)


def hidden_kernel(x_ref, w_ref, bias_ref, active_ref, slope_ref):
    hidden = jnp.dot(x_ref[...], w_ref[...], preferred_element_type=jnp.float32) + bias_ref[...]
    scale = (2.0 / jnp.pi) ** 0.5
    square = hidden * hidden
    inner = scale * hidden * (1.0 + 0.044715 * square)
    bent = jnp.tanh(inner)
    half = 0.5 * (1.0 + bent)
    active_ref[...] = (hidden * half).astype(active_ref.dtype)
    growth = scale * (1.0 + (3.0 * 0.044715) * square)
    slope = half + 0.5 * hidden * (1.0 - bent * bent) * growth
    slope_ref[...] = slope.astype(slope_ref.dtype)


def hidden_rows(x, w, bias):
    rows, depth = x.shape
    width = w.shape[1]
    block, columns = min(1024, rows), min(1024, width)
    return pl.pallas_call(
        hidden_kernel,
        grid=(width // columns, rows // block),
        in_specs=[
            pl.BlockSpec((block, depth), lambda j, i: (i, 0)),
            pl.BlockSpec((depth, columns), lambda j, i: (0, j)),
            pl.BlockSpec((1, columns), lambda j, i: (0, j)),
        ],
        out_specs=[pl.BlockSpec((block, columns), lambda j, i: (i, j))] * 2,
        out_shape=[jax.ShapeDtypeStruct((rows, width), jnp.bfloat16)] * 2,
        compiler_params=pltpu.CompilerParams(vmem_limit_bytes=VMEM_BYTES),
        cost_estimate=SHORT,
    )(x, w, bias.reshape(1, width))


def whole_call(kernel, in_specs, out_specs, out_shape, scratch):
    return pl.pallas_call(
        kernel,
        in_specs=in_specs,
        out_specs=out_specs,
        out_shape=out_shape,
        scratch_shapes=scratch,
        compiler_params=pltpu.CompilerParams(vmem_limit_bytes=VMEM_BYTES),
        cost_estimate=SHORT,
    )


def columns_of(ref, index, size):
    return ref.at[:, pl.ds(pl.multiple_of(index * size, size), size)]


def rows_of(ref, index, size):
    return ref.at[pl.ds(pl.multiple_of(index * size, size), size), :]


def nt_dot(a, b):
    return lax.dot_general(a, b, ROWS_BY_ROWS, preferred_element_type=jnp.float32)


def tn_dot(a, b):
    return lax.dot_general(a, b, COLUMNS_BY_COLUMNS, preferred_element_type=jnp.float32)


ANY = pl.BlockSpec(memory_space=pl.ANY)
SMEM = pl.BlockSpec(memory_space=pltpu.SMEM)
VMEM = pl.BlockSpec(memory_space=pltpu.VMEM)


def tile_loop(count, tiles, tile_sems, where, compute):
    def write(step, slot):
        return pltpu.make_async_copy(tiles.at[slot], where(step), tile_sems.at[slot])

    @pl.loop(0, count)
    def _(step):
        slot = lax.rem(step, 2)

        @pl.when(step >= 2)
        def _():
            write(step, slot).wait()

        tiles[slot] = compute(step).astype(tiles.dtype)
        write(step, slot).start()

    for step in range(max(count - 2, 0), count):
        write(step, step % 2).wait()


def first_grads_kernel(starts_ref, active, *refs):
    count = len(refs) - 9
    pieces = refs[:count]
    rows_out, down_out, grad_buf, active_buf, tiles = refs[count:-4]
    piece_sems, load_sems, row_sems, tile_sems = refs[-4:]
    _, rows, half = grad_buf.shape
    blocks, _, block = active_buf.shape

    def piece_copy(slot, side):
        size = pieces[slot].shape[0]
        there = pl.ds(pl.multiple_of(starts_ref[slot], size), size)
        return pltpu.make_async_copy(
            pieces[slot].at[:, pl.ds(side * half, half)],
            grad_buf.at[side, there, :],
            piece_sems.at[slot, side],
        )

    def active_copy(index):
        return pltpu.make_async_copy(
            columns_of(active, index, block), active_buf.at[index], load_sems.at[index]
        )

    def row_copy(side):
        return pltpu.make_async_copy(
            grad_buf.at[side], rows_out.at[:, pl.ds(side * half, half)], row_sems.at[side]
        )

    active_copy(0).start()
    for side in range(2):
        for slot in range(count):
            piece_copy(slot, side).start()
    for index in range(1, blocks):
        active_copy(index).start()

    def compute(step):
        for index in range(blocks):
            pl.when(step == 2 * index)(active_copy(index).wait)
        for side in range(2):

            @pl.when(step == side)
            def _(side=side):
                for slot in range(count):
                    piece_copy(slot, side).wait()
                row_copy(side).start()

        return tn_dot(active_buf[lax.div(step, 2)], grad_buf[lax.rem(step, 2)])

    tile_loop(
        2 * blocks,
        tiles,
        tile_sems,
        lambda step: down_out.at[
            pl.ds(pl.multiple_of(lax.div(step, 2) * block, block), block),
            pl.ds(pl.multiple_of(lax.rem(step, 2) * half, half), half),
        ],
        compute,
    )
    for side in range(2):
        row_copy(side).wait()


def first_grads(pieces, active):
    low = jnp.bfloat16
    rows, hidden = active.shape
    depth = pieces[0][1].shape[1]
    half, block = depth // 2, min(512, hidden)
    count = len(pieces)
    starts = jnp.stack([jnp.asarray(start, jnp.int32) for start, _ in pieces])
    return whole_call(
        first_grads_kernel,
        [SMEM] + [ANY] * (1 + count),
        [ANY, ANY],
        [
            jax.ShapeDtypeStruct((rows, depth), low),
            jax.ShapeDtypeStruct((hidden, depth), low),
        ],
        [
            pltpu.VMEM((2, rows, half), low),
            pltpu.VMEM((hidden // block, rows, block), low),
            pltpu.VMEM((2, block, half), low),
            pltpu.SemaphoreType.DMA((count, 2)),
            pltpu.SemaphoreType.DMA((hidden // block,)),
            pltpu.SemaphoreType.DMA((2,)),
            pltpu.SemaphoreType.DMA((2,)),
        ],
    )(starts, active, *[piece for _, piece in pieces])


def feed_kernel(starts_ref, active, weight, *refs, places):
    cuts = refs[:-5]
    active_buf, weight_buf, out_buf, load_sems, cut_sems = refs[-5:]
    owners, halves = len(places), len(places[0])
    rows = active_buf.shape[0]
    half = weight_buf.shape[2]
    owner_rows = rows // owners
    piece = owner_rows // halves

    def weight_load(side):
        return pltpu.make_async_copy(
            weight.at[:, pl.ds(side * half, half)], weight_buf.at[side], load_sems.at[side]
        )

    def row_load(owner):
        here = pl.ds(pl.multiple_of(starts_ref[owner], owner_rows), owner_rows)
        return pltpu.make_async_copy(
            active.at[here, :], active_buf.at[here, :], load_sems.at[2 + owner]
        )

    weight_load(0).start()
    row_load(0).start()
    weight_load(1).start()
    for owner in range(1, owners):
        row_load(owner).start()

    def cut_copy(owner, part_of, side):
        return pltpu.make_async_copy(
            out_buf.at[side, pl.ds(owner * owner_rows + part_of * piece, piece), :],
            cuts[places[owner][part_of][0]].at[
                pl.ds(places[owner][part_of][1], piece),
                pl.ds(pl.multiple_of(side * half, half), half),
            ],
            cut_sems.at[side, owner * halves + part_of],
        )

    @pl.loop(0, 2 * owners)
    def _(step):
        owner, side = lax.div(step, 2), lax.rem(step, 2)
        for own in range(owners):
            pl.when(step == 2 * own)(row_load(own).wait)
        for own in range(2):
            pl.when(step == own)(weight_load(own).wait)
        here = pl.ds(pl.multiple_of(starts_ref[owner], owner_rows), owner_rows)
        there = pl.ds(pl.multiple_of(owner * owner_rows, owner_rows), owner_rows)
        out_buf[side, there, :] = jnp.dot(
            active_buf[here, :], weight_buf[side], preferred_element_type=jnp.float32
        ).astype(out_buf.dtype)
        for own in range(owners):

            @pl.when(owner == own)
            def _(own=own):
                for part_of in range(halves):
                    cut_copy(own, part_of, side).start()

    for side in range(2):
        for own in range(owners):
            for part_of in range(halves):
                cut_copy(own, part_of, side).wait()


def feed_rows(active, weight):
    low = jnp.bfloat16
    rows, hidden = active.shape
    depth = weight.shape[1]
    half = depth // 2
    starts, places, sizes = owner_cuts(rows)
    owners, halves = len(places), len(places[0])
    return tuple(
        whole_call(
            functools.partial(feed_kernel, places=places),
            [SMEM] + [ANY] * 2,
            [ANY] * len(sizes),
            [jax.ShapeDtypeStruct((size, depth), low) for size in sizes],
            [
                pltpu.VMEM((rows, hidden), low),
                pltpu.VMEM((2, hidden, half), low),
                pltpu.VMEM((2, rows, half), low),
                pltpu.SemaphoreType.DMA((2 + owners,)),
                pltpu.SemaphoreType.DMA((2, owners * halves)),
            ],
        )(starts, active, weight)
    )


def hidden_grads_kernel(grad_rows, weight, slope, x, hidden_out, up_out, sum_out, *refs):
    grad_buf, weight_buf, slope_buf, x_buf, hidden_buf, tiles = refs[:6]
    load_sems, slope_sems, hidden_sems, tile_sems = refs[6:]
    rows = grad_buf.shape[0]
    parts, _, part = hidden_buf.shape
    x_blocks, _, x_block = x_buf.shape
    chunk = slope_buf.shape[1]
    chunks = rows // chunk

    def load(source, target, index):
        return pltpu.make_async_copy(source, target, load_sems.at[index])

    def grad_load(index):
        here = pl.ds(pl.multiple_of(index * chunk, chunk), chunk)
        return load(grad_rows.at[here, :], grad_buf.at[here, :], index)

    def weight_load(index):
        here = pl.ds(pl.multiple_of(index * part, part), part)
        return load(weight.at[here, :], weight_buf.at[here, :], chunks + index)

    x_loads = [
        load(columns_of(x, i, x_block), x_buf.at[i], chunks + parts + i) for i in range(x_blocks)
    ]

    def slope_copy(step, slot):
        place = (
            pl.ds(pl.multiple_of(lax.rem(step, chunks) * chunk, chunk), chunk),
            pl.ds(pl.multiple_of(lax.div(step, chunks) * part, part), part),
        )
        return pltpu.make_async_copy(slope.at[place], slope_buf.at[slot], slope_sems.at[slot])

    def hidden_copy(index):
        return pltpu.make_async_copy(
            hidden_buf.at[index],
            hidden_out.at[:, pl.ds(index * part, part)],
            hidden_sems.at[index],
        )

    weight_load(0).start()
    grad_load(0).start()
    slope_copy(0, 0).start()
    for index in range(1, chunks):
        grad_load(index).start()
    for index in range(1, parts):
        weight_load(index).start()
    for copy in x_loads:
        copy.start()
    sum_out[...] = jnp.zeros_like(sum_out)

    @pl.loop(0, parts * chunks)
    def _(step):
        slot = lax.rem(step, 2)
        index = lax.div(step, chunks)

        @pl.when(step + 1 < parts * chunks)
        def _():
            slope_copy(step + 1, 1 - slot).start()

        @pl.when(lax.rem(step, chunks) == 0)
        def _():
            weight_load(index).wait()

        @pl.when(index == 0)
        def _():
            grad_load(step).wait()

        slope_copy(step, slot).wait()
        here = pl.ds(pl.multiple_of(lax.rem(step, chunks) * chunk, chunk), chunk)
        units = pl.ds(pl.multiple_of(index * part, part), part)
        product = nt_dot(grad_buf[here, :], weight_buf[units, :])
        low = (product * wide(slope_buf[slot])).astype(hidden_buf.dtype)
        hidden_buf[index, here, :] = low
        sum_out[index] += jnp.sum(wide(low), axis=0, keepdims=True)

    for index in range(parts):
        hidden_copy(index).start()
    for copy in x_loads:
        copy.wait()
    tile_loop(
        x_blocks * parts,
        tiles,
        tile_sems,
        lambda step: up_out.at[
            pl.ds(pl.multiple_of(lax.div(step, parts) * x_block, x_block), x_block),
            pl.ds(pl.multiple_of(lax.rem(step, parts) * part, part), part),
        ],
        lambda step: tn_dot(x_buf[lax.div(step, parts)], hidden_buf[lax.rem(step, parts)]),
    )
    for index in range(parts):
        hidden_copy(index).wait()


def hidden_grads(grad_rows, weight, slope, x):
    low = jnp.bfloat16
    rows, depth = grad_rows.shape
    hidden = weight.shape[0]
    part, x_block, chunk = min(1024, hidden), min(512, depth), min(512, rows)
    return whole_call(
        hidden_grads_kernel,
        [ANY] * 4,
        [ANY, ANY, VMEM],
        [
            jax.ShapeDtypeStruct((rows, hidden), low),
            jax.ShapeDtypeStruct((depth, hidden), low),
            jax.ShapeDtypeStruct((hidden // part, 1, part), jnp.float32),
        ],
        [
            pltpu.VMEM((rows, depth), low),
            pltpu.VMEM((hidden, depth), low),
            pltpu.VMEM((2, chunk, part), low),
            pltpu.VMEM((depth // x_block, rows, x_block), low),
            pltpu.VMEM((hidden // part, rows, part), low),
            pltpu.VMEM((2, x_block, part), low),
            pltpu.SemaphoreType.DMA((rows // chunk + hidden // part + depth // x_block,)),
            pltpu.SemaphoreType.DMA((2,)),
            pltpu.SemaphoreType.DMA((hidden // part,)),
            pltpu.SemaphoreType.DMA((2,)),
        ],
    )(grad_rows, weight, slope, x)


def last_grads_kernel(
    x, joined, grad_rows, mixed, out, x_buf, joined_buf, tiles, x_sems, joined_sems, tile_sems
):
    blocks = x_buf.shape[0] // 2
    block = x_buf.shape[2]

    def x_load(index):
        source = x if index < blocks else grad_rows
        return pltpu.make_async_copy(
            columns_of(source, index % blocks, block), x_buf.at[index], x_sems.at[index]
        )

    def joined_load(slot):
        source = joined.at[slot] if slot < 3 else mixed
        return pltpu.make_async_copy(source, joined_buf.at[slot], joined_sems.at[slot])

    joined_load(0).start()
    for index in range(blocks):
        x_load(index).start()
    for slot in range(1, 4):
        joined_load(slot).start()
    for index in range(blocks, 2 * blocks):
        x_load(index).start()

    def compute(step):
        for slot in range(4):
            pl.when(step == slot * blocks)(joined_load(slot).wait)
        for index in range(blocks):
            pl.when(step == index)(x_load(index).wait)
            pl.when(step == 3 * blocks + index)(x_load(blocks + index).wait)
        slot = lax.div(step, blocks)
        index = lax.rem(step, blocks) + blocks * lax.div(slot, 3)
        return tn_dot(x_buf[index], joined_buf[slot])

    tile_loop(
        4 * blocks,
        tiles,
        tile_sems,
        lambda step: rows_of(out.at[lax.div(step, blocks)], lax.rem(step, blocks), block),
        compute,
    )


def last_grads(x, joined, grad_rows, mixed):
    low = jnp.bfloat16
    rows, depth = x.shape
    width = joined.shape[2]
    block = min(1024, depth)
    return whole_call(
        last_grads_kernel,
        [ANY] * 4,
        ANY,
        jax.ShapeDtypeStruct((4, depth, width), low),
        [
            pltpu.VMEM((2 * depth // block, rows, block), low),
            pltpu.VMEM((4, rows, width), low),
            pltpu.VMEM((2, block, width), low),
            pltpu.SemaphoreType.DMA((2 * depth // block,)),
            pltpu.SemaphoreType.DMA((4,)),
            pltpu.SemaphoreType.DMA((2,)),
        ],
    )(x, joined, grad_rows, mixed)


def normed_grads_kernel(
    starts_ref, joined, qkv, hidden, up, x, mean_ref, root_ref, gain_ref, shift_ref, *refs, places
):
    cuts = refs[:-8]
    joined_buf, qkv_buf, hidden_buf, up_buf, x_buf, out_buf, load_sems, cut_sems = refs[-8:]
    owners, halves = len(places), len(places[0])
    rows = hidden_buf.shape[0]
    owner_rows = rows // owners
    piece = owner_rows // halves
    columns = up_buf.shape[0]
    chunk = min(512, columns)
    chunks = columns // chunk

    def load(source, target, index):
        return pltpu.make_async_copy(source, target, load_sems.at[index])

    def row_loads(owner):
        here = pl.ds(pl.multiple_of(starts_ref[owner], owner_rows), owner_rows)
        at = 2 + owner * 3
        return (
            load(hidden.at[here, :], hidden_buf.at[here, :], at),
            load(joined.at[:, here, :], joined_buf.at[:, here, :], at + 1),
            load(x.at[here, :], x_buf.at[here, :], at + 2),
        )

    weights = [load(up, up_buf, 0), load(qkv, qkv_buf, 1)]
    weights[0].start()
    first_loads = row_loads(0)
    for copy in (*first_loads[:2], weights[1], first_loads[2]):
        copy.start()
    for owner in range(1, owners):
        for copy in row_loads(owner):
            copy.start()
    gain_ref[...] = jnp.zeros_like(gain_ref)
    shift_ref[...] = jnp.zeros_like(shift_ref)
    for copy in weights:
        copy.wait()

    def cut_copy(owner, part_of):
        array, row = places[owner][part_of]
        return pltpu.make_async_copy(
            out_buf.at[pl.ds(owner * owner_rows + part_of * piece, piece), :],
            cuts[array].at[pl.ds(row, piece), :],
            cut_sems.at[owner * halves + part_of],
        )

    @pl.loop(0, owners)
    def _(owner):
        here = pl.ds(pl.multiple_of(starts_ref[owner], owner_rows), owner_rows)
        there = pl.ds(pl.multiple_of(owner * owner_rows, owner_rows), owner_rows)
        for copy in row_loads(owner):
            copy.wait()
        for index in range(chunks):
            mine = slice(index * chunk, (index + 1) * chunk)
            total = nt_dot(hidden_buf[here, :], up_buf[mine, :])
            for slot in range(3):
                total += nt_dot(joined_buf[slot, here, :], qkv_buf[slot, mine, :])
            out_buf[there, mine] = total.astype(out_buf.dtype)
            hat = (wide(x_buf[here, mine]) - mean_ref[here, :]) * root_ref[here, :]
            gain_ref[:, mine] += jnp.sum(total * hat, axis=0, keepdims=True)
            shift_ref[:, mine] += jnp.sum(total, axis=0, keepdims=True)
        for own in range(owners):

            @pl.when(owner == own)
            def _(own=own):
                for part_of in range(halves):
                    cut_copy(own, part_of).start()

    for own in range(owners):
        for part_of in range(halves):
            cut_copy(own, part_of).wait()


def normed_grads(joined, qkv, hidden, up, x, mean, root, first, last):
    low = jnp.bfloat16
    rows, units = hidden.shape
    width = joined.shape[2]
    columns = last - first
    starts, places, sizes = owner_cuts(rows)
    owners, halves = len(places), len(places[0])
    line = jax.ShapeDtypeStruct((1, columns), jnp.float32)

    def kernel(starts_ref, joined, qkv, hidden, up, x, *refs):
        mine = pl.ds(first, columns)
        normed_grads_kernel(
            starts_ref,
            joined,
            qkv.at[:, mine, :],
            hidden,
            up.at[mine, :],
            x.at[:, mine],
            *refs,
            places=places,
        )

    result = whole_call(
        kernel,
        [SMEM] + [ANY] * 5 + [VMEM] * 2,
        [VMEM, VMEM] + [ANY] * len(sizes),
        [line, line] + [jax.ShapeDtypeStruct((size, columns), low) for size in sizes],
        [
            pltpu.VMEM((3, rows, width), low),
            pltpu.VMEM((3, columns, width), low),
            pltpu.VMEM((rows, units), low),
            pltpu.VMEM((columns, units), low),
            pltpu.VMEM((rows, columns), low),
            pltpu.VMEM((rows, columns), low),
            pltpu.SemaphoreType.DMA((2 + 3 * owners,)),
            pltpu.SemaphoreType.DMA((owners * halves,)),
        ],
    )(starts, joined, qkv, hidden, up, x, mean, root)
    return result[0], result[1], tuple(result[2:])


def finish_kernel(*refs):
    mixed, dense = refs[:4], refs[4:9]
    token_ref, bias_ref = refs[9:11]
    last_first, last_second, first_near, second_near, low, high = refs[11:17]
    out_ref = refs[17]
    half = low.shape[0]
    far = dense[3].shape[0]
    total = jnp.dot(mixed[0][...], dense[0][...], preferred_element_type=jnp.float32)
    total += jnp.dot(mixed[1][...], dense[1][...], preferred_element_type=jnp.float32)
    total += jnp.dot(mixed[2][...], dense[2][...], preferred_element_type=jnp.float32)
    total += jnp.dot(mixed[3][:, :far], dense[3][...], preferred_element_type=jnp.float32)
    total += jnp.dot(mixed[3][:, far:], dense[4][...], preferred_element_type=jnp.float32)
    total += wide(token_ref[...]) + bias_ref[...]
    for here, parts in (
        (slice(0, half), (low, first_near, last_first)),
        (slice(half, 2 * half), (high, second_near, last_second)),
    ):
        feed = wide(parts[0][...]) + wide(parts[1][...]) + wide(parts[2][...])
        out_ref[here, :] = (total[here] + feed).astype(out_ref.dtype)


def finish_output(mixed_parts, dense_parts, tokens, bias, feed_parts):
    rows, depth = tokens.shape
    if len(feed_parts) == 1:
        attended = jnp.dot(mixed_parts[0], dense_parts[0], preferred_element_type=jnp.float32)
        return (wide(tokens) + attended + feed_parts[0] + bias).astype(tokens.dtype)
    columns = min(512, depth)

    def column_block(piece):
        return pl.BlockSpec((piece.shape[0], columns), lambda j: (0, j))

    return pl.pallas_call(
        finish_kernel,
        grid=(depth // columns,),
        in_specs=[pl.BlockSpec(piece.shape, lambda j: (0, 0)) for piece in mixed_parts]
        + [column_block(piece) for piece in dense_parts]
        + [column_block(tokens), pl.BlockSpec((1, columns), lambda j: (0, j))]
        + [column_block(piece) for piece in feed_parts[:2]]
        + [pl.BlockSpec((rows // 2, columns), lambda j: (1, j))] * 2
        + [column_block(piece) for piece in feed_parts[4:]],
        out_specs=column_block(tokens),
        out_shape=jax.ShapeDtypeStruct(tokens.shape, tokens.dtype),
        compiler_params=pltpu.CompilerParams(vmem_limit_bytes=VMEM_BYTES),
        cost_estimate=SHORT,
    )(*mixed_parts, *dense_parts, tokens, bias.reshape(1, depth), *feed_parts)


def token_grads_kernel(*refs, steps):
    left, right = refs[:6], refs[6:12]
    token_ref, grad_ref, mean_ref, root_ref, gain_ref, out_ref = refs[12:]
    split = left[4].shape[1]
    mean_own, root_own = mean_ref[...], root_ref[...]

    def rows_of_half(upper):
        scaled, hats = [], []
        for side, parts in enumerate((left, right)):
            columns = slice(side * split, (side + 1) * split)
            total = sum(wide(parts[at + upper][...]) for at in (4, 2, 0))
            scaled.append(total * gain_ref[:, columns])
            hats.append((wide(token_ref[:, columns]) - mean_own) * root_own)
        count = 2 * split
        mean = sum(jnp.sum(v, axis=-1, keepdims=True) for v in scaled) / count
        slant = sum(jnp.sum(v * h, axis=-1, keepdims=True) for v, h in zip(scaled, hats)) / count
        for side in range(2):
            columns = slice(side * split, (side + 1) * split)
            grad = root_own * (scaled[side] - mean - hats[side] * slant)
            out_ref[:, columns] = (wide(grad_ref[:, columns]) + grad).astype(out_ref.dtype)

    step = pl.program_id(0)
    pl.when(step < steps)(lambda: rows_of_half(0))
    pl.when(step >= steps)(lambda: rows_of_half(1))


def token_grads(left_parts, right_parts, tokens, cotangent, mean, root, gain):
    if len(left_parts) == 1:
        grad = jnp.concatenate([left_parts[0], right_parts[0]], axis=1)
        hat = (wide(tokens) - mean) * root
        scaled = grad * gain
        grad_input = root * (
            scaled
            - jnp.mean(scaled, axis=-1, keepdims=True)
            - hat * jnp.mean(scaled * hat, axis=-1, keepdims=True)
        )
        return (wide(cotangent) + grad_input).astype(tokens.dtype)
    half, split = left_parts[4].shape
    rows, depth = tokens.shape
    chunk = min(256, half)
    steps = half // chunk
    low_part = pl.BlockSpec((chunk, split), lambda i: (jnp.minimum(i, steps - 1), 0))
    high_part = pl.BlockSpec((chunk, split), lambda i: (jnp.maximum(i - steps, 0), 0))
    low_near = pl.BlockSpec((chunk, split), lambda i: (steps + jnp.minimum(i, steps - 1), 0))
    high_near = pl.BlockSpec((chunk, split), lambda i: (jnp.maximum(i, steps), 0))
    row_block = pl.BlockSpec((chunk, depth), lambda i: (i, 0))
    thin = pl.BlockSpec((chunk, 1), lambda i: (i, 0))
    return pl.pallas_call(
        functools.partial(token_grads_kernel, steps=steps),
        grid=(rows // chunk,),
        in_specs=[low_part, high_part, low_near, high_near, low_part, high_part] * 2
        + [row_block, row_block, thin, thin, pl.BlockSpec((1, depth), lambda i: (0, 0))],
        out_specs=row_block,
        out_shape=jax.ShapeDtypeStruct(tokens.shape, tokens.dtype),
        compiler_params=pltpu.CompilerParams(vmem_limit_bytes=VMEM_BYTES),
        cost_estimate=SHORT,
    )(*left_parts, *right_parts, tokens, cotangent, mean, root, gain.reshape(1, -1))


def attention_kernel(
    q_ref,
    k_ref,
    v_ref,
    g_ref,
    cos_ref,
    above_ref,
    below_ref,
    mixed_ref,
    grads_ref,
    sums_ref,
    keys_across,
    values_across,
    query_total,
    key_total,
    value_total,
    weight_buf,
    top_buf,
    out_buf,
    across_buf,
    *,
    block,
    block_count,
):
    step = pl.program_id(1)
    scale = HEAD_DIM**-0.5
    rate = scale * 1.4426950408889634

    @pl.when(step == 0)
    def _():
        keys_across[...] = k_ref[...].T
        values_across[...] = v_ref[...].T
        key_total[...] = jnp.zeros_like(key_total)
        value_total[...] = jnp.zeros_like(value_total)

    rows = pl.ds(pl.multiple_of(step * block, block), block)
    queries, grads = q_ref[rows, :], g_ref[rows, :]
    lane = lax.broadcasted_iota(jnp.int32, (block, PAIR), 1)
    own_lanes = [lane // HEAD_DIM == head for head in range(2)]
    query_heads = [jnp.where(own, queries, jnp.zeros_like(queries)) for own in own_lanes]
    grad_heads = [jnp.where(own, grads, jnp.zeros_like(grads)) for own in own_lanes]
    parts = [slice(head * HEAD_DIM, (head + 1) * HEAD_DIM) for head in range(2)]

    def weigh(there, index, first):
        keys = k_ref[there, :]
        score_heads = [
            lax.dot_general(keys, own, ROWS_BY_ROWS, preferred_element_type=jnp.float32)
            for own in query_heads
        ]
        for head in range(2):
            scores = score_heads[head]
            if first:
                key_pos = lax.broadcasted_iota(jnp.int32, (block, block), 0)
                query_pos = lax.broadcasted_iota(jnp.int32, (block, block), 1)
                scores = jnp.where(key_pos <= query_pos, scores, masked_score)
            top = jnp.max(scores, axis=0, keepdims=True) * rate
            if not first:
                before = top_buf[head, 0]
                top = jnp.maximum(top, before)
            weights = jnp.exp2(scores * rate - top)
            weight_buf[head, there, :] = weights
            top_buf[head, 2 + index] = top
            total = jnp.sum(weights, axis=0, keepdims=True)
            out = jnp.dot(
                values_across[parts[head], there],
                weights.astype(jnp.bfloat16),
                preferred_element_type=jnp.float32,
            )
            if not first:
                shrink = jnp.exp2(before - top)
                total += top_buf[head, 1] * shrink
                out += out_buf[parts[head], :] * shrink
            top_buf[head, 0] = top
            top_buf[head, 1] = total
            out_buf[parts[head], :] = out

    def over_blocks(act):
        act(rows, step, True)

        @pl.when(lax.rem(step, 2) == 1)
        def _():
            act(pl.ds(pl.multiple_of((step - 1) * block, block), block), step - 1, False)

        @pl.loop(0, lax.div(step, 2))
        def _(index):
            start = pl.multiple_of(index * 2 * block, 2 * block)
            act(pl.ds(start, 2 * block), 2 * index, False)

    over_blocks(weigh)

    grads_across = grads.T.astype(jnp.float32)
    inner, share = [], []
    for head in range(2):
        share.append(1.0 / top_buf[head, 1])
        out = out_buf[parts[head], :] * share[head]
        out_buf[parts[head], :] = out
        inner.append(jnp.sum(out * grads_across[parts[head]], axis=0, keepdims=True))
    mixed_ref[rows, :] = out_buf[...].T.astype(mixed_ref.dtype)

    def differentiate(there, index, first):
        values = v_ref[there, :]
        prob_heads = [
            lax.dot_general(values, own, ROWS_BY_ROWS, preferred_element_type=jnp.float32)
            for own in grad_heads
        ]
        value_parts, key_parts = [], []
        for head in range(2):
            factor = jnp.exp2(top_buf[head, 2 + index] - top_buf[head, 0]) * share[head]
            exact = weight_buf[head, there, :] * factor
            rounded = exact.astype(jnp.bfloat16)
            grad_scores = (exact * (prob_heads[head] - inner[head])).astype(jnp.bfloat16)
            value_parts.append(
                jnp.dot(rounded, grad_heads[head], preferred_element_type=jnp.float32)
            )
            key_parts.append(
                jnp.dot(grad_scores, query_heads[head], preferred_element_type=jnp.float32)
            )
            across = jnp.dot(
                keys_across[parts[head], there], grad_scores, preferred_element_type=jnp.float32
            )
            if first:
                across_buf[parts[head], :] = across
            else:
                across_buf[parts[head], :] += across
        value_total[there, :] += value_parts[0] + value_parts[1]
        key_total[there, :] += key_parts[0] + key_parts[1]

    over_blocks(differentiate)
    query_total[rows, :] = across_buf[...].T

    @pl.when(step == block_count - 1)
    def _():
        lanes = cos_ref[...], above_ref[...], below_ref[...]
        for slot, field in enumerate(
            (
                turn_back(query_total[...] * scale, *lanes),
                turn_back(key_total[...] * scale, *lanes),
                value_total[...],
            )
        ):
            low = field.astype(grads_ref.dtype)
            grads_ref[slot] = low
            sums_ref[slot] = jnp.sum(low.astype(jnp.float32), axis=0, keepdims=True)


def attention(joined, grad_mixed, lanes, first, last, earlier=None):
    rows, width = grad_mixed.shape
    block = min(512, LENGTH)
    pairs, block_count = width // PAIR, LENGTH // block
    row_block = pl.BlockSpec((LENGTH, PAIR), lambda p, i: (0, first + p))
    table = pl.BlockSpec((LENGTH, PAIR), lambda p, i: (0, 0))
    kept = () if earlier is None else tuple(earlier)
    kernel = functools.partial(attention_kernel, block=block, block_count=block_count)

    def body(*refs):
        kernel(*refs[:7], *refs[7 + len(kept) :])

    return pl.pallas_call(
        body,
        grid=(last - first, block_count),
        in_specs=[
            row_block,
            pl.BlockSpec((LENGTH, PAIR), lambda p, i: (0, pairs + first + p)),
            pl.BlockSpec((LENGTH, PAIR), lambda p, i: (0, 2 * pairs + first + p)),
            row_block,
            table,
            table,
            table,
        ]
        + [pl.BlockSpec(memory_space=pl.ANY)] * len(kept),
        out_specs=[
            row_block,
            pl.BlockSpec((3, LENGTH, PAIR), lambda p, i: (0, 0, first + p)),
            pl.BlockSpec((3, 1, PAIR), lambda p, i: (0, 0, first + p)),
        ],
        out_shape=[
            jax.ShapeDtypeStruct((rows, width), jnp.bfloat16),
            jax.ShapeDtypeStruct((3, rows, width), jnp.bfloat16),
            jax.ShapeDtypeStruct((3, 1, width), jnp.float32),
        ],
        scratch_shapes=[
            pltpu.VMEM((PAIR, LENGTH), jnp.bfloat16),
            pltpu.VMEM((PAIR, LENGTH), jnp.bfloat16),
            pltpu.VMEM((LENGTH, PAIR), jnp.float32),
            pltpu.VMEM((LENGTH, PAIR), jnp.float32),
            pltpu.VMEM((LENGTH, PAIR), jnp.float32),
            pltpu.VMEM((2, LENGTH, block), jnp.float32),
            pltpu.VMEM((2, 2 + block_count, 1, block), jnp.float32),
            pltpu.VMEM((PAIR, block), jnp.float32),
            pltpu.VMEM((PAIR, block), jnp.float32),
        ],
        input_output_aliases={7 + i: i for i in range(len(kept))},
        compiler_params=pltpu.CompilerParams(vmem_limit_bytes=VMEM_BYTES),
        cost_estimate=SHORT,
    )(joined, joined, joined, grad_mixed, *lanes, *kept)


def norm_kernel(starts_ref, gain_ref, shift_ref, following_ref, *refs):
    count = (len(refs) - 6) // 3
    pieces = refs[:count]
    raw, normed, mean_ref, root_ref, following_out = refs[count : count + 5]
    buffers = refs[count + 5 : 2 * count + 5]
    results = refs[2 * count + 5 : 3 * count + 5]
    sems = refs[-1]
    following_out[...] = following_ref[...]
    for slot in range(count):
        pltpu.make_async_copy(pieces[slot], buffers[slot], sems.at[0, slot]).start()
    writes = []
    for slot in range(count):
        buffer, result = buffers[slot], results[slot]
        size = buffer.shape[0]
        where = pl.ds(pl.multiple_of(starts_ref[slot], size), size)
        pltpu.make_async_copy(pieces[slot], buffer, sems.at[0, slot]).wait()
        write = pltpu.make_async_copy(buffer, raw.at[where, :], sems.at[1, slot])
        write.start()
        writes.append(write)
        chunk = min(128, size)

        @pl.loop(0, size // chunk)
        def _(step, buffer=buffer, result=result, slot=slot):
            here = pl.ds(pl.multiple_of(step * chunk, chunk), chunk)
            rows = buffer[here, :].astype(jnp.float32)
            mean = jnp.mean(rows, axis=-1, keepdims=True)
            centred = rows - mean
            variance = jnp.mean(centred * centred, axis=-1, keepdims=True)
            root = lax.rsqrt(variance + epsilon)
            out = centred * root * gain_ref[...] + shift_ref[...]
            result[here, :] = out.astype(result.dtype)
            there = pl.ds(pl.multiple_of(starts_ref[slot] + step * chunk, chunk), chunk)
            mean_ref[there, :] = mean
            root_ref[there, :] = root

        write = pltpu.make_async_copy(result, normed.at[where, :], sems.at[2, slot])
        write.start()
        writes.append(write)
    for write in writes:
        write.wait()


def norm_rows(pieces, gain, shift, following):
    depth = gain.shape[0]
    total = sum(piece.shape[0] for _, piece in pieces)
    count = len(pieces)
    low = jnp.bfloat16
    starts = jnp.stack([jnp.asarray(start, jnp.int32) for start, _ in pieces])
    any_space = pl.BlockSpec(memory_space=pl.ANY)
    vmem = pl.BlockSpec(memory_space=pltpu.VMEM)
    stage = [pltpu.VMEM(piece.shape, low) for _, piece in pieces]
    return pl.pallas_call(
        norm_kernel,
        in_specs=[pl.BlockSpec(memory_space=pltpu.SMEM), vmem, vmem, vmem] + [any_space] * count,
        out_specs=[any_space, any_space, vmem, vmem, vmem],
        out_shape=[
            jax.ShapeDtypeStruct((total, depth), low),
            jax.ShapeDtypeStruct((total, depth), low),
            jax.ShapeDtypeStruct((total, 1), jnp.float32),
            jax.ShapeDtypeStruct((total, 1), jnp.float32),
            jax.ShapeDtypeStruct(following.shape, following.dtype),
        ],
        scratch_shapes=stage + stage + [pltpu.SemaphoreType.DMA((3, count))],
        compiler_params=pltpu.CompilerParams(vmem_limit_bytes=VMEM_BYTES),
        cost_estimate=SHORT,
    )(
        starts,
        gain.reshape(1, depth),
        shift.reshape(1, depth),
        following,
        *[piece for _, piece in pieces],
    )


def on_device(
    tokens,
    norm_gain,
    norm_shift,
    weight_qkv,
    bias_qkv,
    weight_dense,
    weight_up,
    bias_up,
    weight_down,
    bias_out,
    cotangent,
):
    f32, low = jnp.float32, jnp.bfloat16
    depth = tokens.shape[1]
    local_rows = tokens.shape[0]
    tensor_index = lax.axis_index("tensor")

    full_up = lax.all_gather(weight_up, "dp", axis=0, tiled=True)
    token_parts = gather_start(tokens)
    lanes = lane_tables(LENGTH)
    out_part = jnp.sum(cotangent, axis=0, dtype=f32)
    lanes, out_part, token_parts = after((lanes, out_part, token_parts))
    full_qkv = lax.all_gather(
        after(jnp.transpose(weight_qkv, (1, 0, 2)), token_parts), "dp", axis=1, tiled=True
    )
    token_parts = gather_pass(token_parts)
    all_tokens, gathered, mean, root, sent = norm_rows(
        gathered_pieces(token_parts), norm_gain, norm_shift, cotangent
    )
    grad_parts = gather_start(sent)

    full_dense = lax.all_gather(after(weight_dense, gathered), "dp", axis=1, tiled=True)
    own_mean = lax.dynamic_slice_in_dim(mean, tensor_index * local_rows, local_rows, 0)
    own_root = lax.dynamic_slice_in_dim(root, tensor_index * local_rows, local_rows, 0)
    active, slope = hidden_rows(gathered, full_up, bias_up)
    own_mean, own_root, active = after((own_mean, own_root, active))
    grad_parts, active = after((grad_parts, active))
    full_down = lax.all_gather(after(weight_down, grad_parts), "dp", axis=1, tiled=True)
    grad_parts = gather_pass(grad_parts)
    joined = joined_rows(after(gathered, active, grad_parts[:3]), full_qkv, bias_qkv, lanes)
    grad_parts, joined = after((grad_parts, joined))
    grad_rows, grad_down = first_grads(gathered_pieces(grad_parts), active)
    grad_mixed = jnp.einsum(
        "td,kd->tk", grad_rows, after(full_dense, grad_down), preferred_element_type=f32
    ).astype(low)
    dense_parts = gather_start(after(full_dense, grad_mixed))
    grad_down_sum = lax.psum_scatter(grad_down, "dp", scatter_dimension=1, tiled=True)

    pairs = grad_mixed.shape[1] // PAIR
    part = attention(joined, grad_mixed, lanes, 0, pairs // 2)
    dense_parts, part = after((dense_parts, part))
    dense_parts = gather_pass(dense_parts)
    feed_cuts = feed_rows(after(active, part[0]), full_down)
    feed_cuts, dense_parts = after((feed_cuts, dense_parts))
    feed_parts = scatter_send(feed_cuts)
    grad_hidden, grad_up, bias_up_part = hidden_grads(
        after(grad_rows, feed_cuts), full_down, slope, gathered
    )
    grad_up, feed_parts = after((grad_up, feed_parts))
    feed_parts = scatter_fold(feed_parts)
    grad_up_sum = lax.psum_scatter(
        after(grad_up, feed_parts[:2]), "dp", scatter_dimension=0, tiled=True
    )
    feed_parts = scatter_pass(feed_parts)
    part = attention(after(joined, grad_up), grad_mixed, lanes, pairs // 2, pairs, part)
    mixed, grad_joined, bias_qkv_part = part
    mixed, grad_joined, feed_parts = after((mixed, grad_joined, feed_parts))

    mixed_parts = exchange_start(mixed)
    grad_last = last_grads(gathered, grad_joined, grad_rows, mixed)
    grad_last, mixed_parts = after((grad_last, mixed_parts))
    grad_last_sum = lax.psum_scatter(
        grad_last, "dp", scatter_dimension=1, tiled=True
    )
    half = depth // 2
    sources = full_qkv, grad_hidden, full_up, all_tokens, mean, root
    *left_sums, left_cuts = normed_grads(after(grad_joined, grad_last), *sources, 0, half)
    left_parts = scatter_send(left_cuts)
    *right_sums, right_cuts = normed_grads(after(grad_joined, left_cuts), *sources, half, depth)
    right_cuts, right_sums, left_parts = after((right_cuts, right_sums, left_parts))
    sums = jnp.concatenate(
        [left_sums[0][0], right_sums[0][0], left_sums[1][0], right_sums[1][0], out_part]
    ).reshape(-1, PAIR)
    right_parts = scatter_send(right_cuts)
    left_parts = scatter_pass(scatter_fold(left_parts))
    block_out = finish_output(
        after(mixed_parts, right_cuts), dense_parts, tokens, bias_out, feed_parts
    )
    small = jnp.concatenate(
        [sums.reshape(-1), bias_qkv_part.reshape(-1), bias_up_part.reshape(-1)]
    ).reshape(-1, PAIR)
    block_out, small = after((block_out, small))
    small = jnp.sum(lax.all_gather(small, "dp", axis=0), axis=0)
    block_out, right_parts, left_parts, small = after(
        (block_out, right_parts, left_parts, small)
    )
    right_parts = scatter_fold(right_parts)
    right_parts, small, grad_up_sum, grad_down_sum = after(
        (right_parts, small, grad_up_sum, grad_down_sum)
    )
    right_parts = scatter_pass(right_parts)
    small = small.reshape(-1)
    over_all = exchange_sum(small[: 3 * depth].reshape(-1, PAIR), "tensor")
    grad_gain, grad_shift, grad_bias_out = over_all.reshape(3, depth)
    bias_size = bias_qkv.size
    grad_bias_qkv = small[3 * depth : 3 * depth + bias_size].reshape(bias_qkv.shape)
    grad_bias_up = small[3 * depth + bias_size :]
    last = jnp.transpose(grad_last_sum, (1, 0, 2)).astype(f32)
    ready = grad_up_sum.astype(f32), grad_down_sum.astype(f32), last
    ready, left_parts = after((ready, left_parts))
    grad_up_sum, grad_down_sum, last = ready
    grad_tokens = token_grads(
        left_parts, right_parts, tokens, cotangent, own_mean, own_root, norm_gain
    )
    return (
        block_out,
        grad_tokens,
        grad_gain,
        grad_shift,
        last[:, :3],
        grad_bias_qkv,
        jnp.transpose(last[:, 3]),
        grad_up_sum,
        grad_bias_up,
        grad_down_sum,
        grad_bias_out,
    )


def solution(mesh):
    in_specs = (
        P(("dp", "tensor"), None),
        P(),
        P(),
        P("dp", None, "tensor"),
        P(None, "tensor"),
        P("tensor", "dp"),
        P("dp", "tensor"),
        P("tensor"),
        P("tensor", "dp"),
        P(),
        P(("dp", "tensor"), None),
    )
    out_specs = (
        P(("dp", "tensor"), None),
        P(("dp", "tensor"), None),
        P(),
        P(),
        P("dp", None, "tensor"),
        P(None, "tensor"),
        P("tensor", "dp"),
        P("dp", "tensor"),
        P("tensor"),
        P("tensor", "dp"),
        P(),
    )
    return jax.shard_map(
        on_device, mesh=mesh, in_specs=in_specs, out_specs=out_specs, check_vma=False
    )
```
